32 devices in a mesh: lon: 8 (over y, x, core), lat: 4 (over z).
Axes of the slice: x: 2, y: 2, z: 4, core: 2. Of those that a mesh axis runs over, the one named last changes fastest.
Arguments:
- fields: float32 [8, 64, 16, 1024], P(None, None, 'lat', 'lon'), may hold values from -6 to 6
- courant: float32 [2, 64, 16, 1024], P(None, None, 'lat', 'lon'), may hold values from -0.5 to 0.5
- cos_zenith: float32 [16, 1024], P('lat', 'lon'), may hold values from 0.2 to 1
- albedo: float32 [16, 1024], P('lat', 'lon'), may hold values from 0.05 to 0.5
- extinction: float32 [14], replicated, may hold values from 0.05 to 4
- single_albedo: float32 [14], replicated, may hold values from 0.2 to 0.95
- band_weight: float32 [14], replicated, may hold values from 0.02 to 0.14
- sun_order: int32 [16, 8, 128], P('lat', 'lon'), may hold values from 0 to 127, each once within a row
- sun_count: int32 [16, 8], P('lat', 'lon'), may hold values from 0 to 128, as said below
Outputs:
- new_fields: float32 [8, 64, 16, 1024], P(None, None, 'lat', 'lon')
- heating: float32 [64, 16, 1024], P(None, 'lat', 'lon')
The draws below stay inside these ranges and needn't reach their ends.
Inputs may be any that keep to these rules, and one draw needn't show every extreme that they name: `sun_count`: for every latitude the counts of tiles t and t + 4 sum to 128.
All inputs are finite; a program needn't handle non-finite values.
Results may differ from the reference program's by a relative error of at most 0.00005.
Values sent between devices are 32-bit elements; how exact they have to be, the bound alone decides.
No kernel may reach another device: no remote copies, remote signals or barrier semaphores. Data moves between devices by JAX's collectives and lax.ppermute only.
A program may use at most 128 MiB of HBM per device.

```python
import math
import jax
import jax.numpy as jnp
from jax import lax

FIELDS = 8
BANDS = 14
LEV = 64
LON_DEV = 128
TILES = 8
NLON = 1024
NLAT = 16


def draw_sun_count(key, part):
    tiles = NLON // LON_DEV
    half_tiles = tiles // 2
    key_count = jax.random.fold_in(key, 11)
    key_side = jax.random.fold_in(key, 23)
    counts = jax.random.randint(key_count, (NLAT, half_tiles), LON_DEV // 2, LON_DEV + 1)
    counts = counts.at[0, 0].set(LON_DEV)
    side = jax.random.randint(key_side, (NLAT, half_tiles), 0, 2)
    first = jnp.where(side == 1, counts, LON_DEV - counts)
    second = LON_DEV - first
    return jnp.concatenate([first, second], axis=1).astype(jnp.int32)


def level_of(stream_key, dims, split, least, high):
    gain = 1.0
    for position, shards_of in split:
        draws = jax.random.uniform(jax.random.fold_in(jax.random.fold_in(stream_key, 6), position), (shards_of,), jnp.float32, least / len(split), high / len(split))
        gain = gain * jnp.repeat(jnp.exp(draws), dims[position] // shards_of).reshape((-1,) + (1,) * (len(dims) - 1 - position))
    return gain


def scatter_about(key, extent, spread, reach, cuts=(), held_as=jnp.bfloat16):
    entries = jax.random.normal(key, extent, jnp.float32) * spread
    if len(cuts) > 0:
        entries = level_of(key, extent, cuts, -0.22, 0.18) * entries
    return jnp.clip(entries, min=-reach, max=reach).astype(held_as)


def setup_inputs(seed: int = 0) -> dict:
    key_of = jax.random.split(jax.random.key(seed), 10)
    return {
        "fields": scatter_about(key_of[0], (FIELDS, LEV, NLAT, NLON), 1.0, 6.0, ((2, 4), (3, 8)), jnp.float32),
        "courant": jnp.clip(jax.random.uniform(key_of[1], (2, LEV, NLAT, NLON), jnp.float32, -0.5, 0.5) * level_of(key_of[1], (2, LEV, NLAT, NLON), ((2, 4), (3, 8)), -0.4, 0.0), -0.5, 0.5),
        "cos_zenith": jnp.clip(0.2 + 0.8 * jax.random.uniform(key_of[2], (NLAT, NLON), jnp.float32) ** level_of(key_of[2], (NLAT, NLON), ((0, 4), (1, 8)), -0.2, 0.2), 0.2, 1.0),
        "albedo": jnp.clip(0.05 + 0.45 * jax.random.uniform(key_of[3], (NLAT, NLON), jnp.float32) ** level_of(key_of[3], (NLAT, NLON), ((0, 4), (1, 8)), -0.2, 0.2), 0.05, 0.5),
        "extinction": jnp.clip(jnp.exp(jax.random.uniform(key_of[4], (BANDS,), jnp.float32, math.log(0.05), math.log(4.0))), 0.05, 4.0),
        "single_albedo": jnp.clip(jax.random.uniform(key_of[5], (BANDS,), jnp.float32, 0.2, 0.95), 0.2, 0.95),
        "band_weight": jnp.clip(jax.random.uniform(key_of[6], (BANDS,), jnp.float32, 0.02, 0.14), 0.02, 0.14),
        "sun_order": jax.vmap(lambda own: jax.random.permutation(own, LON_DEV))(jax.random.split(key_of[7], NLAT * TILES)).reshape((NLAT, TILES, LON_DEV)).astype(jnp.int32),
        "sun_count": draw_sun_count(jax.random.fold_in(key_of[9], 71), 0),
    }


def tendency(field, east_num, north_num):
    right = jnp.roll(field, -1, axis=2)
    left = jnp.roll(field, 1, axis=2)
    right_two = jnp.roll(field, -2, axis=2)
    east = east_num * (7.0 * (field + right) - (left + right_two)) / 12.0
    div_east = east - jnp.roll(east, 1, axis=2)
    padded = jnp.pad(field, ((0, 0), (2, 2), (0, 0)))
    north = north_num * (7.0 * (padded[:, 2:-2] + padded[:, 3:-1]) - (padded[:, 1:-3] + padded[:, 4:])) / 12.0
    shifted = jnp.concatenate([jnp.zeros_like(north[:, :1]), north[:, :-1]], axis=1)
    div_north = north - shifted
    return -(div_east + div_north)


def optics(water, cosz, extinction, single_albedo):
    levels = water.shape[0]
    tau = (extinction * (4.0 / levels))[None, :, None] * water[:, None, :]
    depth = jnp.cumsum(tau, axis=0)
    mu = cosz[None, None, :]
    s_top = jnp.exp(-(depth - tau) / mu)
    s_bot = jnp.exp(-depth / mu)
    direct = jnp.exp(-tau / mu)
    decay = jnp.exp(-1.66 * tau)
    scat = 0.5 * single_albedo[None, :, None] * (1.0 - decay)
    transmit = decay + scat
    source = 0.5 * single_albedo[None, :, None] * mu * s_top * (1.0 - direct)
    return scat, transmit, source, s_top, s_bot


def up_step(carry, layer):
    a_below, b_below = carry
    reflect, transmit, source = layer
    den = 1.0 - reflect * a_below
    a_here = reflect + transmit * transmit * a_below / den
    b_here = transmit * (a_below * source + b_below) / den + source
    return (a_here, b_here), (a_here, b_here, den, b_below)


def down_step(d_top, layer):
    transmit, reflect, source, den, b_below = layer
    d_bot = (transmit * d_top + reflect * b_below + source) / den
    return d_bot, d_top


def radiate(water, cosz, surface, extinction, single_albedo, band_weight):
    reflect, transmit, source, s_top, s_bot = optics(water, cosz, extinction, single_albedo)
    mu = cosz[None, :]
    a_floor = jnp.broadcast_to(surface[None, :], reflect.shape[1:])
    b_floor = a_floor * mu * s_bot[-1]
    _, (a_all, b_all, den_all, b_next) = lax.scan(up_step, (a_floor, b_floor), (reflect, transmit, source), reverse=True)
    d_floor, d_all = lax.scan(down_step, jnp.zeros_like(a_floor), (transmit, reflect, source, den_all, b_next))
    net_top = mu[None] * s_top + d_all - (a_all * d_all + b_all)
    net_floor = mu * s_bot[-1] + d_floor - (a_floor * d_floor + b_floor)
    net_bot = jnp.concatenate([net_top[1:], net_floor[None]], axis=0)
    absorbed = net_top - net_bot
    return water.shape[0] * jnp.sum(absorbed * band_weight[None, :, None], axis=1)


def reference(fields, courant, cos_zenith, albedo, extinction, single_albedo, band_weight, sun_order, sun_count):
    east_num = courant[0]
    north_num = courant[1]

    def advance(field):
        section = field + tendency(field, east_num, north_num)
        return 0.5 * ((field + section) + tendency(section, east_num, north_num))

    advanced = lax.map(advance, fields)
    inverse = jnp.argsort(sun_order, axis=-1).astype(jnp.int32)
    sunlit = (inverse < sun_count[:, :, None]).astype(jnp.float32).reshape(NLAT, NLON)
    water = jax.nn.softplus(fields[1])
    tiles = NLON // LON_DEV

    def by_tile(array):
        lead = array.shape[0]
        return array.reshape(lead, NLAT, tiles, LON_DEV).transpose(2, 0, 1, 3).reshape(tiles, lead, NLAT * LON_DEV)

    packed = by_tile(jnp.concatenate([water, cos_zenith[None], albedo[None]], axis=0))

    def one_tile(block):
        return radiate(block[:LEV], block[LEV], block[LEV + 1], extinction, single_albedo, band_weight)

    heat_tiles = lax.map(one_tile, packed)
    heat_all = heat_tiles.reshape(tiles, LEV, NLAT, LON_DEV).transpose(1, 2, 0, 3).reshape(LEV, NLAT, NLON)
    heating = heat_all * sunlit[None]
    new_fields = jnp.concatenate([advanced[:1] + 0.5 * heating[None], advanced[1:]], axis=0)
    return new_fields, heating
```

```python
import functools
import math

import jax
import jax.numpy as jnp
from jax import lax
from jax.experimental import pallas as pl
from jax.experimental.pallas import tpu as pltpu
from jax.sharding import PartitionSpec as P

GROUPS = ((0, 4), (4, 8))
SUB = 8
LANES = 128
LOG2E = math.log2(math.e)
VMEM = pl.BlockSpec(memory_space=pltpu.VMEM)
SMEM = pl.BlockSpec(memory_space=pltpu.SMEM)
ANY = pl.BlockSpec(memory_space=pl.ANY)
PARAMS = pltpu.CompilerParams(vmem_limit_bytes=24 * 1024 * 1024)


def swaps(block, axis, ring):
    n = lax.axis_size(axis)
    first = [(i, i ^ 1) for i in range(n)]
    second = []
    for i in range(1, n if ring else n - 1, 2):
        second += [(i, (i + 1) % n), ((i + 1) % n, i)]
    return lax.ppermute(block[0], axis, first), lax.ppermute(block[1], axis, second)


def lane_index():
    return lax.broadcasted_iota(jnp.int32, (SUB, LANES), 1)


def is_even(axis):
    return lax.rem(lax.axis_index(axis), 2) == 0


def pack(rows, block, blocks, packed, lane):
    for r, value in enumerate(rows):
        k = r * blocks + block
        packed = jnp.where(lane // 4 == k, pltpu.roll(value, (4 * k + 2) % LANES, 1), packed)
    return packed


def native_rows(ref, index, block, nrows):
    return [ref[index, pl.ds(SUB * nrows * block + r, SUB, stride=nrows), :] for r in range(nrows)]


def put_sends(even, rows, za, zb, index, block):
    span = pl.ds(SUB * block, SUB)
    za[index, span, :] = jnp.where(even, rows[2], rows[0])
    za[index + 1, span, :] = jnp.where(even, rows[3], rows[1])
    zb[index, span, :] = jnp.where(even, rows[0], rows[2])
    zb[index + 1, span, :] = jnp.where(even, rows[1], rows[3])


def pack_kernel(lo, hi, with_courant, fields, courant, za, zb, packed):
    nrows = 4
    blocks = fields.shape[1] // nrows // SUB
    lane = lane_index()
    even = is_even("lat")

    def one(i, _):
        acc = jnp.zeros((SUB, LANES), jnp.float32)
        for b in range(blocks):
            rows = native_rows(fields, lo + i, b, nrows)
            put_sends(even, rows, za, zb, 2 * i, b)
            acc = pack(rows, b, blocks, acc, lane)
        packed[i] = acc
        return 0

    lax.fori_loop(0, hi - lo, one, 0)
    if with_courant:
        acc = jnp.zeros((SUB, LANES), jnp.float32)
        for b in range(blocks):
            acc = pack(native_rows(courant, 0, b, nrows), b, blocks, acc, lane)
            top = courant[1, pl.ds(SUB * nrows * b + nrows - 1, SUB, stride=nrows), :]
            za[2 * (hi - lo), pl.ds(SUB * b, SUB), :] = top
            zb[2 * (hi - lo), pl.ds(SUB * b, SUB), :] = top
        packed[hi - lo] = acc


def seam(own, first, second, c_first, c_second, lon_even, lane):
    west = jnp.where(lon_even, second, first)
    east = jnp.where(lon_even, first, second)
    c_west = pltpu.roll(jnp.where(lon_even, c_second, c_first), LANES - 1, 1)
    q_m1 = pltpu.roll(west, LANES - 1, 1)
    q_0 = pltpu.roll(own, LANES - 2, 1)
    q_1 = pltpu.roll(own, LANES - 3, 1)
    flux = c_west * (7.0 * (q_m1 + q_0) - (west + q_1)) * (1.0 / 12.0)
    place = lane % 4
    return jnp.where(place == 0, flux, jnp.where(place == 1, west, east))


def divergence(q, c_east, c_north, packed, block, blocks, lane):
    north = []
    for r in range(5):
        north.append(
            c_north[r] * (7.0 * (q[r + 1] + q[r + 2]) - (q[r] + q[r + 3])) * (1.0 / 12.0)
        )
    out = []
    zero, low, last = lane == 0, lane < 2, lane == LANES - 1
    for r in range(4):
        k = r * blocks + block
        here = q[r + 2]
        halo = pltpu.roll(packed, (2 * LANES - 4 * k - 2) % LANES, 1)
        edge = pltpu.roll(packed, (2 * LANES - 4 * k - 1) % LANES, 1)
        right = pltpu.roll(jnp.where(zero, halo, here), LANES - 1, 1)
        right_two = pltpu.roll(jnp.where(low, halo, here), LANES - 2, 1)
        left = pltpu.roll(jnp.where(last, halo, here), 1, 1)
        flux = c_east[r] * (7.0 * (here + right) - (left + right_two)) * (1.0 / 12.0)
        flux_west = pltpu.roll(jnp.where(last, edge, flux), 1, 1)
        out.append((flux - flux_west) + (north[r + 1] - north[r]))
    return out


def halo_rows(rows, lat_even, ra, rb, index, block):
    span = pl.ds(SUB * block, SUB)
    a0, a1 = ra[index, span, :], ra[index + 1, span, :]
    b0, b1 = rb[index, span, :], rb[index + 1, span, :]
    south = [jnp.where(lat_even, b0, a0), jnp.where(lat_even, b1, a1)]
    north = [jnp.where(lat_even, a0, b0), jnp.where(lat_even, a1, b1)]
    return south + rows + north


def courant_rows(courant, lat_even, ca, cb, block, nrows):
    span = pl.ds(SUB * block, SUB)
    row = ca.shape[0] - 1
    below = jnp.where(lat_even, cb[row, span, :], ca[row, span, :])
    return native_rows(courant, 0, block, nrows), [below] + native_rows(courant, 1, block, nrows)


def first_kernel(
    lo, hi, fields, courant, own, ra, rb, rl, rr, ca, cb, cl, cr, section, za, zb, packed
):
    nrows = 4
    blocks = fields.shape[1] // nrows // SUB
    lane = lane_index()
    lat_even, lon_even = is_even("lat"), is_even("lon")
    c_row = cl.shape[0] - 1

    def one(i, _):
        halo = seam(own[i], rl[i], rr[i], cl[c_row], cr[c_row], lon_even, lane)
        acc = jnp.zeros((SUB, LANES), jnp.float32)
        for b in range(blocks):
            rows = native_rows(fields, lo + i, b, nrows)
            q = halo_rows(rows, lat_even, ra, rb, 2 * i, b)
            c_east, c_north = courant_rows(courant, lat_even, ca, cb, b, nrows)
            div = divergence(q, c_east, c_north, halo, b, blocks, lane)
            new = [rows[r] - div[r] for r in range(nrows)]
            for r in range(nrows):
                section[nrows * i + r, pl.ds(SUB * b, SUB), :] = new[r]
            put_sends(lat_even, new, za, zb, 2 * i, b)
            acc = pack(new, b, blocks, acc, lane)
        packed[i] = acc
        return 0

    lax.fori_loop(0, hi - lo, one, 0)


def second_kernel(
    lo, hi, fields, courant, section, own, ra, rb, rl, rr, ca, cb, cl, cr, heating, *rest
):
    out, buffer, sems = rest[-3:]
    nrows = 4
    blocks = fields.shape[1] // nrows // SUB
    lane = lane_index()
    lat_even, lon_even = is_even("lat"), is_even("lon")
    c_row = cl.shape[0] - 1

    def copy(i):
        return pltpu.make_async_copy(buffer.at[i], out.at[lo + i], sems.at[i])

    def one(i, _):
        halo = seam(own[i], rl[i], rr[i], cl[c_row], cr[c_row], lon_even, lane)
        for b in range(blocks):
            rows = native_rows(fields, lo + i, b, nrows)
            own_rows = [section[nrows * i + r, pl.ds(SUB * b, SUB), :] for r in range(nrows)]
            s = halo_rows(own_rows, lat_even, ra, rb, 2 * i, b)
            c_east, c_north = courant_rows(courant, lat_even, ca, cb, b, nrows)
            div = divergence(s, c_east, c_north, halo, b, blocks, lane)
            for r in range(nrows):
                buffer[i, pl.ds(SUB * nrows * b + r, SUB, stride=nrows), :] = 0.5 * (
                    (rows[r] + own_rows[r]) - div[r]
                )
        if lo == 0:

            @pl.when(i == 0)
            def _():
                buffer[0] = buffer[0] + 0.5 * heating[...]

        copy(i).start()
        return 0

    lax.fori_loop(0, hi - lo, one, 0)
    for i in range(hi - lo):
        copy(i).wait()


def radiation_kernel(
    fields, cosz, albedo, ext, single, weight, order, count, after, heat, water, depth, save_a, save_b, save_t, save_g
):
    del after
    nrows, _ = cosz.shape
    levels = fields.shape[1] // nrows
    pairs = ext.shape[0] // 2
    x = fields[0]
    wet = jnp.maximum(x, 0.0) + jnp.log1p(jnp.exp(-jnp.abs(x)))
    heat[...] = wet
    total = jnp.zeros((nrows, LANES), jnp.float32)
    depth[0] = jnp.zeros((2 * nrows, LANES), jnp.float32)
    for l in range(levels):
        w = heat[pl.ds(nrows * l, nrows), :]
        total = total + w
        water[l, pl.ds(0, nrows), :] = w
        water[l, pl.ds(nrows, nrows), :] = w
        depth[l + 1, pl.ds(0, nrows), :] = total
        depth[l + 1, pl.ds(nrows, nrows), :] = total

    mu = jnp.concatenate([cosz[...], cosz[...]], axis=0)
    floor_albedo = jnp.concatenate([albedo[...], albedo[...]], axis=0)
    first = lax.broadcasted_iota(jnp.int32, (2 * nrows, LANES), 0) < nrows

    def by_band(ref):
        return [jnp.where(first, ref[2 * p], ref[2 * p + 1]) for p in range(pairs)]

    scale = 4.0 / levels
    inv_mu = 1.0 / mu
    ext_of, half_of, weight_of = by_band(ext), by_band(single), by_band(weight)
    beam = [-(e * scale * LOG2E) * inv_mu for e in ext_of]
    diffuse = [-(1.66 * scale * LOG2E) * e for e in ext_of]
    half = [0.5 * s for s in half_of]
    half_mu = [0.5 * s * mu for s in half_of]

    def up(step, carry):
        l = levels - 1 - step
        a_all, b_all, s_all = carry
        w = water[l]
        above = depth[l]
        new_a, new_b, new_s = [], [], []
        for p in range(pairs):
            a, b, s_bot = a_all[p], b_all[p], s_all[p]
            decay = jnp.exp2(diffuse[p] * w)
            s_top = jnp.exp2(beam[p] * above)
            reflect = half[p] - half[p] * decay
            transmit = decay + reflect
            source = half_mu[p] * (s_top - s_bot)
            den = 1.0 - reflect * a
            inv = pl.reciprocal(den, approx=True)
            inv = inv * (2.0 - den * inv)
            t = transmit * inv
            a_here = reflect + transmit * (t * a)
            b_here = t * (a * source + b) + source
            save_t[l, p] = t
            save_g[l, p] = (reflect * b + source) * inv
            save_a[l, p] = 1.0 - a_here
            save_b[l, p] = mu * s_top - b_here
            new_a.append(a_here)
            new_b.append(b_here)
            new_s.append(s_top)
        return tuple(new_a), tuple(new_b), tuple(new_s)

    s_floor = [jnp.exp2(beam[p] * depth[levels]) for p in range(pairs)]
    a_floor = [floor_albedo for _ in range(pairs)]
    b_floor = [floor_albedo * (mu * s_floor[p]) for p in range(pairs)]
    lax.fori_loop(0, levels, up, (tuple(a_floor), tuple(b_floor), tuple(s_floor)))

    sunlit = []
    column = lax.broadcasted_iota(jnp.int32, (LANES, LANES), 1)
    rank = lax.broadcasted_iota(jnp.int32, (LANES, LANES), 0)
    for r in range(nrows):
        place = jnp.transpose(jnp.broadcast_to(order[pl.ds(r, 1), :], (LANES, LANES)))
        hit = (place == column) & (rank < count[r, 0])
        sunlit.append(jnp.max(jnp.where(hit, 1.0, 0.0), axis=0, keepdims=True))
    gain = float(levels) * jnp.concatenate(sunlit, axis=0)

    def weighted(l, d_all):
        net = jnp.zeros((2 * nrows, LANES), jnp.float32)
        for p in range(pairs):
            net = net + weight_of[p] * (save_b[l, p] + d_all[p] * save_a[l, p])
        return net

    def put(l, absorbed):
        both = absorbed[:nrows] + absorbed[nrows:]
        heat[pl.ds(pl.multiple_of(nrows * l, nrows), nrows), :] = gain * both

    def down(l, carry):
        d_all, net_above = carry
        d_new = tuple(save_t[l - 1, p] * d_all[p] + save_g[l - 1, p] for p in range(pairs))
        net = weighted(l, d_new)
        put(l - 1, net_above - net)
        return d_new, net

    d_top = tuple(jnp.zeros((2 * nrows, LANES), jnp.float32) for _ in range(pairs))
    d_low, net_low = lax.fori_loop(1, levels, down, (d_top, weighted(0, d_top)))
    net = jnp.zeros((2 * nrows, LANES), jnp.float32)
    for p in range(pairs):
        d_floor = save_t[levels - 1, p] * d_low[p] + save_g[levels - 1, p]
        at_floor = (mu * s_floor[p] - b_floor[p]) + d_floor * (1.0 - a_floor[p])
        net = net + weight_of[p] * at_floor
    put(levels - 1, net_low - net)


def shape(*dims):
    return jax.ShapeDtypeStruct(dims, jnp.float32)


def per_device(
    fields, courant, cos_zenith, albedo, extinction, single_albedo, band_weight, sun_order, sun_count
):
    nfields, levels, nrows, ncols = fields.shape
    flat = fields.reshape(nfields, levels * nrows, ncols)
    wind = courant.reshape(2, levels * nrows, ncols)

    sent, got = [], []
    for lo, hi in GROUPS:
        n, extra = hi - lo, int(lo == 0)
        rows = shape(2 * n + extra, levels, ncols)
        za, zb, packed = pl.pallas_call(
            functools.partial(pack_kernel, lo, hi, lo == 0),
            out_shape=(rows, rows, shape(n + extra, SUB, ncols)),
            in_specs=[VMEM, VMEM],
            out_specs=(VMEM, VMEM, VMEM),
            compiler_params=PARAMS,
            name=f"pack_{lo}",
        )(flat, wind)
        sent.append(packed)
        got.append(swaps((za, zb), "lat", False) + swaps((packed, packed), "lon", True))

    sections, sent_two, got_two = [], [], []
    for g, (lo, hi) in enumerate(GROUPS):
        n = hi - lo
        rows = shape(2 * n, levels, ncols)
        section, za, zb, packed = pl.pallas_call(
            functools.partial(first_kernel, lo, hi),
            out_shape=(shape(nrows * n, levels, ncols), rows, rows, shape(n, SUB, ncols)),
            in_specs=[VMEM] * 11,
            out_specs=(VMEM,) * 4,
            compiler_params=PARAMS,
            name=f"first_{lo}",
        )(flat, wind, sent[g], *got[g], *got[0])
        sections.append(section)
        sent_two.append(packed)
        got_two.append(swaps((za, zb), "lat", False) + swaps((packed, packed), "lon", True))

    pairs = extinction.shape[0] // 2
    store = pltpu.VMEM((levels, pairs, 2 * nrows, ncols), jnp.float32)
    heating = pl.pallas_call(
        radiation_kernel,
        out_shape=shape(levels * nrows, ncols),
        grid=(1,),
        in_specs=[
            pl.BlockSpec((1, levels * nrows, ncols), lambda i: (1, 0, 0)),
            VMEM, VMEM, SMEM, SMEM, SMEM, VMEM, SMEM, ANY,
        ],
        out_specs=pl.BlockSpec((levels * nrows, ncols), lambda i: (0, 0)),
        scratch_shapes=[
            pltpu.VMEM((levels, 2 * nrows, ncols), jnp.float32),
            pltpu.VMEM((levels + 1, 2 * nrows, ncols), jnp.float32),
            store, store, store, store,
        ],
        compiler_params=PARAMS,
        cost_estimate=pl.CostEstimate(flops=20_000_000, bytes_accessed=400_000, transcendentals=1_500_000),
        name="radiation",
    )(
        flat, cos_zenith, albedo, extinction, single_albedo, band_weight,
        sun_order.reshape(nrows, ncols), sun_count, sent_two[-1],
    )

    out = None
    for g, (lo, hi) in enumerate(GROUPS):
        n = hi - lo
        args = [flat, wind, sections[g], sent_two[g], *got_two[g], *got[0], heating]
        specs = [VMEM] * len(args)
        aliases = {}
        if out is not None:
            aliases = {len(args): 0}
            args.append(out)
            specs.append(ANY)
        out = pl.pallas_call(
            functools.partial(second_kernel, lo, hi),
            out_shape=shape(nfields, levels * nrows, ncols),
            in_specs=specs,
            out_specs=ANY,
            scratch_shapes=[
                pltpu.VMEM((n, levels * nrows, ncols), jnp.float32),
                pltpu.SemaphoreType.DMA((n,)),
            ],
            input_output_aliases=aliases,
            compiler_params=PARAMS,
            name=f"second_{lo}",
        )(*args)
    return out.reshape(fields.shape), heating.reshape(levels, nrows, ncols)


def solution(mesh):
    in_specs = (
        P(None, None, "lat", "lon"),
        P(None, None, "lat", "lon"),
        P("lat", "lon"),
        P("lat", "lon"),
        P(),
        P(),
        P(),
        P("lat", "lon", None),
        P("lat", "lon"),
    )
    out_specs = (P(None, None, "lat", "lon"), P(None, "lat", "lon"))
    return jax.shard_map(
        per_device, mesh=mesh, in_specs=in_specs, out_specs=out_specs, check_vma=False
    )
```

```python
import functools
import math

import jax
import jax.numpy as jnp
from jax import lax
from jax.experimental import pallas as pl
from jax.experimental.pallas import tpu as pltpu
from jax.sharding import PartitionSpec as P

SPLIT = 2
SUB = 8
LANES = 128
LOG2E = math.log2(math.e)
VMEM = pl.BlockSpec(memory_space=pltpu.VMEM)
SMEM = pl.BlockSpec(memory_space=pltpu.SMEM)
ANY = pl.BlockSpec(memory_space=pl.ANY)
PARAMS = pltpu.CompilerParams(vmem_limit_bytes=24 * 1024 * 1024)


def scratch(*dims):
    return pltpu.VMEM(dims, jnp.float32)


def shape(*dims):
    return jax.ShapeDtypeStruct(dims, jnp.float32)


def swaps(first_block, second_block, axis, ring):
    n = lax.axis_size(axis)
    first = [(i, i ^ 1) for i in range(n)]
    second = []
    for i in range(1, n if ring else n - 1, 2):
        second += [(i, (i + 1) % n), ((i + 1) % n, i)]
    return lax.ppermute(first_block, axis, first), lax.ppermute(second_block, axis, second)


def is_even(axis):
    return lax.rem(lax.axis_index(axis), 2) == 0


def native(ref, index, r, nrows):
    levels = ref.shape[1] // nrows
    return ref[index, pl.ds(r, levels, stride=nrows), :]


def tile_of(low, high):
    return jnp.transpose(jnp.concatenate([low, high], axis=0))


def put_lat_sends(even, tiles, pair, nrows, za, zb):
    north = jnp.where(even, 2, 0)
    for k in range(2):
        span = pl.ds(pl.multiple_of((2 * pair + k) * LANES, LANES), LANES)
        za[span, :] = tiles[nrows * pair + north + k]
        zb[span, :] = tiles[nrows * pair + (2 - north) + k]


def put_lon_sends(even, tiles, pair, at, nrows, la, lb):
    for r in range(nrows):
        west = tiles[nrows * pair + r, pl.ds(0, 2), :]
        east = tiles[nrows * pair + r, pl.ds(LANES - 2, 2), :]
        la[pl.ds(at + 2 * r, 2), :] = jnp.where(even, east, west)
        lb[pl.ds(at + 2 * r, 2), :] = jnp.where(even, west, east)


def pack_first(pairs, nrows, fields, courant, tiles, za, zb, nat, nat_late, nat_wind, sems):
    n = 2 * pairs
    copies = [pltpu.make_async_copy(fields.at[i], nat.at[i], sems.at[i]) for i in range(n)]
    wind = pltpu.make_async_copy(courant, nat_wind, sems.at[n])
    late = pltpu.make_async_copy(fields.at[pl.ds(n, nat_late.shape[0])], nat_late, sems.at[n + 1])
    for copy in copies + [wind, late]:
        copy.start()
    even = is_even("lat")
    for p in range(pairs):
        copies[2 * p].wait()
        copies[2 * p + 1].wait()
        for r in range(nrows):
            tiles[nrows * p + r] = tile_of(native(nat, 2 * p, r, nrows), native(nat, 2 * p + 1, r, nrows))
        put_lat_sends(even, tiles, p, nrows, za, zb)
    wind.wait()
    top = native(nat_wind, 1, nrows - 1, nrows) * (1.0 / 12.0)
    top = tile_of(top, top)
    half = LANES // 2
    lane = lax.broadcasted_iota(jnp.int32, (half, LANES), 1)
    top = jnp.where(lane < half, top[:half], top[half:])
    span = pl.ds(2 * pairs * LANES, half)
    za[span, :] = top
    zb[span, :] = top
    late.wait()


def pack_second(pairs, nrows, nat, nat_wind, tiles_first, tiles, za, zb, ce, cn, la, lb):
    lat_even, lon_even = is_even("lat"), is_even("lon")
    for p in range(pairs):
        for r in range(nrows):
            tiles[nrows * p + r] = tile_of(native(nat, 2 * p, r, nrows), native(nat, 2 * p + 1, r, nrows))
        put_lat_sends(lat_even, tiles, p, nrows, za, zb)
    for r in range(nrows):
        east = native(nat_wind, 0, r, nrows) * (1.0 / 12.0)
        north = native(nat_wind, 1, r, nrows) * (1.0 / 12.0)
        ce[r] = tile_of(east, east)
        cn[r] = tile_of(north, north)
    early = tiles_first.shape[0] // nrows
    for p in range(early):
        put_lon_sends(lon_even, tiles_first, p, 2 * nrows * p, nrows, la, lb)
    for p in range(pairs):
        put_lon_sends(lon_even, tiles, p, 2 * nrows * (early + p), nrows, la, lb)
    at = 2 * nrows * (early + pairs)
    for r in range(nrows):
        edge = ce[r, pl.ds(LANES - 1, 1), :]
        la[pl.ds(at + r, 1), :] = edge
        lb[pl.ds(at + r, 1), :] = edge


def put_sides(even, la, lb, west, east):
    rows = la.shape[0]
    a, b = la[...], lb[...]
    west[pl.ds(SUB, rows), :] = jnp.where(even, b, a)
    east[pl.ds(SUB, rows), :] = jnp.where(even, a, b)


def put_edges(q, pair, at, nrows, west, east, edge_w, edge_e):
    for r in range(nrows):
        tile = nrows * pair + r
        edge_w[r, pl.ds(0, SUB), :] = west[pl.ds(at + 2 + 2 * r, SUB), :]
        edge_w[r, pl.ds(SUB, SUB), :] = q[tile, pl.ds(0, SUB), :]
        edge_e[r, pl.ds(0, SUB), :] = q[tile, pl.ds(LANES - SUB, SUB), :]
        edge_e[r, pl.ds(SUB, SUB), :] = east[pl.ds(at + SUB + 2 * r, SUB), :]


def put_wind_edges(ce, at, nrows, west, edge_c):
    for r in range(nrows):
        edge_c[r, pl.ds(0, SUB), :] = west[pl.ds(at + 1 + r, SUB), :]
        edge_c[r, pl.ds(SUB, SUB), :] = ce[r, pl.ds(0, SUB), :]


def put_fluxes(q, pair, nrows, ce, edge_w, edge_e, edge_c, flux):
    def face(c, left, here, right, right_two):
        return c * (7.0 * (here + right) - (left + right_two))

    for r in range(nrows):
        tile = nrows * pair + r
        window = [edge_w[r, pl.ds(k, SUB), :] for k in range(4)]
        flux[r, pl.ds(1, SUB), :] = face(edge_c[r, pl.ds(1, SUB), :], *window)
        for b in range(LANES // SUB):
            at = SUB * b

            def load(shift):
                if at + shift < 0:
                    return edge_w[r, pl.ds(SUB + shift, SUB), :]
                if at + shift + SUB > LANES:
                    return edge_e[r, pl.ds(shift, SUB), :]
                return q[tile, pl.ds(at + shift, SUB), :]

            flux[r, pl.ds(SUB + at, SUB), :] = face(
                ce[r, pl.ds(at, SUB), :], load(-1), load(0), load(1), load(2)
            )


def divergence(q, pair, nrows, b, lat_even, ra, rb, cn, below, flux):
    at = SUB * b
    here = pl.ds(at, SUB)

    def halo(k):
        span = pl.ds(pl.multiple_of((2 * pair + k) * LANES, LANES) + at, SUB)
        a, b_ = ra[span, :], rb[span, :]
        return jnp.where(lat_even, b_, a), jnp.where(lat_even, a, b_)

    (s0, n0), (s1, n1) = halo(0), halo(1)
    own = [q[nrows * pair + r, here, :] for r in range(nrows)]
    rows = [s0, s1] + own + [n0, n1]
    winds = [below[here, :]] + [cn[r, here, :] for r in range(nrows)]
    north = []
    for r in range(nrows + 1):
        north.append(winds[r] * (7.0 * (rows[r + 1] + rows[r + 2]) - (rows[r] + rows[r + 3])))
    div = []
    for r in range(nrows):
        east = flux[r, pl.ds(SUB + at, SUB), :] - flux[r, pl.ds(SUB + at - 1, SUB), :]
        div.append(east + (north[r + 1] - north[r]))
    return own, div


def edge_scratch(nrows, lon_rows):
    return [
        scratch(lon_rows + 2 * SUB, LANES),
        scratch(lon_rows + 2 * SUB, LANES),
        scratch(nrows, 2 * SUB, LANES),
        scratch(nrows, 2 * SUB, LANES),
        scratch(nrows, 2 * SUB, LANES),
        scratch(nrows, LANES + SUB, LANES),
    ]


def first_stage(pairs, done, nrows, is_first, *refs):
    q, ce, cn, ra, rb, la, lb = refs[:7]
    refs = refs[7:]
    lat_even, lon_even = is_even("lat"), is_even("lon")
    if is_first:
        section, za, zb, below, *refs = refs
        half = LANES // 2
        span = pl.ds(2 * pairs * LANES, half)
        a = jnp.where(lat_even, rb[span, :], ra[span, :])
        turned = pltpu.roll(a, half, 1)
        low = lax.broadcasted_iota(jnp.int32, (half, LANES), 1) < half
        below[pl.ds(0, half), :] = jnp.where(low, a, turned)
        below[pl.ds(half, half), :] = jnp.where(low, turned, a)
    else:
        below, earlier, section, za, zb, sa, sb, *refs = refs
    west, east, edge_w, edge_e, edge_c, flux = refs
    put_sides(lon_even, la, lb, west, east)
    put_wind_edges(ce, la.shape[0] - SUB, nrows, west, edge_c)

    def one(p, _):
        put_edges(q, p, 2 * nrows * (done + p), nrows, west, east, edge_w, edge_e)
        put_fluxes(q, p, nrows, ce, edge_w, edge_e, edge_c, flux)
        for b in range(LANES // SUB):
            own, div = divergence(q, p, nrows, b, lat_even, ra, rb, cn, below, flux)
            for r in range(nrows):
                section[nrows * p + r, pl.ds(SUB * b, SUB), :] = own[r] - div[r]
        put_lat_sends(lat_even, section, p, nrows, za, zb)
        return 0

    lax.fori_loop(0, pairs, one, 0)
    if not is_first:
        for p in range(done):
            put_lon_sends(lon_even, earlier, p, 2 * nrows * p, nrows, sa, sb)
        for p in range(pairs):
            put_lon_sends(lon_even, section, p, 2 * nrows * (done + p), nrows, sa, sb)


def second_stage(pairs, done, nrows, is_first, *refs):
    q, s, ce, cn, below, ra, rb, la, lb, sa, sb, heating = refs[:12]
    out, buffer, sems, west, east, edge_w, edge_e, edge_c, flux, wind_w, wind_e = refs[-11:]
    levels = LANES // 2
    lat_even, lon_even = is_even("lat"), is_even("lon")
    put_sides(lon_even, la, lb, wind_w, wind_e)
    put_wind_edges(ce, la.shape[0] - SUB, nrows, wind_w, edge_c)
    put_sides(lon_even, sa, sb, west, east)

    def copy(p):
        return pltpu.make_async_copy(
            buffer.at[pl.ds(2 * p, 2)], out.at[pl.ds(2 * (done + p), 2)], sems.at[p]
        )

    def one(p, _):
        put_edges(s, p, 2 * nrows * (done + p), nrows, west, east, edge_w, edge_e)
        put_fluxes(s, p, nrows, ce, edge_w, edge_e, edge_c, flux)
        parts = [[] for _ in range(nrows)]
        for b in range(LANES // SUB):
            own, div = divergence(s, p, nrows, b, lat_even, ra, rb, cn, below, flux)
            for r in range(nrows):
                old = q[nrows * p + r, pl.ds(SUB * b, SUB), :]
                parts[r].append(0.5 * ((old + own[r]) - div[r]))
        for r in range(nrows):
            turned = jnp.transpose(jnp.concatenate(parts[r], axis=0))
            for h in range(2):
                buffer[2 * p + h, pl.ds(r, levels, stride=nrows), :] = turned[levels * h : levels * (h + 1)]
        if is_first:

            @pl.when(p == 0)
            def _():
                buffer[0] = buffer[0] + 0.5 * heating[...]

        copy(p).start()
        return 0

    lax.fori_loop(0, pairs, one, 0)
    for p in range(pairs):
        copy(p).wait()


def radiation(
    nat, cosz_in, albedo_in, ext_in, single_in, weight_in, order_in, count_in, after, heat,
    water, depth, save_a, save_b, save_t, save_g, cosz, albedo, ext, single, weight, order, count, sems
):
    del after
    copies = []
    for i, (src, dst) in enumerate(
        (
            (cosz_in, cosz), (albedo_in, albedo), (ext_in, ext), (single_in, single),
            (weight_in, weight), (order_in, order), (count_in, count),
        )
    ):
        copies.append(pltpu.make_async_copy(src, dst, sems.at[i]))
        copies[-1].start()
    nrows, _ = cosz.shape
    levels = nat.shape[1] // nrows
    pairs = ext.shape[0] // 2
    x = nat[1]
    heat[...] = jnp.maximum(x, 0.0) + jnp.log1p(jnp.exp(-jnp.abs(x)))
    total = jnp.zeros((nrows, LANES), jnp.float32)
    depth[0] = jnp.zeros((2 * nrows, LANES), jnp.float32)
    for l in range(levels):
        w = heat[pl.ds(nrows * l, nrows), :]
        total = total + w
        water[l, pl.ds(0, nrows), :] = w
        water[l, pl.ds(nrows, nrows), :] = w
        depth[l + 1, pl.ds(0, nrows), :] = total
        depth[l + 1, pl.ds(nrows, nrows), :] = total
    for copy in copies:
        copy.wait()

    mu = jnp.concatenate([cosz[...], cosz[...]], axis=0)
    floor_albedo = jnp.concatenate([albedo[...], albedo[...]], axis=0)
    first = lax.broadcasted_iota(jnp.int32, (2 * nrows, LANES), 0) < nrows

    def by_band(ref):
        return [jnp.where(first, ref[2 * p], ref[2 * p + 1]) for p in range(pairs)]

    scale = 4.0 / levels
    inv_mu = 1.0 / mu
    ext_of, half_of, weight_of = by_band(ext), by_band(single), by_band(weight)
    beam = [-(e * scale * LOG2E) * inv_mu for e in ext_of]
    diffuse = [-(1.66 * scale * LOG2E) * e for e in ext_of]
    half = [0.5 * s for s in half_of]
    strength = [w * mu for w in weight_of]

    def up(step, carry):
        l = levels - 1 - step
        a_all, b_all, s_all = carry
        w = water[l]
        above = depth[l]
        new_a, new_b, new_s = [], [], []
        for p in range(pairs):
            a, b, s_bot = a_all[p], b_all[p], s_all[p]
            decay = jnp.exp2(diffuse[p] * w)
            s_top = strength[p] * jnp.exp2(beam[p] * above)
            reflect = half[p] - half[p] * decay
            transmit = decay + reflect
            source = half[p] * (s_top - s_bot)
            den = 1.0 - reflect * a
            inv = pl.reciprocal(den, approx=True)
            inv = inv * (2.0 - den * inv)
            t = transmit * inv
            a_here = reflect + transmit * (t * a)
            b_here = t * (a * source + b) + source
            save_t[l, p] = t
            save_g[l, p] = (reflect * b + source) * inv
            save_a[l, p] = 1.0 - a_here
            save_b[l, p] = s_top - b_here
            new_a.append(a_here)
            new_b.append(b_here)
            new_s.append(s_top)
        return tuple(new_a), tuple(new_b), tuple(new_s)

    s_floor = [strength[p] * jnp.exp2(beam[p] * depth[levels]) for p in range(pairs)]
    a_floor = [floor_albedo for _ in range(pairs)]
    b_floor = [floor_albedo * s_floor[p] for p in range(pairs)]
    lax.fori_loop(0, levels, up, (tuple(a_floor), tuple(b_floor), tuple(s_floor)))

    sunlit = []
    column = lax.broadcasted_iota(jnp.int32, (LANES, LANES), 1)
    rank = lax.broadcasted_iota(jnp.int32, (LANES, LANES), 0)
    for r in range(nrows):
        place = jnp.transpose(jnp.broadcast_to(order[r], (LANES, LANES)))
        hit = (place == column) & (rank < count[r])
        sunlit.append(jnp.max(jnp.where(hit, 1.0, 0.0), axis=0, keepdims=True))
    gain = float(levels) * jnp.concatenate(sunlit, axis=0)

    def net_flux(l, d_all):
        net = jnp.zeros((2 * nrows, LANES), jnp.float32)
        for p in range(pairs):
            net = net + (save_b[l, p] + d_all[p] * save_a[l, p])
        return net

    def put(l, absorbed):
        both = absorbed[:nrows] + absorbed[nrows:]
        heat[pl.ds(pl.multiple_of(nrows * l, nrows), nrows), :] = gain * both

    def down(l, carry):
        d_all, net_above = carry
        d_new = tuple(save_t[l - 1, p] * d_all[p] + save_g[l - 1, p] for p in range(pairs))
        net = net_flux(l, d_new)
        put(l - 1, net_above - net)
        return d_new, net

    d_top = tuple(jnp.zeros((2 * nrows, LANES), jnp.float32) for _ in range(pairs))
    d_low, net_low = lax.fori_loop(1, levels, down, (d_top, net_flux(0, d_top)))
    net = jnp.zeros((2 * nrows, LANES), jnp.float32)
    for p in range(pairs):
        d_floor = save_t[levels - 1, p] * d_low[p] + save_g[levels - 1, p]
        net = net + ((s_floor[p] - b_floor[p]) + d_floor * (1.0 - a_floor[p]))
    put(levels - 1, net_low - net)


def call(kernel, name, out_shape, specs, out_specs, args, scratches, **kw):
    return pl.pallas_call(
        kernel,
        out_shape=out_shape,
        in_specs=specs,
        out_specs=out_specs,
        scratch_shapes=scratches,
        compiler_params=PARAMS,
        name=name,
        **kw,
    )(*args)


def per_device(
    fields, courant, cos_zenith, albedo, extinction, single_albedo, band_weight, sun_order, sun_count
):
    nfields, levels, nrows, ncols = fields.shape
    flat = fields.reshape(nfields, levels * nrows, ncols)
    wind = courant.reshape(2, levels * nrows, ncols)
    npairs = nfields // 2
    counts = (SPLIT, npairs - SPLIT)
    starts = (0, SPLIT)
    early, late = counts
    lon_rows = 2 * nrows * npairs

    z0 = shape((2 * early) * ncols + ncols // 2, LANES)
    tiles0, za, zb, nat, nat_late, nat_wind = call(
        functools.partial(pack_first, early, nrows),
        "pack_first",
        (
            shape(nrows * early, ncols, LANES), z0, z0,
            shape(2 * early, levels * nrows, ncols), shape(2 * late, levels * nrows, ncols),
            shape(2, levels * nrows, ncols),
        ),
        [ANY, ANY],
        (VMEM,) * 6,
        (flat, wind),
        [pltpu.SemaphoreType.DMA((2 * early + 2,))],
    )
    lat0 = swaps(za, zb, "lat", False)
    z1 = shape(2 * late * ncols, LANES)
    lon = shape(lon_rows + SUB, LANES)
    winds = shape(nrows, ncols, LANES)
    tiles1, za, zb, ce, cn, la, lb = call(
        functools.partial(pack_second, late, nrows),
        "pack_second",
        (shape(nrows * late, ncols, LANES), z1, z1, winds, winds, lon, lon),
        [VMEM] * 3,
        (VMEM,) * 7,
        (nat_late, nat_wind, tiles0),
        [],
    )
    lon_q = swaps(la, lb, "lon", True)
    lat1 = swaps(za, zb, "lat", False)

    edges = edge_scratch(nrows, lon_rows + SUB)
    z0 = shape(2 * early * ncols, LANES)
    section0, za, zb, below = call(
        functools.partial(first_stage, early, 0, nrows, True),
        "first_stage_0",
        (shape(nrows * early, ncols, LANES), z0, z0, shape(ncols, LANES)),
        [VMEM] * 7,
        (VMEM,) * 4,
        (tiles0, ce, cn, *lat0, *lon_q),
        edges,
    )
    lat2 = swaps(za, zb, "lat", False)
    lon = shape(lon_rows, LANES)
    section1, za, zb, la, lb = call(
        functools.partial(first_stage, late, early, nrows, False),
        "first_stage_1",
        (shape(nrows * late, ncols, LANES), z1, z1, lon, lon),
        [VMEM] * 9,
        (VMEM,) * 5,
        (tiles1, ce, cn, *lat1, *lon_q, below, section0),
        edges,
    )
    lat3 = swaps(za, zb, "lat", False)
    lon_s = swaps(la, lb, "lon", True)

    pairs = extinction.shape[0] // 2
    store = scratch(levels, pairs, 2 * nrows, ncols)
    heating = call(
        radiation,
        "radiation",
        shape(levels * nrows, ncols),
        [VMEM] + [ANY] * 8,
        VMEM,
        (
            nat, cos_zenith, albedo, extinction, single_albedo, band_weight, sun_order,
            sun_count.reshape(nrows), la,
        ),
        [
            scratch(levels, 2 * nrows, ncols), scratch(levels + 1, 2 * nrows, ncols),
            store, store, store, store,
            scratch(nrows, ncols), scratch(nrows, ncols),
            pltpu.SMEM(extinction.shape, jnp.float32), pltpu.SMEM(extinction.shape, jnp.float32),
            pltpu.SMEM(extinction.shape, jnp.float32), pltpu.VMEM((nrows, 1, ncols), jnp.int32),
            pltpu.SMEM((nrows,), jnp.int32), pltpu.SemaphoreType.DMA((7,)),
        ],
        cost_estimate=pl.CostEstimate(flops=20_000_000, bytes_accessed=400_000, transcendentals=1_500_000),
    )

    out = None
    for g, (tiles, section, lat) in enumerate(((tiles0, section0, lat2), (tiles1, section1, lat3))):
        args = [tiles, section, ce, cn, below, *lat, *lon_q, *lon_s, heating]
        specs = [VMEM] * len(args)
        aliases = {}
        if out is not None:
            aliases = {len(args): 0}
            args.append(out)
            specs.append(ANY)
        out = call(
            functools.partial(second_stage, counts[g], starts[g], nrows, g == 0),
            f"second_stage_{g}",
            shape(nfields, levels * nrows, ncols),
            specs,
            ANY,
            args,
            [
                scratch(2 * counts[g], levels * nrows, ncols),
                pltpu.SemaphoreType.DMA((counts[g],)),
                *edge_scratch(nrows, lon_rows),
                scratch(lon_rows + 3 * SUB, LANES),
                scratch(lon_rows + 3 * SUB, LANES),
            ],
            input_output_aliases=aliases,
        )
    return out.reshape(fields.shape), heating.reshape(levels, nrows, ncols)


def solution(mesh):
    in_specs = (
        P(None, None, "lat", "lon"),
        P(None, None, "lat", "lon"),
        P("lat", "lon"),
        P("lat", "lon"),
        P(),
        P(),
        P(),
        P("lat", "lon", None),
        P("lat", "lon"),
    )
    out_specs = (P(None, None, "lat", "lon"), P(None, "lat", "lon"))
    return jax.shard_map(
        per_device, mesh=mesh, in_specs=in_specs, out_specs=out_specs, check_vma=False
    )
```

```python
import functools
import math

import jax
import jax.numpy as jnp
from jax import lax
from jax.experimental import pallas as pl
from jax.experimental.pallas import tpu as pltpu
from jax.sharding import PartitionSpec as P

SPLIT = 2
SUB = 8
LANES = 128
LOG2E = math.log2(math.e)
VMEM = pl.BlockSpec(memory_space=pltpu.VMEM)
HBM = pl.BlockSpec(memory_space=pltpu.HBM)
MIB = 1024 * 1024


def scratch(*dims):
    return pltpu.VMEM(dims, jnp.float32)


def shape(*dims):
    return jax.ShapeDtypeStruct(dims, jnp.float32)


def lon_swaps(first_block, second_block):
    n = lax.axis_size("lon")
    first = [(i, i ^ 1) for i in range(n)]
    second = [(i, (i + 1 if i % 2 else i - 1) % n) for i in range(n)]
    return lax.ppermute(first_block, "lon", first), lax.ppermute(second_block, "lon", second)


def lat_swaps(first_block, second_block):
    nlon, nlat = lax.axis_size("lon"), lax.axis_size("lat")
    second = []
    for i in range(nlon):
        for j in range(nlat):
            k = j + 1 if j % 2 else j - 1
            to = i * nlat + k if 0 <= k < nlat else (i ^ 1) * nlat + j
            second.append((i * nlat + j, to))
    got = lax.ppermute(second_block, ("lon", "lat"), second)
    return lax.ppermute(first_block, "lat", [(j, j ^ 1) for j in range(nlat)]), got


def is_even(axis):
    return lax.rem(lax.axis_index(axis), 2) == 0


def sublanes():
    return lax.broadcasted_iota(jnp.int32, (SUB, LANES), 0)


def lanes():
    return lax.broadcasted_iota(jnp.int32, (SUB, LANES), 1)


def half_turn(block):
    return pltpu.roll(block, SUB // 2, 0)


def native(ref, index, r, nrows):
    levels = ref.shape[1] // nrows
    return ref[index, pl.ds(r, levels, stride=nrows), :]


def tile_of(low, high):
    return jnp.transpose(jnp.concatenate([low, high], axis=0))


def put_lat_sends(even, tiles, pair, nrows, za, zb):
    north = jnp.where(even, 2, 0)
    for k in range(2):
        span = pl.ds(pl.multiple_of((2 * pair + k) * LANES, LANES), LANES)
        za[span, :] = tiles[nrows * pair + north + k]
        zb[span, :] = tiles[nrows * pair + (2 - north) + k]


def take_sides(tile):
    head = sublanes() < SUB // 2
    return jnp.where(head, tile[pl.ds(0, SUB), :], tile[pl.ds(LANES - SUB, SUB), :])


def pack_first(pairs, nrows, fields, courant, tiles, za, zb, nat, nat_late, nat_wind, sems):
    n = 2 * pairs
    copies = [pltpu.make_async_copy(fields.at[i], nat.at[i], sems.at[i]) for i in range(n)]
    wind = pltpu.make_async_copy(courant, nat_wind, sems.at[n])
    late = pltpu.make_async_copy(fields.at[pl.ds(n, nat_late.shape[0])], nat_late, sems.at[n + 1])
    for copy in copies + [wind, late]:
        copy.start()
    even = is_even("lat")
    for p in range(pairs):
        copies[2 * p].wait()
        copies[2 * p + 1].wait()
        for r in range(nrows):
            tiles[nrows * p + r] = tile_of(native(nat, 2 * p, r, nrows), native(nat, 2 * p + 1, r, nrows))
        put_lat_sends(even, tiles, p, nrows, za, zb)
    wind.wait()
    top = native(nat_wind, 1, nrows - 1, nrows) * (1.0 / 12.0)
    top = tile_of(top, top)
    half = LANES // 2
    lane = lax.broadcasted_iota(jnp.int32, (half, LANES), 1)
    top = jnp.where(lane < half, top[:half], top[half:])
    span = pl.ds(2 * pairs * LANES, half)
    za[span, :] = top
    zb[span, :] = top
    late.wait()


def pack_middle(pairs, nrows, nat, nat_wind, tiles_first, tiles, ce, cn, la, lb):
    for p in range(pairs):
        for r in range(nrows):
            tiles[nrows * p + r] = tile_of(native(nat, 2 * p, r, nrows), native(nat, 2 * p + 1, r, nrows))
    for r in range(nrows):
        east = native(nat_wind, 0, r, nrows) * (1.0 / 12.0)
        north = native(nat_wind, 1, r, nrows) * (1.0 / 12.0)
        ce[r] = tile_of(east, east)
        cn[r] = tile_of(north, north)
    even = is_even("lon")
    head, low = sublanes() < SUB // 2, lanes() < LANES // 2
    blocks = [take_sides(ref.at[t]) for ref in (tiles_first, tiles) for t in range(ref.shape[0])]
    blocks += [jnp.where(low, take_sides(ce.at[r]), take_sides(cn.at[r])) for r in range(nrows)]
    for i in range(0, len(blocks), 2):
        one, two = blocks[i : i + 2]
        east = jnp.where(head, half_turn(one), two)
        west = jnp.where(head, one, half_turn(two))
        span = pl.ds(SUB * (i // 2), SUB)
        la[span, :] = jnp.where(even, east, west)
        lb[span, :] = jnp.where(even, west, east)


def pack_last(pairs, done, nrows, tiles, la, lb, za, zb, side):
    lat_even, lon_even = is_even("lat"), is_even("lon")
    ntiles = nrows * (done + pairs)
    head, low = sublanes() < SUB // 2, lanes() < LANES // 2
    blocks = []
    for i in range(la.shape[0] // SUB):
        span = pl.ds(SUB * i, SUB)
        a, b = la[span, :], lb[span, :]
        east, west = jnp.where(lon_even, a, b), jnp.where(lon_even, b, a)
        blocks += [jnp.where(head, east, half_turn(west)), jnp.where(head, half_turn(east), west)]
    winds = blocks[ntiles:]
    turned = [pltpu.roll(wind, LANES // 2, 1) for wind in winds]
    blocks[ntiles:] = [jnp.where(low, x, y) for x, y in zip(winds, turned)]
    blocks += [jnp.where(low, y, x) for x, y in zip(winds, turned)]
    for t, value in enumerate(blocks):
        side[pl.ds(SUB * t, SUB), :] = value
    north = jnp.where(lat_even, 2, 0)
    at = 2 * pairs * LANES
    row = sublanes()
    outer = (row < 2) | (row >= SUB - 2)

    def corner(p, first):
        start = pl.multiple_of(SUB * (nrows * p + first), SUB)
        one, two = side[pl.ds(start, SUB), :], side[pl.ds(start + SUB, SUB), :]
        return jnp.where(outer, one, half_turn(two))

    for p in range(done + pairs):
        to = pl.ds(at + SUB * p, SUB)
        za[to, :] = corner(p, north)
        zb[to, :] = corner(p, 2 - north)
    to = pl.ds(at + SUB * (done + pairs), SUB)
    top = side[pl.ds(SUB * (ntiles + 2 * nrows - 1), SUB), :]
    za[to, :] = top
    zb[to, :] = top
    for p in range(pairs):
        put_lat_sends(lat_even, tiles, p, nrows, za, zb)


def put_edges(q, first, side, at, nrows, edge_w, edge_e):
    for r in range(nrows):
        beside = side[pl.ds(pl.multiple_of(SUB * (at + r), SUB), SUB), :]
        edge_w[r, pl.ds(SUB, SUB), :] = beside
        edge_w[r, pl.ds(2 * SUB, SUB), :] = q[first + r, pl.ds(0, SUB), :]
        edge_e[r, pl.ds(0, SUB), :] = q[first + r, pl.ds(LANES - SUB, SUB), :]
        edge_e[r, pl.ds(SUB, SUB), :] = beside


def through(c, before, left, right, after):
    return c * (7.0 * (left + right) - (before + after))


def put_fluxes(q, first, nrows, ce, edge_w, edge_e, edge_c, flux):
    for r in range(nrows):
        window = [edge_w[r, pl.ds(SUB + k, SUB), :] for k in range(4)]
        flux[r, pl.ds(1, SUB), :] = through(edge_c[r, pl.ds(SUB + 1, SUB), :], *window)
        for b in range(LANES // SUB):
            at = SUB * b

            def load(shift):
                if at + shift < 0:
                    return edge_w[r, pl.ds(2 * SUB + shift, SUB), :]
                if at + shift + SUB > LANES:
                    return edge_e[r, pl.ds(shift, SUB), :]
                return q[first + r, pl.ds(at + shift, SUB), :]

            flux[r, pl.ds(SUB + at, SUB), :] = through(
                ce[r, pl.ds(at, SUB), :], load(-1), load(0), load(1), load(2)
            )


def lat_divergence(rows, winds):
    north = [through(winds[r], *rows[r : r + 4]) for r in range(len(winds))]
    return [north[r + 1] - north[r] for r in range(len(winds) - 1)]


def sources():
    at, n = lax.axis_index("lat"), lax.axis_size("lat")
    even = lax.rem(at, 2) == 0
    return (even, jnp.logical_not(even), jnp.logical_and(even, at > 0), jnp.logical_and(jnp.logical_not(even), at < n - 1))


def partners(where, ra, rb, span):
    north_a, south_a, south_b, north_b = where
    a, b = ra[span, :], rb[span, :]
    south = jnp.where(south_a, a, jnp.where(south_b, b, 0.0))
    return south, jnp.where(north_a, a, jnp.where(north_b, b, 0.0))


def divergence(q, pair, nrows, b, where, ra, rb, cn, below, flux):
    at = SUB * b
    here = pl.ds(at, SUB)

    def halo(k):
        start = pl.multiple_of((2 * pair + k) * LANES, LANES) + at
        return partners(where, ra, rb, pl.ds(start, SUB))

    (s0, n0), (s1, n1) = halo(0), halo(1)
    own = [q[nrows * pair + r, here, :] for r in range(nrows)]
    winds = [below[here, :]] + [cn[r, here, :] for r in range(nrows)]
    north = lat_divergence([s0, s1] + own + [n0, n1], winds)
    div = []
    for r in range(nrows):
        east = flux[r, pl.ds(SUB + at, SUB), :] - flux[r, pl.ds(SUB + at - 1, SUB), :]
        div.append(east + north[r])
    return own, div


def put_side_section(at, nrows, where, ra, rb, corner, side, ntiles, edge_w, edge_e, edge_c, edge_d, out):
    head = sublanes() < SUB // 2

    def shifted(w, e, r, k):
        return jnp.where(head, e[r, pl.ds(SUB + k, SUB), :], w[r, pl.ds(SUB + k, SUB), :])

    def beside(t):
        return side[pl.ds(pl.multiple_of(SUB * t, SUB), SUB), :]

    start = pl.multiple_of(corner + SUB * (at // nrows), SUB)
    south, above = partners(where, ra, rb, pl.ds(start, SUB))
    s0, s1 = south, half_turn(south)
    n0, n1 = above, half_turn(above)
    own = [beside(at + r) for r in range(nrows)]
    last = pl.ds(corner + SUB * (ntiles // nrows), SUB)
    winds = [partners(where, ra, rb, last)[0]]
    winds += [beside(ntiles + nrows + r) for r in range(nrows)]
    north = lat_divergence([s0, s1] + own + [n0, n1], winds)
    for r in range(nrows):
        v = [shifted(edge_w, edge_e, r, k) for k in range(-2, 3)]
        east = through(beside(ntiles + r), *v[1:])
        west = through(shifted(edge_c, edge_d, r, -1), *v[:-1])
        new = own[r] - ((east - west) + north[r])
        out[pl.ds(pl.multiple_of(SUB * (at + r), SUB), SUB), :] = new


def edge_scratch(nrows):
    return [scratch(nrows, 3 * SUB, LANES)] * 4 + [scratch(nrows, LANES + SUB, LANES)]


def first_stage_early(pairs, nrows, q, ce, cn, side, ra, rb, section, za, zb, below, *edges):
    edge_w, edge_e, edge_c, edge_d, flux = edges
    lat_even, where = is_even("lat"), sources()
    half = LANES // 2
    a = partners(where, ra, rb, pl.ds(2 * pairs * LANES, half))[0]
    turned = pltpu.roll(a, half, 1)
    low = lax.broadcasted_iota(jnp.int32, (half, LANES), 1) < half
    below[pl.ds(0, half), :] = jnp.where(low, a, turned)
    below[pl.ds(half, half), :] = jnp.where(low, turned, a)
    put_edges(ce, 0, side, side.shape[0] // SUB - 2 * nrows, nrows, edge_c, edge_d)

    def one(p, _):
        put_edges(q, nrows * p, side, nrows * p, nrows, edge_w, edge_e)
        put_fluxes(q, nrows * p, nrows, ce, edge_w, edge_e, edge_c, flux)
        for b in range(LANES // SUB):
            own, div = divergence(q, p, nrows, b, where, ra, rb, cn, below, flux)
            for r in range(nrows):
                section[nrows * p + r, pl.ds(SUB * b, SUB), :] = own[r] - div[r]
        put_lat_sends(lat_even, section, p, nrows, za, zb)
        return 0

    lax.fori_loop(0, pairs, one, 0)


def first_stage_late(
    pairs, done, nrows, q, ce, cn, side, ra, rb, below, q_early, section, za, zb, sides, *edges
):
    edge_w, edge_e, edge_c, edge_d, flux = edges
    lat_even, where = is_even("lat"), sources()
    ntiles = nrows * (done + pairs)
    corner = 2 * pairs * LANES
    put_edges(ce, 0, side, ntiles, nrows, edge_c, edge_d)

    def side_section(at):
        put_side_section(
            at, nrows, where, ra, rb, corner, side, ntiles, edge_w, edge_e, edge_c, edge_d, sides
        )

    def one(p, _):
        at = nrows * (done + p)
        put_edges(q, nrows * p, side, at, nrows, edge_w, edge_e)
        put_fluxes(q, nrows * p, nrows, ce, edge_w, edge_e, edge_c, flux)
        for b in range(LANES // SUB):
            own, div = divergence(q, p, nrows, b, where, ra, rb, cn, below, flux)
            for r in range(nrows):
                section[nrows * p + r, pl.ds(SUB * b, SUB), :] = own[r] - div[r]
        put_lat_sends(lat_even, section, p, nrows, za, zb)
        side_section(at)
        return 0

    def another(p, _):
        put_edges(q_early, nrows * p, side, nrows * p, nrows, edge_w, edge_e)
        side_section(nrows * p)
        return 0

    lax.fori_loop(0, pairs, one, 0)
    lax.fori_loop(0, done, another, 0)


def second_stage(pairs, done, nrows, is_first, *refs):
    q, s, ce, cn, below, ra, rb, side, sides, heating = refs[:10]
    buffer, sems, edge_w, edge_e, edge_c, edge_d, flux = refs[-7:]
    out = refs[11]
    levels = LANES // 2
    where = sources()
    if is_first:
        out, heat_out = refs[10:12]
        heat_copy = pltpu.make_async_copy(heating, heat_out, sems.at[pairs])
        heat_copy.start()
    put_edges(ce, 0, side, side.shape[0] // SUB - 2 * nrows, nrows, edge_c, edge_d)

    def copy(p):
        return pltpu.make_async_copy(
            buffer.at[pl.ds(2 * p, 2)], out.at[pl.ds(2 * (done + p), 2)], sems.at[p]
        )

    def one(p, _):
        put_edges(s, nrows * p, sides, nrows * (done + p), nrows, edge_w, edge_e)
        put_fluxes(s, nrows * p, nrows, ce, edge_w, edge_e, edge_c, flux)
        parts = [[] for _ in range(nrows)]
        for b in range(LANES // SUB):
            own, div = divergence(s, p, nrows, b, where, ra, rb, cn, below, flux)
            for r in range(nrows):
                old = q[nrows * p + r, pl.ds(SUB * b, SUB), :]
                parts[r].append(0.5 * ((old + own[r]) - div[r]))
        for r in range(nrows):
            turned = jnp.transpose(jnp.concatenate(parts[r], axis=0))
            for h in range(2):
                buffer[2 * p + h, pl.ds(r, levels, stride=nrows), :] = turned[levels * h : levels * (h + 1)]
        if is_first:

            @pl.when(p == 0)
            def _():
                buffer[0] = buffer[0] + 0.5 * heating[...]

        copy(p).start()
        return 0

    lax.fori_loop(0, pairs, one, 0)
    for p in range(pairs):
        copy(p).wait()
    if is_first:
        heat_copy.wait()


def radiation(
    nat, cosz_in, albedo_in, ext_in, single_in, weight_in, order_in, count_in, after, heat,
    water, depth, save_a, save_b, save_t, save_g, cosz, albedo, ext, single, weight, order, count, sems
):
    del after
    copies = []
    for i, (src, dst) in enumerate(
        (
            (cosz_in, cosz), (albedo_in, albedo), (ext_in, ext), (single_in, single),
            (weight_in, weight), (order_in, order), (count_in, count),
        )
    ):
        copies.append(pltpu.make_async_copy(src, dst, sems.at[i]))
        copies[-1].start()
    nrows, _ = cosz.shape
    levels = nat.shape[1] // nrows
    pairs = ext.shape[0] // 2
    x = nat[1]
    heat[...] = jnp.maximum(x, 0.0) + jnp.log1p(jnp.exp(-jnp.abs(x)))
    total = jnp.zeros((nrows, LANES), jnp.float32)
    depth[0] = jnp.zeros((2 * nrows, LANES), jnp.float32)
    for l in range(levels):
        w = heat[pl.ds(nrows * l, nrows), :]
        total = total + w
        water[l, pl.ds(0, nrows), :] = w
        water[l, pl.ds(nrows, nrows), :] = w
        depth[l + 1, pl.ds(0, nrows), :] = total
        depth[l + 1, pl.ds(nrows, nrows), :] = total
    for copy in copies:
        copy.wait()

    mu = jnp.concatenate([cosz[...], cosz[...]], axis=0)
    floor_albedo = jnp.concatenate([albedo[...], albedo[...]], axis=0)
    first = lax.broadcasted_iota(jnp.int32, (2 * nrows, LANES), 0) < nrows

    def by_band(ref):
        return [jnp.where(first, ref[2 * p], ref[2 * p + 1]) for p in range(pairs)]

    scale = 4.0 / levels
    inv_mu = 1.0 / mu
    ext_of, half_of, weight_of = by_band(ext), by_band(single), by_band(weight)
    beam = [-(e * scale * LOG2E) * inv_mu for e in ext_of]
    diffuse = [-(1.66 * scale * LOG2E) * e for e in ext_of]
    half = [0.5 * s for s in half_of]
    strength = [w * mu for w in weight_of]

    def up(step, carry):
        l = levels - 1 - step
        a_all, b_all, s_all = carry
        w = water[l]
        above = depth[l]
        new_a, new_b, new_s = [], [], []
        for p in range(pairs):
            a, b, s_bot = a_all[p], b_all[p], s_all[p]
            decay = jnp.exp2(diffuse[p] * w)
            s_top = strength[p] * jnp.exp2(beam[p] * above)
            reflect = half[p] - half[p] * decay
            transmit = decay + reflect
            source = half[p] * (s_top - s_bot)
            den = 1.0 - reflect * a
            inv = pl.reciprocal(den, approx=True)
            inv = inv * (2.0 - den * inv)
            t = transmit * inv
            a_here = reflect + transmit * (t * a)
            b_here = t * (a * source + b) + source
            save_t[l, p] = t
            save_g[l, p] = (reflect * b + source) * inv
            save_a[l, p] = 1.0 - a_here
            save_b[l, p] = s_top - b_here
            new_a.append(a_here)
            new_b.append(b_here)
            new_s.append(s_top)
        return tuple(new_a), tuple(new_b), tuple(new_s)

    s_floor = [strength[p] * jnp.exp2(beam[p] * depth[levels]) for p in range(pairs)]
    a_floor = [floor_albedo for _ in range(pairs)]
    b_floor = [floor_albedo * s_floor[p] for p in range(pairs)]
    lax.fori_loop(0, levels, up, (tuple(a_floor), tuple(b_floor), tuple(s_floor)))

    sunlit = []
    column = lax.broadcasted_iota(jnp.int32, (LANES, LANES), 1)
    rank = lax.broadcasted_iota(jnp.int32, (LANES, LANES), 0)
    for r in range(nrows):
        place = jnp.transpose(jnp.broadcast_to(order[r], (LANES, LANES)))
        hit = (place == column) & (rank < count[r])
        sunlit.append(jnp.max(jnp.where(hit, 1.0, 0.0), axis=0, keepdims=True))
    gain = float(levels) * jnp.concatenate(sunlit, axis=0)

    def net_flux(l, d_all):
        net = jnp.zeros((2 * nrows, LANES), jnp.float32)
        for p in range(pairs):
            net = net + (save_b[l, p] + d_all[p] * save_a[l, p])
        return net

    def put(l, absorbed):
        both = absorbed[:nrows] + absorbed[nrows:]
        heat[pl.ds(pl.multiple_of(nrows * l, nrows), nrows), :] = gain * both

    def down(l, carry):
        d_all, net_above = carry
        d_new = tuple(save_t[l - 1, p] * d_all[p] + save_g[l - 1, p] for p in range(pairs))
        net = net_flux(l, d_new)
        put(l - 1, net_above - net)
        return d_new, net

    d_top = tuple(jnp.zeros((2 * nrows, LANES), jnp.float32) for _ in range(pairs))
    d_low, net_low = lax.fori_loop(1, levels, down, (d_top, net_flux(0, d_top)))
    net = jnp.zeros((2 * nrows, LANES), jnp.float32)
    for p in range(pairs):
        d_floor = save_t[levels - 1, p] * d_low[p] + save_g[levels - 1, p]
        net = net + ((s_floor[p] - b_floor[p]) + d_floor * (1.0 - a_floor[p]))
    put(levels - 1, net_low - net)


def in_hbm(x):
    return pltpu.with_memory_space_constraint(x, pltpu.HBM)


def call(kernel, name, out_shape, specs, out_specs, args, scratches, moved=1000, limit=24, **kw):
    return pl.pallas_call(
        kernel,
        out_shape=out_shape,
        in_specs=specs,
        out_specs=out_specs,
        scratch_shapes=scratches,
        compiler_params=pltpu.CompilerParams(vmem_limit_bytes=limit * MIB),
        name=name,
        cost_estimate=pl.CostEstimate(flops=moved, bytes_accessed=moved, transcendentals=0),
        **kw,
    )(*args)


def per_device(
    fields, courant, cos_zenith, albedo, extinction, single_albedo, band_weight, sun_order, sun_count
):
    nfields, levels, nrows, ncols = fields.shape
    flat = fields.reshape(nfields, levels * nrows, ncols)
    wind = courant.reshape(2, levels * nrows, ncols)
    npairs = nfields // 2
    counts = (SPLIT, npairs - SPLIT)
    starts = (0, SPLIT)
    early, late = counts

    z0 = shape((2 * early) * ncols + ncols // 2, LANES)
    tiles0, za, zb, nat, nat_late, nat_wind = call(
        functools.partial(pack_first, early, nrows),
        "pack_first",
        (
            shape(nrows * early, ncols, LANES), z0, z0,
            shape(2 * early, levels * nrows, ncols), shape(2 * late, levels * nrows, ncols),
            shape(2, levels * nrows, ncols),
        ),
        [HBM, HBM],
        (VMEM,) * 6,
        (in_hbm(flat), in_hbm(wind)),
        [pltpu.SemaphoreType.DMA((2 * early + 2,))],
    )
    lat0 = lat_swaps(za, zb)
    ntiles = nrows * npairs
    winds = shape(nrows, ncols, LANES)
    sides = shape(SUB * (ntiles + 2 * nrows), LANES)
    edge = shape(SUB * (ntiles + nrows) // 2, LANES)
    tiles1, ce, cn, la, lb = call(
        functools.partial(pack_middle, late, nrows),
        "pack_middle",
        (shape(nrows * late, ncols, LANES), winds, winds, edge, edge),
        [VMEM] * 3,
        (VMEM,) * 5,
        (nat_late, nat_wind, tiles0),
        [],
    )
    lon = lon_swaps(la, lb)
    z1 = shape(2 * late * ncols + SUB * (npairs + 1), LANES)
    za, zb, side = call(
        functools.partial(pack_last, late, early, nrows),
        "pack_last",
        (z1, z1, sides),
        [VMEM] * 3,
        (VMEM,) * 3,
        (tiles1, *lon),
        [],
    )
    lat1 = lat_swaps(za, zb)

    edges = edge_scratch(nrows)
    z0 = shape(2 * early * ncols, LANES)
    section0, za, zb, below = call(
        functools.partial(first_stage_early, early, nrows),
        "first_stage_early",
        (shape(nrows * early, ncols, LANES), z0, z0, shape(ncols, LANES)),
        [VMEM] * 6,
        (VMEM,) * 4,
        (tiles0, ce, cn, side, *lat0),
        edges,
        moved=1000_000_000,
    )
    lat2 = lat_swaps(za, zb)
    z1 = shape(2 * late * ncols, LANES)
    section1, za, zb, section_side = call(
        functools.partial(first_stage_late, late, early, nrows),
        "first_stage_late",
        (shape(nrows * late, ncols, LANES), z1, z1, shape(SUB * ntiles, LANES)),
        [VMEM] * 8,
        (VMEM,) * 4,
        (tiles1, ce, cn, side, *lat1, below, tiles0),
        edges,
        moved=12_000_000,
    )
    lat3 = lat_swaps(za, zb)

    pairs = extinction.shape[0] // 2
    store = scratch(levels, pairs, 2 * nrows, ncols)
    heating = call(
        radiation,
        "radiation",
        shape(levels * nrows, ncols),
        [VMEM] + [HBM] * 7 + [VMEM],
        VMEM,
        (
            nat, in_hbm(cos_zenith), in_hbm(albedo), in_hbm(extinction), in_hbm(single_albedo),
            in_hbm(band_weight), in_hbm(sun_order), in_hbm(sun_count.reshape(nrows)), section_side,
        ),
        [
            scratch(levels, 2 * nrows, ncols), scratch(levels + 1, 2 * nrows, ncols),
            store, store, store, store,
            scratch(nrows, ncols), scratch(nrows, ncols),
            pltpu.SMEM(extinction.shape, jnp.float32), pltpu.SMEM(extinction.shape, jnp.float32),
            pltpu.SMEM(extinction.shape, jnp.float32), pltpu.VMEM((nrows, 1, ncols), jnp.int32),
            pltpu.SMEM((nrows,), jnp.int32), pltpu.SemaphoreType.DMA((7,)),
        ],
        moved=16_000_000,
    )

    out = heat_out = None
    for g, (tiles, section, lat) in enumerate(((tiles0, section0, lat2), (tiles1, section1, lat3))):
        args = [tiles, section, ce, cn, below, *lat, side, section_side, heating]
        specs = [VMEM] * len(args)
        results = [shape(nfields, levels * nrows, ncols), shape(levels * nrows, ncols)]
        aliases = {}
        if g:
            aliases = {len(args): 0}
            args.append(out)
            specs.append(HBM)
            results.pop()
        out, *rest = call(
            functools.partial(second_stage, counts[g], starts[g], nrows, g == 0),
            f"second_stage_{g}",
            results,
            specs,
            [HBM] * len(results),
            args,
            [
                scratch(2 * counts[g], levels * nrows, ncols),
                pltpu.SemaphoreType.DMA((counts[g] + 1,)),
                *edges,
            ],
            input_output_aliases=aliases,
        )
        if not g:
            heat_out = rest[0]
    return out.reshape(fields.shape), heat_out.reshape(levels, nrows, ncols)


def solution(mesh):
    in_specs = (
        P(None, None, "lat", "lon"),
        P(None, None, "lat", "lon"),
        P("lat", "lon"),
        P("lat", "lon"),
        P(),
        P(),
        P(),
        P("lat", "lon", None),
        P("lat", "lon"),
    )
    out_specs = (P(None, None, "lat", "lon"), P(None, "lat", "lon"))
    return jax.shard_map(
        per_device, mesh=mesh, in_specs=in_specs, out_specs=out_specs, check_vma=False
    )
```

```python
import functools
import math

import jax
import jax.numpy as jnp
from jax import lax
from jax.experimental import pallas as pl
from jax.experimental.pallas import tpu as pltpu
from jax.sharding import PartitionSpec as P

SPLIT = 2
MOVED = 1
SUB = 8
LANES = 128
LOG2E = math.log2(math.e)
VMEM = pl.BlockSpec(memory_space=pltpu.VMEM)
HBM = pl.BlockSpec(memory_space=pltpu.HBM)
MIB = 1024 * 1024


def scratch(*dims):
    return pltpu.VMEM(dims, jnp.float32)


def shape(*dims):
    return jax.ShapeDtypeStruct(dims, jnp.float32)


def lon_swaps(first_block, second_block):
    n = lax.axis_size("lon")
    first = [(i, i ^ 1) for i in range(n)]
    second = [(i, (i + 1 if i % 2 else i - 1) % n) for i in range(n)]
    return lax.ppermute(first_block, "lon", first), lax.ppermute(second_block, "lon", second)


def lat_swaps(first_block, second_block):
    nlon, nlat = lax.axis_size("lon"), lax.axis_size("lat")
    second = []
    for i in range(nlon):
        for j in range(nlat):
            k = j + 1 if j % 2 else j - 1
            to = i * nlat + k if 0 <= k < nlat else (i ^ 1) * nlat + j
            second.append((i * nlat + j, to))
    got = lax.ppermute(second_block, ("lon", "lat"), second)
    return lax.ppermute(first_block, "lat", [(j, j ^ 1) for j in range(nlat)]), got


def is_even(axis):
    return lax.rem(lax.axis_index(axis), 2) == 0


def sublanes():
    return lax.broadcasted_iota(jnp.int32, (SUB, LANES), 0)


def lanes():
    return lax.broadcasted_iota(jnp.int32, (SUB, LANES), 1)


def half_turn(block):
    return pltpu.roll(block, SUB // 2, 0)


def native(ref, index, r, nrows):
    levels = ref.shape[1] // nrows
    return ref[index, pl.ds(r, levels, stride=nrows), :]


def tile_of(low, high):
    return jnp.transpose(jnp.concatenate([low, high], axis=0))


def put_lat_sends(even, tiles, pair, nrows, za, zb):
    north = jnp.where(even, 2, 0)
    for k in range(2):
        span = pl.ds(pl.multiple_of((2 * pair + k) * LANES, LANES), LANES)
        za[span, :] = tiles[nrows * pair + north + k]
        zb[span, :] = tiles[nrows * pair + (2 - north) + k]


def take_sides(tile):
    head = sublanes() < SUB // 2
    return jnp.where(head, tile[pl.ds(0, SUB), :], tile[pl.ds(LANES - SUB, SUB), :])


def pack_first(pairs, nrows, fields, courant, tiles, za, zb, nat, nat_late, nat_wind, sems):
    n = 2 * pairs
    copies = [pltpu.make_async_copy(fields.at[i], nat.at[i], sems.at[i]) for i in range(n)]
    wind = pltpu.make_async_copy(courant, nat_wind, sems.at[n])
    late = [
        pltpu.make_async_copy(fields.at[pl.ds(n + i, 2)], nat_late.at[pl.ds(i, 2)], sems.at[n + 1 + i // 2])
        for i in range(0, nat_late.shape[0], 2)
    ]
    for copy in copies + [wind] + late:
        copy.start()
    even = is_even("lat")
    for p in range(pairs):
        copies[2 * p].wait()
        copies[2 * p + 1].wait()
        for r in range(nrows):
            tiles[nrows * p + r] = tile_of(native(nat, 2 * p, r, nrows), native(nat, 2 * p + 1, r, nrows))
        put_lat_sends(even, tiles, p, nrows, za, zb)
    wind.wait()
    top = native(nat_wind, 1, nrows - 1, nrows) * (1.0 / 12.0)
    top = tile_of(top, top)
    half = LANES // 2
    lane = lax.broadcasted_iota(jnp.int32, (half, LANES), 1)
    top = jnp.where(lane < half, top[:half], top[half:])
    span = pl.ds((2 * pairs + MOVED) * LANES, half)
    za[span, :] = top
    zb[span, :] = top
    for copy in late:
        copy.wait()
    for i in range(MOVED):
        p, k = divmod(i, 2)
        low, high = (
            tile_of(native(nat_late, 2 * p, r, nrows), native(nat_late, 2 * p + 1, r, nrows)) for r in (k, k + 2)
        )
        span = pl.ds((2 * pairs + i) * LANES, LANES)
        za[span, :] = jnp.where(even, high, low)
        zb[span, :] = jnp.where(even, low, high)


def pack_middle(pairs, nrows, nat, nat_wind, tiles_first, tiles, ce, cn, la, lb):
    for p in range(pairs):
        for r in range(nrows):
            tiles[nrows * p + r] = tile_of(native(nat, 2 * p, r, nrows), native(nat, 2 * p + 1, r, nrows))
    for r in range(nrows):
        east = native(nat_wind, 0, r, nrows) * (1.0 / 12.0)
        north = native(nat_wind, 1, r, nrows) * (1.0 / 12.0)
        ce[r] = tile_of(east, east)
        cn[r] = tile_of(north, north)
    even = is_even("lon")
    head, low = sublanes() < SUB // 2, lanes() < LANES // 2
    blocks = [take_sides(ref.at[t]) for ref in (tiles_first, tiles) for t in range(ref.shape[0])]
    blocks += [jnp.where(low, take_sides(ce.at[r]), take_sides(cn.at[r])) for r in range(nrows)]
    for i in range(0, len(blocks), 2):
        one, two = blocks[i : i + 2]
        east = jnp.where(head, half_turn(one), two)
        west = jnp.where(head, one, half_turn(two))
        span = pl.ds(SUB * (i // 2), SUB)
        la[span, :] = jnp.where(even, east, west)
        lb[span, :] = jnp.where(even, west, east)


def pack_last(pairs, done, nrows, tiles, la, lb, za, zb, side):
    lat_even, lon_even = is_even("lat"), is_even("lon")
    ntiles = nrows * (done + pairs)
    head, low = sublanes() < SUB // 2, lanes() < LANES // 2
    blocks = []
    for i in range(la.shape[0] // SUB):
        span = pl.ds(SUB * i, SUB)
        a, b = la[span, :], lb[span, :]
        east, west = jnp.where(lon_even, a, b), jnp.where(lon_even, b, a)
        blocks += [jnp.where(head, east, half_turn(west)), jnp.where(head, half_turn(east), west)]
    winds = blocks[ntiles:]
    turned = [pltpu.roll(wind, LANES // 2, 1) for wind in winds]
    blocks[ntiles:] = [jnp.where(low, x, y) for x, y in zip(winds, turned)]
    blocks += [jnp.where(low, y, x) for x, y in zip(winds, turned)]
    for t, value in enumerate(blocks):
        side[pl.ds(SUB * t, SUB), :] = value
    north = jnp.where(lat_even, 2, 0)
    at = (2 * pairs - MOVED) * LANES
    row = sublanes()
    outer = (row < 2) | (row >= SUB - 2)

    def corner(p, first):
        start = pl.multiple_of(SUB * (nrows * p + first), SUB)
        one, two = side[pl.ds(start, SUB), :], side[pl.ds(start + SUB, SUB), :]
        return jnp.where(outer, one, half_turn(two))

    for p in range(done + pairs):
        to = pl.ds(at + SUB * p, SUB)
        za[to, :] = corner(p, north)
        zb[to, :] = corner(p, 2 - north)
    to = pl.ds(at + SUB * (done + pairs), SUB)
    top = side[pl.ds(SUB * (ntiles + 2 * nrows - 1), SUB), :]
    za[to, :] = top
    zb[to, :] = top
    for i in range(MOVED, 2 * pairs):
        p, k = divmod(i, 2)
        span = pl.ds((i - MOVED) * LANES, LANES)
        za[span, :] = tiles[nrows * p + north + k]
        zb[span, :] = tiles[nrows * p + (2 - north) + k]


def put_edges(q, first, side, at, nrows, edge_w, edge_e):
    for r in range(nrows):
        beside = side[pl.ds(pl.multiple_of(SUB * (at + r), SUB), SUB), :]
        edge_w[r, pl.ds(SUB, SUB), :] = beside
        edge_w[r, pl.ds(2 * SUB, SUB), :] = q[first + r, pl.ds(0, SUB), :]
        edge_e[r, pl.ds(0, SUB), :] = q[first + r, pl.ds(LANES - SUB, SUB), :]
        edge_e[r, pl.ds(SUB, SUB), :] = beside


def through(c, before, left, right, after):
    return c * (7.0 * (left + right) - (before + after))


def put_fluxes(q, first, nrows, ce, edge_w, edge_e, edge_c, flux):
    for r in range(nrows):
        window = [edge_w[r, pl.ds(SUB + k, SUB), :] for k in range(4)]
        flux[r, pl.ds(1, SUB), :] = through(edge_c[r, pl.ds(SUB + 1, SUB), :], *window)
        for b in range(LANES // SUB):
            at = SUB * b

            def load(shift):
                if at + shift < 0:
                    return edge_w[r, pl.ds(2 * SUB + shift, SUB), :]
                if at + shift + SUB > LANES:
                    return edge_e[r, pl.ds(shift, SUB), :]
                return q[first + r, pl.ds(at + shift, SUB), :]

            flux[r, pl.ds(SUB + at, SUB), :] = through(
                ce[r, pl.ds(at, SUB), :], load(-1), load(0), load(1), load(2)
            )


def lat_divergence(rows, winds):
    north = [through(winds[r], *rows[r : r + 4]) for r in range(len(winds))]
    return [north[r + 1] - north[r] for r in range(len(winds) - 1)]


def sources():
    at, n = lax.axis_index("lat"), lax.axis_size("lat")
    even = lax.rem(at, 2) == 0
    return (even, jnp.logical_not(even), jnp.logical_and(even, at > 0), jnp.logical_and(jnp.logical_not(even), at < n - 1))


def partners(where, ra, rb, span):
    north_a, south_a, south_b, north_b = where
    a, b = ra[span, :], rb[span, :]
    south = jnp.where(south_a, a, jnp.where(south_b, b, 0.0))
    return south, jnp.where(north_a, a, jnp.where(north_b, b, 0.0))


def divergence(q, pair, nrows, b, halo, cn, below, flux):
    at = SUB * b
    here = pl.ds(at, SUB)
    (s0, n0), (s1, n1) = halo(0, at), halo(1, at)
    own = [q[nrows * pair + r, here, :] for r in range(nrows)]
    winds = [below[here, :]] + [cn[r, here, :] for r in range(nrows)]
    north = lat_divergence([s0, s1] + own + [n0, n1], winds)
    div = []
    for r in range(nrows):
        east = flux[r, pl.ds(SUB + at, SUB), :] - flux[r, pl.ds(SUB + at - 1, SUB), :]
        div.append(east + north[r])
    return own, div


def put_side_section(at, nrows, where, ra, rb, corner, side, ntiles, edge_w, edge_e, edge_c, edge_d, out):
    head = sublanes() < SUB // 2

    def shifted(w, e, r, k):
        return jnp.where(head, e[r, pl.ds(SUB + k, SUB), :], w[r, pl.ds(SUB + k, SUB), :])

    def beside(t):
        return side[pl.ds(pl.multiple_of(SUB * t, SUB), SUB), :]

    start = pl.multiple_of(corner + SUB * (at // nrows), SUB)
    south, above = partners(where, ra, rb, pl.ds(start, SUB))
    s0, s1 = south, half_turn(south)
    n0, n1 = above, half_turn(above)
    own = [beside(at + r) for r in range(nrows)]
    last = pl.ds(corner + SUB * (ntiles // nrows), SUB)
    winds = [partners(where, ra, rb, last)[0]]
    winds += [beside(ntiles + nrows + r) for r in range(nrows)]
    north = lat_divergence([s0, s1] + own + [n0, n1], winds)
    for r in range(nrows):
        v = [shifted(edge_w, edge_e, r, k) for k in range(-2, 3)]
        east = through(beside(ntiles + r), *v[1:])
        west = through(shifted(edge_c, edge_d, r, -1), *v[:-1])
        new = own[r] - ((east - west) + north[r])
        out[pl.ds(pl.multiple_of(SUB * (at + r), SUB), SUB), :] = new


def edge_scratch(nrows):
    return [scratch(nrows, 3 * SUB, LANES)] * 4 + [scratch(nrows, LANES + SUB, LANES)]


def first_stage_early(pairs, nrows, q, ce, cn, side, ra, rb, section, za, zb, below, *edges):
    edge_w, edge_e, edge_c, edge_d, flux = edges
    lat_even, where = is_even("lat"), sources()
    half = LANES // 2
    a = partners(where, ra, rb, pl.ds((2 * pairs + MOVED) * LANES, half))[0]
    turned = pltpu.roll(a, half, 1)
    low = lax.broadcasted_iota(jnp.int32, (half, LANES), 1) < half
    below[pl.ds(0, half), :] = jnp.where(low, a, turned)
    below[pl.ds(half, half), :] = jnp.where(low, turned, a)
    put_edges(ce, 0, side, side.shape[0] // SUB - 2 * nrows, nrows, edge_c, edge_d)

    def one(p, _):
        def halo(k, shift):
            start = pl.multiple_of((2 * p + k) * LANES, LANES)
            return partners(where, ra, rb, pl.ds(start + shift, SUB))

        put_edges(q, nrows * p, side, nrows * p, nrows, edge_w, edge_e)
        put_fluxes(q, nrows * p, nrows, ce, edge_w, edge_e, edge_c, flux)
        for b in range(LANES // SUB):
            own, div = divergence(q, p, nrows, b, halo, cn, below, flux)
            for r in range(nrows):
                section[nrows * p + r, pl.ds(SUB * b, SUB), :] = own[r] - div[r]
        put_lat_sends(lat_even, section, p, nrows, za, zb)
        return 0

    lax.fori_loop(0, pairs, one, 0)


def first_stage_late(
    pairs, done, nrows, q, ce, cn, side, ra, rb, ra_first, rb_first, below, q_early, section, za, zb, sides, *edges
):
    edge_w, edge_e, edge_c, edge_d, flux = edges
    lat_even, where = is_even("lat"), sources()
    ntiles = nrows * (done + pairs)
    corner = (2 * pairs - MOVED) * LANES
    put_edges(ce, 0, side, ntiles, nrows, edge_c, edge_d)

    def side_section(at):
        put_side_section(
            at, nrows, where, ra, rb, corner, side, ntiles, edge_w, edge_e, edge_c, edge_d, sides
        )

    def one(p):
        def halo(k, shift):
            i = 2 * p + k
            if i < MOVED:
                return partners(where, ra_first, rb_first, pl.ds((2 * done + i) * LANES + shift, SUB))
            return partners(where, ra, rb, pl.ds((i - MOVED) * LANES + shift, SUB))

        at = nrows * (done + p)
        put_edges(q, nrows * p, side, at, nrows, edge_w, edge_e)
        put_fluxes(q, nrows * p, nrows, ce, edge_w, edge_e, edge_c, flux)
        for b in range(LANES // SUB):
            own, div = divergence(q, p, nrows, b, halo, cn, below, flux)
            for r in range(nrows):
                section[nrows * p + r, pl.ds(SUB * b, SUB), :] = own[r] - div[r]
        put_lat_sends(lat_even, section, p, nrows, za, zb)
        side_section(at)

    def another(p, _):
        put_edges(q_early, nrows * p, side, nrows * p, nrows, edge_w, edge_e)
        side_section(nrows * p)
        return 0

    for p in range(pairs):
        one(p)
    lax.fori_loop(0, done, another, 0)


def second_stage(pairs, done, nrows, is_first, *refs):
    q, s, ce, cn, below, ra, rb, side, sides, heating = refs[:10]
    buffer, sems, edge_w, edge_e, edge_c, edge_d, flux = refs[-7:]
    out = refs[11]
    levels = LANES // 2
    where = sources()
    if is_first:
        out, heat_out = refs[10:12]
        heat_copy = pltpu.make_async_copy(heating, heat_out, sems.at[pairs])
        heat_copy.start()
    put_edges(ce, 0, side, side.shape[0] // SUB - 2 * nrows, nrows, edge_c, edge_d)

    def copy(p):
        return pltpu.make_async_copy(
            buffer.at[pl.ds(2 * p, 2)], out.at[pl.ds(2 * (done + p), 2)], sems.at[p]
        )

    def one(p, _):
        def halo(k, shift):
            start = pl.multiple_of((2 * p + k) * LANES, LANES)
            return partners(where, ra, rb, pl.ds(start + shift, SUB))

        put_edges(s, nrows * p, sides, nrows * (done + p), nrows, edge_w, edge_e)
        put_fluxes(s, nrows * p, nrows, ce, edge_w, edge_e, edge_c, flux)
        parts = [[] for _ in range(nrows)]
        for b in range(LANES // SUB):
            own, div = divergence(s, p, nrows, b, halo, cn, below, flux)
            for r in range(nrows):
                old = q[nrows * p + r, pl.ds(SUB * b, SUB), :]
                parts[r].append(0.5 * ((old + own[r]) - div[r]))
        for r in range(nrows):
            turned = jnp.transpose(jnp.concatenate(parts[r], axis=0))
            for h in range(2):
                buffer[2 * p + h, pl.ds(r, levels, stride=nrows), :] = turned[levels * h : levels * (h + 1)]
        if is_first:

            @pl.when(p == 0)
            def _():
                buffer[0] = buffer[0] + 0.5 * heating[...]

        copy(p).start()
        return 0

    lax.fori_loop(0, pairs, one, 0)
    for p in range(pairs):
        copy(p).wait()
    if is_first:
        heat_copy.wait()


def radiation(
    nat, cosz_in, albedo_in, ext_in, single_in, weight_in, order_in, count_in, after, heat,
    water, depth, save_a, save_b, save_t, save_g, cosz, albedo, ext, single, weight, order, count, sems
):
    del after
    copies = []
    for i, (src, dst) in enumerate(
        (
            (cosz_in, cosz), (albedo_in, albedo), (ext_in, ext), (single_in, single),
            (weight_in, weight), (order_in, order), (count_in, count),
        )
    ):
        copies.append(pltpu.make_async_copy(src, dst, sems.at[i]))
        copies[-1].start()
    nrows, _ = cosz.shape
    levels = nat.shape[1] // nrows
    pairs = ext.shape[0] // 2
    x = nat[1]
    heat[...] = jnp.maximum(x, 0.0) + jnp.log1p(jnp.exp(-jnp.abs(x)))
    total = jnp.zeros((nrows, LANES), jnp.float32)
    depth[0] = jnp.zeros((2 * nrows, LANES), jnp.float32)
    for l in range(levels):
        w = heat[pl.ds(nrows * l, nrows), :]
        total = total + w
        water[l, pl.ds(0, nrows), :] = w
        water[l, pl.ds(nrows, nrows), :] = w
        depth[l + 1, pl.ds(0, nrows), :] = total
        depth[l + 1, pl.ds(nrows, nrows), :] = total
    for copy in copies:
        copy.wait()

    mu = jnp.concatenate([cosz[...], cosz[...]], axis=0)
    floor_albedo = jnp.concatenate([albedo[...], albedo[...]], axis=0)
    first = lax.broadcasted_iota(jnp.int32, (2 * nrows, LANES), 0) < nrows

    def by_band(ref):
        return [jnp.where(first, ref[2 * p], ref[2 * p + 1]) for p in range(pairs)]

    scale = 4.0 / levels
    inv_mu = 1.0 / mu
    ext_of, half_of, weight_of = by_band(ext), by_band(single), by_band(weight)
    beam = [-(e * scale * LOG2E) * inv_mu for e in ext_of]
    diffuse = [-(1.66 * scale * LOG2E) * e for e in ext_of]
    half = [0.5 * s for s in half_of]
    strength = [w * mu for w in weight_of]

    def up(step, carry):
        l = levels - 1 - step
        a_all, b_all, s_all = carry
        w = water[l]
        above = depth[l]
        new_a, new_b, new_s = [], [], []
        for p in range(pairs):
            a, b, s_bot = a_all[p], b_all[p], s_all[p]
            decay = jnp.exp2(diffuse[p] * w)
            s_top = strength[p] * jnp.exp2(beam[p] * above)
            reflect = half[p] - half[p] * decay
            transmit = decay + reflect
            source = half[p] * (s_top - s_bot)
            den = 1.0 - reflect * a
            inv = pl.reciprocal(den, approx=True)
            inv = inv * (2.0 - den * inv)
            t = transmit * inv
            a_here = reflect + transmit * (t * a)
            b_here = t * (a * source + b) + source
            save_t[l, p] = t
            save_g[l, p] = (reflect * b + source) * inv
            save_a[l, p] = 1.0 - a_here
            save_b[l, p] = s_top - b_here
            new_a.append(a_here)
            new_b.append(b_here)
            new_s.append(s_top)
        return tuple(new_a), tuple(new_b), tuple(new_s)

    s_floor = [strength[p] * jnp.exp2(beam[p] * depth[levels]) for p in range(pairs)]
    a_floor = [floor_albedo for _ in range(pairs)]
    b_floor = [floor_albedo * s_floor[p] for p in range(pairs)]
    lax.fori_loop(0, levels, up, (tuple(a_floor), tuple(b_floor), tuple(s_floor)))

    sunlit = []
    column = lax.broadcasted_iota(jnp.int32, (LANES, LANES), 1)
    rank = lax.broadcasted_iota(jnp.int32, (LANES, LANES), 0)
    for r in range(nrows):
        place = jnp.transpose(jnp.broadcast_to(order[r], (LANES, LANES)))
        hit = (place == column) & (rank < count[r])
        sunlit.append(jnp.max(jnp.where(hit, 1.0, 0.0), axis=0, keepdims=True))
    gain = float(levels) * jnp.concatenate(sunlit, axis=0)

    def net_flux(l, d_all):
        net = jnp.zeros((2 * nrows, LANES), jnp.float32)
        for p in range(pairs):
            net = net + (save_b[l, p] + d_all[p] * save_a[l, p])
        return net

    def put(l, absorbed):
        both = absorbed[:nrows] + absorbed[nrows:]
        heat[pl.ds(pl.multiple_of(nrows * l, nrows), nrows), :] = gain * both

    def down(l, carry):
        d_all, net_above = carry
        d_new = tuple(save_t[l - 1, p] * d_all[p] + save_g[l - 1, p] for p in range(pairs))
        net = net_flux(l, d_new)
        put(l - 1, net_above - net)
        return d_new, net

    d_top = tuple(jnp.zeros((2 * nrows, LANES), jnp.float32) for _ in range(pairs))
    d_low, net_low = lax.fori_loop(1, levels, down, (d_top, net_flux(0, d_top)))
    net = jnp.zeros((2 * nrows, LANES), jnp.float32)
    for p in range(pairs):
        d_floor = save_t[levels - 1, p] * d_low[p] + save_g[levels - 1, p]
        net = net + ((s_floor[p] - b_floor[p]) + d_floor * (1.0 - a_floor[p]))
    put(levels - 1, net_low - net)


def in_hbm(x):
    return pltpu.with_memory_space_constraint(x, pltpu.HBM)


def call(kernel, name, out_shape, specs, out_specs, args, scratches, moved=1000, limit=24, **kw):
    return pl.pallas_call(
        kernel,
        out_shape=out_shape,
        in_specs=specs,
        out_specs=out_specs,
        scratch_shapes=scratches,
        compiler_params=pltpu.CompilerParams(vmem_limit_bytes=limit * MIB),
        name=name,
        cost_estimate=pl.CostEstimate(flops=moved, bytes_accessed=moved, transcendentals=0),
        **kw,
    )(*args)


def per_device(
    fields, courant, cos_zenith, albedo, extinction, single_albedo, band_weight, sun_order, sun_count
):
    nfields, levels, nrows, ncols = fields.shape
    flat = fields.reshape(nfields, levels * nrows, ncols)
    wind = courant.reshape(2, levels * nrows, ncols)
    npairs = nfields // 2
    counts = (SPLIT, npairs - SPLIT)
    starts = (0, SPLIT)
    early, late = counts

    z0 = shape((2 * early + MOVED) * ncols + ncols // 2, LANES)
    tiles0, za, zb, nat, nat_late, nat_wind = call(
        functools.partial(pack_first, early, nrows),
        "pack_first",
        (
            shape(nrows * early, ncols, LANES), z0, z0,
            shape(2 * early, levels * nrows, ncols), shape(2 * late, levels * nrows, ncols),
            shape(2, levels * nrows, ncols),
        ),
        [HBM, HBM],
        (VMEM,) * 6,
        (in_hbm(flat), in_hbm(wind)),
        [pltpu.SemaphoreType.DMA((2 * early + 1 + late,))],
    )
    lat0 = lat_swaps(za, zb)
    ntiles = nrows * npairs
    winds = shape(nrows, ncols, LANES)
    sides = shape(SUB * (ntiles + 2 * nrows), LANES)
    edge = shape(SUB * (ntiles + nrows) // 2, LANES)
    tiles1, ce, cn, la, lb = call(
        functools.partial(pack_middle, late, nrows),
        "pack_middle",
        (shape(nrows * late, ncols, LANES), winds, winds, edge, edge),
        [VMEM] * 3,
        (VMEM,) * 5,
        (nat_late, nat_wind, tiles0),
        [],
    )
    lon = lon_swaps(la, lb)
    z1 = shape((2 * late - MOVED) * ncols + SUB * (npairs + 1), LANES)
    za, zb, side = call(
        functools.partial(pack_last, late, early, nrows),
        "pack_last",
        (z1, z1, sides),
        [VMEM] * 3,
        (VMEM,) * 3,
        (tiles1, *lon),
        [],
    )
    lat1 = lat_swaps(za, zb)

    edges = edge_scratch(nrows)
    z0 = shape(2 * early * ncols, LANES)
    section0, za, zb, below = call(
        functools.partial(first_stage_early, early, nrows),
        "first_stage_early",
        (shape(nrows * early, ncols, LANES), z0, z0, shape(ncols, LANES)),
        [VMEM] * 6,
        (VMEM,) * 4,
        (tiles0, ce, cn, side, *lat0),
        edges,
        moved=1000_000_000,
    )
    lat2 = lat_swaps(za, zb)
    z1 = shape(2 * late * ncols, LANES)
    section1, za, zb, section_side = call(
        functools.partial(first_stage_late, late, early, nrows),
        "first_stage_late",
        (shape(nrows * late, ncols, LANES), z1, z1, shape(SUB * ntiles, LANES)),
        [VMEM] * 10,
        (VMEM,) * 4,
        (tiles1, ce, cn, side, *lat1, *lat0, below, tiles0),
        edges,
        moved=12_000_000,
    )
    lat3 = lat_swaps(za, zb)

    pairs = extinction.shape[0] // 2
    store = scratch(levels, pairs, 2 * nrows, ncols)
    heating = call(
        radiation,
        "radiation",
        shape(levels * nrows, ncols),
        [VMEM] + [HBM] * 7 + [VMEM],
        VMEM,
        (
            nat, in_hbm(cos_zenith), in_hbm(albedo), in_hbm(extinction), in_hbm(single_albedo),
            in_hbm(band_weight), in_hbm(sun_order), in_hbm(sun_count.reshape(nrows)), section_side,
        ),
        [
            scratch(levels, 2 * nrows, ncols), scratch(levels + 1, 2 * nrows, ncols),
            store, store, store, store,
            scratch(nrows, ncols), scratch(nrows, ncols),
            pltpu.SMEM(extinction.shape, jnp.float32), pltpu.SMEM(extinction.shape, jnp.float32),
            pltpu.SMEM(extinction.shape, jnp.float32), pltpu.VMEM((nrows, 1, ncols), jnp.int32),
            pltpu.SMEM((nrows,), jnp.int32), pltpu.SemaphoreType.DMA((7,)),
        ],
        moved=16_000_000,
    )

    out = heat_out = None
    for g, (tiles, section, lat) in enumerate(((tiles0, section0, lat2), (tiles1, section1, lat3))):
        args = [tiles, section, ce, cn, below, *lat, side, section_side, heating]
        specs = [VMEM] * len(args)
        results = [shape(nfields, levels * nrows, ncols), shape(levels * nrows, ncols)]
        aliases = {}
        if g:
            aliases = {len(args): 0}
            args.append(out)
            specs.append(HBM)
            results.pop()
        out, *rest = call(
            functools.partial(second_stage, counts[g], starts[g], nrows, g == 0),
            f"second_stage_{g}",
            results,
            specs,
            [HBM] * len(results),
            args,
            [
                scratch(2 * counts[g], levels * nrows, ncols),
                pltpu.SemaphoreType.DMA((counts[g] + 1,)),
                *edges,
            ],
            input_output_aliases=aliases,
        )
        if not g:
            heat_out = rest[0]
    return out.reshape(fields.shape), heat_out.reshape(levels, nrows, ncols)


def solution(mesh):
    in_specs = (
        P(None, None, "lat", "lon"),
        P(None, None, "lat", "lon"),
        P("lat", "lon"),
        P("lat", "lon"),
        P(),
        P(),
        P(),
        P("lat", "lon", None),
        P("lat", "lon"),
    )
    out_specs = (P(None, None, "lat", "lon"), P(None, "lat", "lon"))
    return jax.shard_map(
        per_device, mesh=mesh, in_specs=in_specs, out_specs=out_specs, check_vma=False
    )
```

```python
import functools
import math

import jax
import jax.numpy as jnp
from jax import lax
from jax.experimental import pallas as pl
from jax.experimental.pallas import tpu as pltpu
from jax.sharding import PartitionSpec as P

SPLIT = 2
MOVED = 1
SUB = 8
LANES = 128
LOG2E = math.log2(math.e)
VMEM = pl.BlockSpec(memory_space=pltpu.VMEM)
HBM = pl.BlockSpec(memory_space=pltpu.HBM)
MIB = 1024 * 1024


def scratch(*dims):
    return pltpu.VMEM(dims, jnp.float32)


def shape(*dims):
    return jax.ShapeDtypeStruct(dims, jnp.float32)


def lon_swaps(first_block, second_block):
    n = lax.axis_size("lon")
    first = [(i, i ^ 1) for i in range(n)]
    second = [(i, (i + 1 if i % 2 else i - 1) % n) for i in range(n)]
    return lax.ppermute(first_block, "lon", first), lax.ppermute(second_block, "lon", second)


def lat_swaps(first_block, second_block):
    nlon, nlat = lax.axis_size("lon"), lax.axis_size("lat")
    second = []
    for i in range(nlon):
        for j in range(nlat):
            k = j + 1 if j % 2 else j - 1
            to = i * nlat + k if 0 <= k < nlat else (i ^ 1) * nlat + j
            second.append((i * nlat + j, to))
    got = lax.ppermute(second_block, ("lon", "lat"), second)
    return lax.ppermute(first_block, "lat", [(j, j ^ 1) for j in range(nlat)]), got


def is_even(axis):
    return lax.rem(lax.axis_index(axis), 2) == 0


def sublanes():
    return lax.broadcasted_iota(jnp.int32, (SUB, LANES), 0)


def lanes():
    return lax.broadcasted_iota(jnp.int32, (SUB, LANES), 1)


def half_turn(block):
    return pltpu.roll(block, SUB // 2, 0)


def native(ref, index, r, nrows):
    levels = ref.shape[1] // nrows
    return ref[index, pl.ds(r, levels, stride=nrows), :]


def tile_of(low, high):
    return jnp.transpose(jnp.concatenate([low, high], axis=0))


def put_lat_sends(even, tiles, pair, nrows, za, zb):
    north = jnp.where(even, 2, 0)
    for k in range(2):
        span = pl.ds(pl.multiple_of((2 * pair + k) * LANES, LANES), LANES)
        za[span, :] = tiles[nrows * pair + north + k]
        zb[span, :] = tiles[nrows * pair + (2 - north) + k]


def take_sides(tile):
    head = sublanes() < SUB // 2
    return jnp.where(head, tile[pl.ds(0, SUB), :], tile[pl.ds(LANES - SUB, SUB), :])


def pack_first(pairs, nrows, fields, courant, tiles, za, zb, nat, nat_late, nat_wind, sems):
    n = 2 * pairs
    copies = [pltpu.make_async_copy(fields.at[i], nat.at[i], sems.at[i]) for i in range(n)]
    wind = pltpu.make_async_copy(courant, nat_wind, sems.at[n])
    late = [
        pltpu.make_async_copy(fields.at[pl.ds(n + i, 2)], nat_late.at[pl.ds(i, 2)], sems.at[n + 1 + i // 2])
        for i in range(0, nat_late.shape[0], 2)
    ]
    for copy in copies + [wind] + late:
        copy.start()
    even = is_even("lat")
    for p in range(pairs):
        copies[2 * p].wait()
        copies[2 * p + 1].wait()
        for r in range(nrows):
            tiles[nrows * p + r] = tile_of(native(nat, 2 * p, r, nrows), native(nat, 2 * p + 1, r, nrows))
        put_lat_sends(even, tiles, p, nrows, za, zb)
    wind.wait()
    top = native(nat_wind, 1, nrows - 1, nrows) * (1.0 / 12.0)
    top = tile_of(top, top)
    half = LANES // 2
    lane = lax.broadcasted_iota(jnp.int32, (half, LANES), 1)
    top = jnp.where(lane < half, top[:half], top[half:])
    span = pl.ds((2 * pairs + MOVED) * LANES, half)
    za[span, :] = top
    zb[span, :] = top
    for copy in late:
        copy.wait()
    for i in range(MOVED):
        p, k = divmod(i, 2)
        low, high = (
            tile_of(native(nat_late, 2 * p, r, nrows), native(nat_late, 2 * p + 1, r, nrows)) for r in (k, k + 2)
        )
        span = pl.ds((2 * pairs + i) * LANES, LANES)
        za[span, :] = jnp.where(even, high, low)
        zb[span, :] = jnp.where(even, low, high)


def pack_middle(pairs, nrows, nat, nat_wind, tiles_first, tiles, ce, cn, la, lb):
    for p in range(pairs):
        for r in range(nrows):
            tiles[nrows * p + r] = tile_of(native(nat, 2 * p, r, nrows), native(nat, 2 * p + 1, r, nrows))
    for r in range(nrows):
        east = native(nat_wind, 0, r, nrows) * (1.0 / 12.0)
        north = native(nat_wind, 1, r, nrows) * (1.0 / 12.0)
        ce[r] = tile_of(east, east)
        cn[r] = tile_of(north, north)
    even = is_even("lon")
    head, low = sublanes() < SUB // 2, lanes() < LANES // 2
    blocks = [take_sides(ref.at[t]) for ref in (tiles_first, tiles) for t in range(ref.shape[0])]
    blocks += [jnp.where(low, take_sides(ce.at[r]), take_sides(cn.at[r])) for r in range(nrows)]
    for i in range(0, len(blocks), 2):
        one, two = blocks[i : i + 2]
        east = jnp.where(head, half_turn(one), two)
        west = jnp.where(head, one, half_turn(two))
        span = pl.ds(SUB * (i // 2), SUB)
        la[span, :] = jnp.where(even, east, west)
        lb[span, :] = jnp.where(even, west, east)


def pack_last(pairs, done, nrows, tiles, la, lb, za, zb, side):
    lat_even, lon_even = is_even("lat"), is_even("lon")
    ntiles = nrows * (done + pairs)
    head, low = sublanes() < SUB // 2, lanes() < LANES // 2
    blocks = []
    for i in range(la.shape[0] // SUB):
        span = pl.ds(SUB * i, SUB)
        a, b = la[span, :], lb[span, :]
        east, west = jnp.where(lon_even, a, b), jnp.where(lon_even, b, a)
        blocks += [jnp.where(head, east, half_turn(west)), jnp.where(head, half_turn(east), west)]
    winds = blocks[ntiles:]
    turned = [pltpu.roll(wind, LANES // 2, 1) for wind in winds]
    blocks[ntiles:] = [jnp.where(low, x, y) for x, y in zip(winds, turned)]
    blocks += [jnp.where(low, y, x) for x, y in zip(winds, turned)]
    for t, value in enumerate(blocks):
        side[pl.ds(SUB * t, SUB), :] = value
    north = jnp.where(lat_even, 2, 0)
    at = (2 * pairs - MOVED) * LANES
    row = sublanes()
    outer = (row < 2) | (row >= SUB - 2)

    def corner(p, first):
        start = pl.multiple_of(SUB * (nrows * p + first), SUB)
        one, two = side[pl.ds(start, SUB), :], side[pl.ds(start + SUB, SUB), :]
        return jnp.where(outer, one, half_turn(two))

    for p in range(done + pairs):
        to = pl.ds(at + SUB * p, SUB)
        za[to, :] = corner(p, north)
        zb[to, :] = corner(p, 2 - north)
    to = pl.ds(at + SUB * (done + pairs), SUB)
    top = side[pl.ds(SUB * (ntiles + 2 * nrows - 1), SUB), :]
    za[to, :] = top
    zb[to, :] = top
    for i in range(MOVED, 2 * pairs):
        p, k = divmod(i, 2)
        span = pl.ds((i - MOVED) * LANES, LANES)
        za[span, :] = tiles[nrows * p + north + k]
        zb[span, :] = tiles[nrows * p + (2 - north) + k]


def put_edges(q, first, side, at, nrows, edge_w, edge_e):
    for r in range(nrows):
        beside = side[pl.ds(pl.multiple_of(SUB * (at + r), SUB), SUB), :]
        edge_w[r, pl.ds(SUB, SUB), :] = beside
        edge_w[r, pl.ds(2 * SUB, SUB), :] = q[first + r, pl.ds(0, SUB), :]
        edge_e[r, pl.ds(0, SUB), :] = q[first + r, pl.ds(LANES - SUB, SUB), :]
        edge_e[r, pl.ds(SUB, SUB), :] = beside


def through(c, before, left, right, after):
    return c * (7.0 * (left + right) - (before + after))


def put_fluxes(q, first, nrows, ce, edge_w, edge_e, edge_c, flux):
    for r in range(nrows):
        window = [edge_w[r, pl.ds(SUB + k, SUB), :] for k in range(4)]
        flux[r, pl.ds(1, SUB), :] = through(edge_c[r, pl.ds(SUB + 1, SUB), :], *window)
        for b in range(LANES // SUB):
            at = SUB * b

            def load(shift):
                if at + shift < 0:
                    return edge_w[r, pl.ds(2 * SUB + shift, SUB), :]
                if at + shift + SUB > LANES:
                    return edge_e[r, pl.ds(shift, SUB), :]
                return q[first + r, pl.ds(at + shift, SUB), :]

            flux[r, pl.ds(SUB + at, SUB), :] = through(
                ce[r, pl.ds(at, SUB), :], load(-1), load(0), load(1), load(2)
            )


def lat_divergence(rows, winds):
    north = [through(winds[r], *rows[r : r + 4]) for r in range(len(winds))]
    return [north[r + 1] - north[r] for r in range(len(winds) - 1)]


def sources():
    at, n = lax.axis_index("lat"), lax.axis_size("lat")
    even = lax.rem(at, 2) == 0
    return (even, jnp.logical_not(even), jnp.logical_and(even, at > 0), jnp.logical_and(jnp.logical_not(even), at < n - 1))


def partners(where, ra, rb, span):
    north_a, south_a, south_b, north_b = where
    a, b = ra[span, :], rb[span, :]
    south = jnp.where(south_a, a, jnp.where(south_b, b, 0.0))
    return south, jnp.where(north_a, a, jnp.where(north_b, b, 0.0))


def divergence(q, pair, nrows, b, halo, cn, below, flux):
    at = SUB * b
    here = pl.ds(at, SUB)
    (s0, n0), (s1, n1) = halo(0, at), halo(1, at)
    own = [q[nrows * pair + r, here, :] for r in range(nrows)]
    winds = [below[here, :]] + [cn[r, here, :] for r in range(nrows)]
    north = lat_divergence([s0, s1] + own + [n0, n1], winds)
    div = []
    for r in range(nrows):
        east = flux[r, pl.ds(SUB + at, SUB), :] - flux[r, pl.ds(SUB + at - 1, SUB), :]
        div.append(east + north[r])
    return own, div


def put_side_section(at, nrows, where, ra, rb, corner, side, ntiles, edge_w, edge_e, edge_c, edge_d, out):
    head = sublanes() < SUB // 2

    def shifted(w, e, r, k):
        return jnp.where(head, e[r, pl.ds(SUB + k, SUB), :], w[r, pl.ds(SUB + k, SUB), :])

    def beside(t):
        return side[pl.ds(pl.multiple_of(SUB * t, SUB), SUB), :]

    start = pl.multiple_of(corner + SUB * (at // nrows), SUB)
    south, above = partners(where, ra, rb, pl.ds(start, SUB))
    s0, s1 = south, half_turn(south)
    n0, n1 = above, half_turn(above)
    own = [beside(at + r) for r in range(nrows)]
    last = pl.ds(corner + SUB * (ntiles // nrows), SUB)
    winds = [partners(where, ra, rb, last)[0]]
    winds += [beside(ntiles + nrows + r) for r in range(nrows)]
    north = lat_divergence([s0, s1] + own + [n0, n1], winds)
    for r in range(nrows):
        v = [shifted(edge_w, edge_e, r, k) for k in range(-2, 3)]
        east = through(beside(ntiles + r), *v[1:])
        west = through(shifted(edge_c, edge_d, r, -1), *v[:-1])
        new = own[r] - ((east - west) + north[r])
        out[pl.ds(pl.multiple_of(SUB * (at + r), SUB), SUB), :] = new


def edge_scratch(nrows):
    return [scratch(nrows, 3 * SUB, LANES)] * 4 + [scratch(nrows, LANES + SUB, LANES)]


def first_stage_early(pairs, nrows, q, ce, cn, side, ra, rb, section, za, zb, below, *edges):
    edge_w, edge_e, edge_c, edge_d, flux = edges
    lat_even, where = is_even("lat"), sources()
    half = LANES // 2
    a = partners(where, ra, rb, pl.ds((2 * pairs + MOVED) * LANES, half))[0]
    turned = pltpu.roll(a, half, 1)
    low = lax.broadcasted_iota(jnp.int32, (half, LANES), 1) < half
    below[pl.ds(0, half), :] = jnp.where(low, a, turned)
    below[pl.ds(half, half), :] = jnp.where(low, turned, a)
    put_edges(ce, 0, side, side.shape[0] // SUB - 2 * nrows, nrows, edge_c, edge_d)

    def one(p, _):
        def halo(k, shift):
            start = pl.multiple_of((2 * p + k) * LANES, LANES)
            return partners(where, ra, rb, pl.ds(start + shift, SUB))

        put_edges(q, nrows * p, side, nrows * p, nrows, edge_w, edge_e)
        put_fluxes(q, nrows * p, nrows, ce, edge_w, edge_e, edge_c, flux)
        for b in range(LANES // SUB):
            own, div = divergence(q, p, nrows, b, halo, cn, below, flux)
            for r in range(nrows):
                section[nrows * p + r, pl.ds(SUB * b, SUB), :] = own[r] - div[r]
        put_lat_sends(lat_even, section, p, nrows, za, zb)
        return 0

    lax.fori_loop(0, pairs, one, 0)


def first_stage_late(
    pairs, done, nrows, q, ce, cn, side, ra, rb, ra_first, rb_first, below, q_early, section, za, zb, sides, *edges
):
    edge_w, edge_e, edge_c, edge_d, flux = edges
    lat_even, where = is_even("lat"), sources()
    ntiles = nrows * (done + pairs)
    corner = (2 * pairs - MOVED) * LANES
    put_edges(ce, 0, side, ntiles, nrows, edge_c, edge_d)

    def side_section(at):
        put_side_section(
            at, nrows, where, ra, rb, corner, side, ntiles, edge_w, edge_e, edge_c, edge_d, sides
        )

    def one(p):
        def halo(k, shift):
            i = 2 * p + k
            if i < MOVED:
                return partners(where, ra_first, rb_first, pl.ds((2 * done + i) * LANES + shift, SUB))
            return partners(where, ra, rb, pl.ds((i - MOVED) * LANES + shift, SUB))

        at = nrows * (done + p)
        put_edges(q, nrows * p, side, at, nrows, edge_w, edge_e)
        put_fluxes(q, nrows * p, nrows, ce, edge_w, edge_e, edge_c, flux)
        for b in range(LANES // SUB):
            own, div = divergence(q, p, nrows, b, halo, cn, below, flux)
            for r in range(nrows):
                section[nrows * p + r, pl.ds(SUB * b, SUB), :] = own[r] - div[r]
        put_lat_sends(lat_even, section, p, nrows, za, zb)
        side_section(at)

    def another(p, _):
        put_edges(q_early, nrows * p, side, nrows * p, nrows, edge_w, edge_e)
        side_section(nrows * p)
        return 0

    for p in range(pairs):
        one(p)
    lax.fori_loop(0, done, another, 0)


def put_rows(buffer, pair, rows, nrows):
    levels = LANES // 2
    for r in range(nrows):
        turned = jnp.transpose(jnp.concatenate(rows[r], axis=0))
        for h in range(2):
            buffer[2 * pair + h, pl.ds(r, levels, stride=nrows), :] = turned[levels * h : levels * (h + 1)]


def second_stage_early(
    pairs, later, nrows, q, s, ce, cn, below, ra, rb, side, sides, heating, q_late, s_late,
    out, heat_out, part, buffer, sems, *edges
):
    edge_w, edge_e, edge_c, edge_d, flux = edges
    where = sources()
    heat_copy = pltpu.make_async_copy(heating, heat_out, sems.at[pairs])
    heat_copy.start()
    put_edges(ce, 0, side, side.shape[0] // SUB - 2 * nrows, nrows, edge_c, edge_d)

    def copy(p):
        return pltpu.make_async_copy(buffer.at[pl.ds(2 * p, 2)], out.at[pl.ds(2 * p, 2)], sems.at[p])

    def one(p, _):
        def halo(k, shift):
            start = pl.multiple_of((2 * p + k) * LANES, LANES)
            return partners(where, ra, rb, pl.ds(start + shift, SUB))

        put_edges(s, nrows * p, sides, nrows * p, nrows, edge_w, edge_e)
        put_fluxes(s, nrows * p, nrows, ce, edge_w, edge_e, edge_c, flux)
        parts = [[] for _ in range(nrows)]
        for b in range(LANES // SUB):
            own, div = divergence(s, p, nrows, b, halo, cn, below, flux)
            for r in range(nrows):
                old = q[nrows * p + r, pl.ds(SUB * b, SUB), :]
                parts[r].append(0.5 * ((old + own[r]) - div[r]))
        put_rows(buffer, p, parts, nrows)

        @pl.when(p == 0)
        def _():
            buffer[0] = buffer[0] + 0.5 * heating[...]

        copy(p).start()
        return 0

    def another(p, _):
        put_edges(s_late, nrows * p, sides, nrows * (pairs + p), nrows, edge_w, edge_e)
        put_fluxes(s_late, nrows * p, nrows, ce, edge_w, edge_e, edge_c, flux)
        for b in range(LANES // SUB):
            here = pl.ds(SUB * b, SUB)
            s0, s1, s2, s3 = own = [s_late[nrows * p + r, here, :] for r in range(nrows)]
            c = [below[here, :]] + [cn[r, here, :] for r in range(nrows)]
            north = [
                c[0] * (7.0 * s0 - s1),
                c[1] * (7.0 * (s0 + s1) - s2),
                through(c[2], *own),
                c[3] * (7.0 * (s2 + s3) - s1),
                c[4] * (7.0 * s3 - s2),
            ]
            for r in range(nrows):
                east = flux[r, pl.ds(SUB * (b + 1), SUB), :] - flux[r, pl.ds(SUB * (b + 1) - 1, SUB), :]
                old = q_late[nrows * p + r, here, :]
                part[nrows * p + r, here, :] = 0.5 * ((old + own[r]) - (east + (north[r + 1] - north[r])))
        return 0

    lax.fori_loop(0, pairs, one, 0)
    lax.fori_loop(0, later, another, 0)
    for p in range(pairs):
        copy(p).wait()
    heat_copy.wait()


def second_stage_late(pairs, done, nrows, part, cn, below, ra, rb, before, out, buffer, sems):
    del before
    where = sources()

    def copy(p):
        return pltpu.make_async_copy(
            buffer.at[pl.ds(2 * p, 2)], out.at[pl.ds(2 * (done + p), 2)], sems.at[p]
        )

    def one(p, _):
        rows = [[] for _ in range(nrows)]
        for b in range(LANES // SUB):
            here = pl.ds(SUB * b, SUB)

            def halo(k):
                start = pl.multiple_of((2 * p + k) * LANES, LANES) + SUB * b
                return partners(where, ra, rb, pl.ds(start, SUB))

            (south_two, north_one), (south_one, north_two) = halo(0), halo(1)
            low = 0.5 * cn[0, here, :] * south_one
            high = 0.5 * cn[2, here, :] * north_one
            bottom = 0.5 * below[here, :] * (7.0 * south_one - south_two)
            top = 0.5 * cn[3, here, :] * (7.0 * north_one - north_two)
            p0, p1, p2, p3 = (part[nrows * p + r, here, :] for r in range(nrows))
            for r, value in enumerate((p0 + (low + bottom), p1 - low, p2 + high, p3 - (top + high))):
                rows[r].append(value)
        put_rows(buffer, p, rows, nrows)
        copy(p).start()
        return 0

    lax.fori_loop(0, pairs, one, 0)
    for p in range(pairs):
        copy(p).wait()


def radiation(
    nat, cosz_in, albedo_in, ext_in, single_in, weight_in, order_in, count_in, after, heat,
    water, depth, save_a, save_b, save_t, save_g, cosz, albedo, ext, single, weight, order, count, sems
):
    del after
    copies = []
    for i, (src, dst) in enumerate(
        (
            (cosz_in, cosz), (albedo_in, albedo), (ext_in, ext), (single_in, single),
            (weight_in, weight), (order_in, order), (count_in, count),
        )
    ):
        copies.append(pltpu.make_async_copy(src, dst, sems.at[i]))
        copies[-1].start()
    nrows, _ = cosz.shape
    levels = nat.shape[1] // nrows
    pairs = ext.shape[0] // 2
    x = nat[1]
    heat[...] = jnp.maximum(x, 0.0) + jnp.log1p(jnp.exp(-jnp.abs(x)))
    total = jnp.zeros((nrows, LANES), jnp.float32)
    depth[0] = jnp.zeros((2 * nrows, LANES), jnp.float32)
    for l in range(levels):
        w = heat[pl.ds(nrows * l, nrows), :]
        total = total + w
        water[l, pl.ds(0, nrows), :] = w
        water[l, pl.ds(nrows, nrows), :] = w
        depth[l + 1, pl.ds(0, nrows), :] = total
        depth[l + 1, pl.ds(nrows, nrows), :] = total
    for copy in copies:
        copy.wait()

    mu = jnp.concatenate([cosz[...], cosz[...]], axis=0)
    floor_albedo = jnp.concatenate([albedo[...], albedo[...]], axis=0)
    first = lax.broadcasted_iota(jnp.int32, (2 * nrows, LANES), 0) < nrows

    def by_band(ref):
        return [jnp.where(first, ref[2 * p], ref[2 * p + 1]) for p in range(pairs)]

    scale = 4.0 / levels
    inv_mu = 1.0 / mu
    ext_of, half_of, weight_of = by_band(ext), by_band(single), by_band(weight)
    beam = [-(e * scale * LOG2E) * inv_mu for e in ext_of]
    diffuse = [-(1.66 * scale * LOG2E) * e for e in ext_of]
    half = [0.5 * s for s in half_of]
    strength = [w * mu for w in weight_of]

    def up(step, carry):
        l = levels - 1 - step
        a_all, b_all, s_all = carry
        w = water[l]
        above = depth[l]
        new_a, new_b, new_s = [], [], []
        for p in range(pairs):
            a, b, s_bot = a_all[p], b_all[p], s_all[p]
            decay = jnp.exp2(diffuse[p] * w)
            s_top = strength[p] * jnp.exp2(beam[p] * above)
            reflect = half[p] - half[p] * decay
            transmit = decay + reflect
            source = half[p] * (s_top - s_bot)
            den = 1.0 - reflect * a
            inv = pl.reciprocal(den, approx=True)
            inv = inv * (2.0 - den * inv)
            t = transmit * inv
            a_here = reflect + transmit * (t * a)
            b_here = t * (a * source + b) + source
            save_t[l, p] = t
            save_g[l, p] = (reflect * b + source) * inv
            save_a[l, p] = 1.0 - a_here
            save_b[l, p] = s_top - b_here
            new_a.append(a_here)
            new_b.append(b_here)
            new_s.append(s_top)
        return tuple(new_a), tuple(new_b), tuple(new_s)

    s_floor = [strength[p] * jnp.exp2(beam[p] * depth[levels]) for p in range(pairs)]
    a_floor = [floor_albedo for _ in range(pairs)]
    b_floor = [floor_albedo * s_floor[p] for p in range(pairs)]
    lax.fori_loop(0, levels, up, (tuple(a_floor), tuple(b_floor), tuple(s_floor)))

    sunlit = []
    column = lax.broadcasted_iota(jnp.int32, (LANES, LANES), 1)
    rank = lax.broadcasted_iota(jnp.int32, (LANES, LANES), 0)
    for r in range(nrows):
        place = jnp.transpose(jnp.broadcast_to(order[r], (LANES, LANES)))
        hit = (place == column) & (rank < count[r])
        sunlit.append(jnp.max(jnp.where(hit, 1.0, 0.0), axis=0, keepdims=True))
    gain = float(levels) * jnp.concatenate(sunlit, axis=0)

    def net_flux(l, d_all):
        net = jnp.zeros((2 * nrows, LANES), jnp.float32)
        for p in range(pairs):
            net = net + (save_b[l, p] + d_all[p] * save_a[l, p])
        return net

    def put(l, absorbed):
        both = absorbed[:nrows] + absorbed[nrows:]
        heat[pl.ds(pl.multiple_of(nrows * l, nrows), nrows), :] = gain * both

    def down(l, carry):
        d_all, net_above = carry
        d_new = tuple(save_t[l - 1, p] * d_all[p] + save_g[l - 1, p] for p in range(pairs))
        net = net_flux(l, d_new)
        put(l - 1, net_above - net)
        return d_new, net

    d_top = tuple(jnp.zeros((2 * nrows, LANES), jnp.float32) for _ in range(pairs))
    d_low, net_low = lax.fori_loop(1, levels, down, (d_top, net_flux(0, d_top)))
    net = jnp.zeros((2 * nrows, LANES), jnp.float32)
    for p in range(pairs):
        d_floor = save_t[levels - 1, p] * d_low[p] + save_g[levels - 1, p]
        net = net + ((s_floor[p] - b_floor[p]) + d_floor * (1.0 - a_floor[p]))
    put(levels - 1, net_low - net)


def in_hbm(x):
    return pltpu.with_memory_space_constraint(x, pltpu.HBM)


def call(kernel, name, out_shape, specs, out_specs, args, scratches, moved=1000, limit=24, **kw):
    return pl.pallas_call(
        kernel,
        out_shape=out_shape,
        in_specs=specs,
        out_specs=out_specs,
        scratch_shapes=scratches,
        compiler_params=pltpu.CompilerParams(vmem_limit_bytes=limit * MIB),
        name=name,
        cost_estimate=pl.CostEstimate(flops=moved, bytes_accessed=moved, transcendentals=0),
        **kw,
    )(*args)


def per_device(
    fields, courant, cos_zenith, albedo, extinction, single_albedo, band_weight, sun_order, sun_count
):
    nfields, levels, nrows, ncols = fields.shape
    flat = fields.reshape(nfields, levels * nrows, ncols)
    wind = courant.reshape(2, levels * nrows, ncols)
    npairs = nfields // 2
    early, late = SPLIT, npairs - SPLIT

    z0 = shape((2 * early + MOVED) * ncols + ncols // 2, LANES)
    tiles0, za, zb, nat, nat_late, nat_wind = call(
        functools.partial(pack_first, early, nrows),
        "pack_first",
        (
            shape(nrows * early, ncols, LANES), z0, z0,
            shape(2 * early, levels * nrows, ncols), shape(2 * late, levels * nrows, ncols),
            shape(2, levels * nrows, ncols),
        ),
        [HBM, HBM],
        (VMEM,) * 6,
        (in_hbm(flat), in_hbm(wind)),
        [pltpu.SemaphoreType.DMA((2 * early + 1 + late,))],
    )
    lat0 = lat_swaps(za, zb)
    ntiles = nrows * npairs
    winds = shape(nrows, ncols, LANES)
    sides = shape(SUB * (ntiles + 2 * nrows), LANES)
    edge = shape(SUB * (ntiles + nrows) // 2, LANES)
    tiles1, ce, cn, la, lb = call(
        functools.partial(pack_middle, late, nrows),
        "pack_middle",
        (shape(nrows * late, ncols, LANES), winds, winds, edge, edge),
        [VMEM] * 3,
        (VMEM,) * 5,
        (nat_late, nat_wind, tiles0),
        [],
    )
    lon = lon_swaps(la, lb)
    z1 = shape((2 * late - MOVED) * ncols + SUB * (npairs + 1), LANES)
    za, zb, side = call(
        functools.partial(pack_last, late, early, nrows),
        "pack_last",
        (z1, z1, sides),
        [VMEM] * 3,
        (VMEM,) * 3,
        (tiles1, *lon),
        [],
    )
    lat1 = lat_swaps(za, zb)

    edges = edge_scratch(nrows)
    z0 = shape(2 * early * ncols, LANES)
    section0, za, zb, below = call(
        functools.partial(first_stage_early, early, nrows),
        "first_stage_early",
        (shape(nrows * early, ncols, LANES), z0, z0, shape(ncols, LANES)),
        [VMEM] * 6,
        (VMEM,) * 4,
        (tiles0, ce, cn, side, *lat0),
        edges,
        moved=1000_000_000,
    )
    lat2 = lat_swaps(za, zb)
    z1 = shape(2 * late * ncols, LANES)
    section1, za, zb, section_side = call(
        functools.partial(first_stage_late, late, early, nrows),
        "first_stage_late",
        (shape(nrows * late, ncols, LANES), z1, z1, shape(SUB * ntiles, LANES)),
        [VMEM] * 10,
        (VMEM,) * 4,
        (tiles1, ce, cn, side, *lat1, *lat0, below, tiles0),
        edges,
        moved=12_000_000,
    )
    lat3 = lat_swaps(za, zb)

    pairs = extinction.shape[0] // 2
    store = scratch(levels, pairs, 2 * nrows, ncols)
    heating = call(
        radiation,
        "radiation",
        shape(levels * nrows, ncols),
        [VMEM] + [HBM] * 7 + [VMEM],
        VMEM,
        (
            nat, in_hbm(cos_zenith), in_hbm(albedo), in_hbm(extinction), in_hbm(single_albedo),
            in_hbm(band_weight), in_hbm(sun_order), in_hbm(sun_count.reshape(nrows)), section_side,
        ),
        [
            scratch(levels, 2 * nrows, ncols), scratch(levels + 1, 2 * nrows, ncols),
            store, store, store, store,
            scratch(nrows, ncols), scratch(nrows, ncols),
            pltpu.SMEM(extinction.shape, jnp.float32), pltpu.SMEM(extinction.shape, jnp.float32),
            pltpu.SMEM(extinction.shape, jnp.float32), pltpu.VMEM((nrows, 1, ncols), jnp.int32),
            pltpu.SMEM((nrows,), jnp.int32), pltpu.SemaphoreType.DMA((7,)),
        ],
        moved=16_000_000,
    )

    full = shape(nfields, levels * nrows, ncols)
    out, heat_out, part = call(
        functools.partial(second_stage_early, early, late, nrows),
        "second_stage_early",
        (full, shape(levels * nrows, ncols), shape(nrows * late, ncols, LANES)),
        [VMEM] * 12,
        (HBM, HBM, VMEM),
        (tiles0, section0, ce, cn, below, *lat2, side, section_side, heating, tiles1, section1),
        [scratch(2 * early, levels * nrows, ncols), pltpu.SemaphoreType.DMA((early + 1,)), *edges],
    )
    out = call(
        functools.partial(second_stage_late, late, early, nrows),
        "second_stage_late",
        full,
        [VMEM] * 5 + [HBM],
        HBM,
        (part, cn, below, *lat3, out),
        [scratch(2 * late, levels * nrows, ncols), pltpu.SemaphoreType.DMA((late,))],
        input_output_aliases={5: 0},
    )
    return out.reshape(fields.shape), heat_out.reshape(levels, nrows, ncols)


def solution(mesh):
    in_specs = (
        P(None, None, "lat", "lon"),
        P(None, None, "lat", "lon"),
        P("lat", "lon"),
        P("lat", "lon"),
        P(),
        P(),
        P(),
        P("lat", "lon", None),
        P("lat", "lon"),
    )
    out_specs = (P(None, None, "lat", "lon"), P(None, "lat", "lon"))
    return jax.shard_map(
        per_device, mesh=mesh, in_specs=in_specs, out_specs=out_specs, check_vma=False
    )
```

```python
import functools
import math

import jax
import jax.numpy as jnp
from jax import lax
from jax.experimental import pallas as pl
from jax.experimental.pallas import tpu as pltpu
from jax.sharding import PartitionSpec as P

SPLIT = 2
MOVED = 0
SUB = 8
LANES = 128
LOG2E = math.log2(math.e)
VMEM = pl.BlockSpec(memory_space=pltpu.VMEM)
HBM = pl.BlockSpec(memory_space=pltpu.HBM)
MIB = 1024 * 1024


def scratch(*dims):
    return pltpu.VMEM(dims, jnp.float32)


def shape(*dims):
    return jax.ShapeDtypeStruct(dims, jnp.float32)


def lon_swaps(first_block, second_block):
    n = lax.axis_size("lon")
    first = [(i, i ^ 1) for i in range(n)]
    second = [(i, (i + 1 if i % 2 else i - 1) % n) for i in range(n)]
    return lax.ppermute(first_block, "lon", first), lax.ppermute(second_block, "lon", second)


def lat_swaps(first_block, second_block):
    nlon, nlat = lax.axis_size("lon"), lax.axis_size("lat")
    second = []
    for i in range(nlon):
        for j in range(nlat):
            k = j + 1 if j % 2 else j - 1
            to = i * nlat + k if 0 <= k < nlat else (i ^ 1) * nlat + j
            second.append((i * nlat + j, to))
    got = lax.ppermute(second_block, ("lon", "lat"), second)
    return lax.ppermute(first_block, "lat", [(j, j ^ 1) for j in range(nlat)]), got


def is_even(axis):
    return lax.rem(lax.axis_index(axis), 2) == 0


def sublanes():
    return lax.broadcasted_iota(jnp.int32, (SUB, LANES), 0)


def lanes():
    return lax.broadcasted_iota(jnp.int32, (SUB, LANES), 1)


def half_turn(block):
    return pltpu.roll(block, SUB // 2, 0)


def native(ref, index, r, nrows):
    levels = ref.shape[1] // nrows
    return ref[index, pl.ds(r, levels, stride=nrows), :]


def tile_of(low, high):
    return jnp.transpose(jnp.concatenate([low, high], axis=0))


def put_lat_sends(even, tiles, pair, nrows, za, zb):
    north = jnp.where(even, 2, 0)
    for k in range(2):
        span = pl.ds(pl.multiple_of((2 * pair + k) * LANES, LANES), LANES)
        za[span, :] = tiles[nrows * pair + north + k]
        zb[span, :] = tiles[nrows * pair + (2 - north) + k]


def take_sides(tile):
    head = sublanes() < SUB // 2
    return jnp.where(head, tile[pl.ds(0, SUB), :], tile[pl.ds(LANES - SUB, SUB), :])


def pack_first(pairs, nrows, fields, courant, tiles, za, zb, nat, nat_late, nat_wind, sems):
    n = 2 * pairs
    copies = [pltpu.make_async_copy(fields.at[i], nat.at[i], sems.at[i]) for i in range(n)]
    wind = pltpu.make_async_copy(courant, nat_wind, sems.at[n])
    late = [
        pltpu.make_async_copy(fields.at[pl.ds(n + i, 2)], nat_late.at[pl.ds(i, 2)], sems.at[n + 1 + i // 2])
        for i in range(0, nat_late.shape[0], 2)
    ]
    for copy in copies + [wind] + late:
        copy.start()
    even = is_even("lat")
    for p in range(pairs):
        copies[2 * p].wait()
        copies[2 * p + 1].wait()
        for r in range(nrows):
            tiles[nrows * p + r] = tile_of(native(nat, 2 * p, r, nrows), native(nat, 2 * p + 1, r, nrows))
        put_lat_sends(even, tiles, p, nrows, za, zb)
    wind.wait()
    top = native(nat_wind, 1, nrows - 1, nrows) * (1.0 / 12.0)
    top = tile_of(top, top)
    half = LANES // 2
    lane = lax.broadcasted_iota(jnp.int32, (half, LANES), 1)
    top = jnp.where(lane < half, top[:half], top[half:])
    span = pl.ds((2 * pairs + MOVED) * LANES, half)
    za[span, :] = top
    zb[span, :] = top
    for copy in late:
        copy.wait()
    for i in range(MOVED):
        p, k = divmod(i, 2)
        low, high = (
            tile_of(native(nat_late, 2 * p, r, nrows), native(nat_late, 2 * p + 1, r, nrows)) for r in (k, k + 2)
        )
        span = pl.ds((2 * pairs + i) * LANES, LANES)
        za[span, :] = jnp.where(even, high, low)
        zb[span, :] = jnp.where(even, low, high)


def pack_middle(pairs, nrows, nat, nat_wind, tiles_first, tiles, ce, cn, la, lb, za, zb):
    up = jnp.where(is_even("lat"), 2, 0)
    for p in range(pairs):
        for r in range(nrows):
            tiles[nrows * p + r] = tile_of(native(nat, 2 * p, r, nrows), native(nat, 2 * p + 1, r, nrows))
    for r in range(nrows):
        east = native(nat_wind, 0, r, nrows) * (1.0 / 12.0)
        north = native(nat_wind, 1, r, nrows) * (1.0 / 12.0)
        ce[r] = tile_of(east, east)
        cn[r] = tile_of(north, north)
    for i in range(MOVED, 2 * pairs):
        p, k = divmod(i, 2)
        span = pl.ds((i - MOVED) * LANES, LANES)
        za[span, :] = tiles[nrows * p + up + k]
        zb[span, :] = tiles[nrows * p + (2 - up) + k]
    even = is_even("lon")
    head, low = sublanes() < SUB // 2, lanes() < LANES // 2
    blocks = [take_sides(ref.at[t]) for ref in (tiles_first, tiles) for t in range(ref.shape[0])]
    blocks += [jnp.where(low, take_sides(ce.at[r]), take_sides(cn.at[r])) for r in range(nrows)]
    for i in range(0, len(blocks), 2):
        one, two = blocks[i : i + 2]
        east = jnp.where(head, half_turn(one), two)
        west = jnp.where(head, one, half_turn(two))
        span = pl.ds(SUB * (i // 2), SUB)
        la[span, :] = jnp.where(even, east, west)
        lb[span, :] = jnp.where(even, west, east)


def put_side(la, lb, ntiles, side):
    lon_even = is_even("lon")
    head, low = sublanes() < SUB // 2, lanes() < LANES // 2
    blocks = []
    for i in range(la.shape[0] // SUB):
        span = pl.ds(SUB * i, SUB)
        a, b = la[span, :], lb[span, :]
        east, west = jnp.where(lon_even, a, b), jnp.where(lon_even, b, a)
        blocks += [jnp.where(head, east, half_turn(west)), jnp.where(head, half_turn(east), west)]
    winds = blocks[ntiles:]
    turned = [pltpu.roll(wind, LANES // 2, 1) for wind in winds]
    blocks[ntiles:] = [jnp.where(low, x, y) for x, y in zip(winds, turned)]
    blocks += [jnp.where(low, y, x) for x, y in zip(winds, turned)]
    for t, value in enumerate(blocks):
        side[pl.ds(SUB * t, SUB), :] = value


def put_corners(lat_even, ntiles, nrows, at, side, za, zb):
    row = sublanes()
    outer = (row < 2) | (row >= SUB - 2)
    north = jnp.where(lat_even, 2, 0)

    def corner(p, first):
        start = pl.multiple_of(SUB * (nrows * p + first), SUB)
        one, two = side[pl.ds(start, SUB), :], side[pl.ds(start + SUB, SUB), :]
        return jnp.where(outer, one, half_turn(two))

    npairs = ntiles // nrows
    for p in range(npairs):
        to = pl.ds(at + SUB * p, SUB)
        za[to, :] = corner(p, north)
        zb[to, :] = corner(p, 2 - north)
    to = pl.ds(at + SUB * npairs, SUB)
    top = side[pl.ds(SUB * (ntiles + 2 * nrows - 1), SUB), :]
    za[to, :] = top
    zb[to, :] = top


def put_edges(q, first, side, at, nrows, edge_w, edge_e):
    for r in range(nrows):
        beside = side[pl.ds(pl.multiple_of(SUB * (at + r), SUB), SUB), :]
        edge_w[r, pl.ds(SUB, SUB), :] = beside
        edge_w[r, pl.ds(2 * SUB, SUB), :] = q[first + r, pl.ds(0, SUB), :]
        edge_e[r, pl.ds(0, SUB), :] = q[first + r, pl.ds(LANES - SUB, SUB), :]
        edge_e[r, pl.ds(SUB, SUB), :] = beside


def through(c, before, left, right, after):
    return c * (7.0 * (left + right) - (before + after))


def put_fluxes(q, first, nrows, ce, edge_w, edge_e, edge_c, flux):
    for r in range(nrows):
        window = [edge_w[r, pl.ds(SUB + k, SUB), :] for k in range(4)]
        flux[r, pl.ds(1, SUB), :] = through(edge_c[r, pl.ds(SUB + 1, SUB), :], *window)
        for b in range(LANES // SUB):
            at = SUB * b

            def load(shift):
                if at + shift < 0:
                    return edge_w[r, pl.ds(2 * SUB + shift, SUB), :]
                if at + shift + SUB > LANES:
                    return edge_e[r, pl.ds(shift, SUB), :]
                return q[first + r, pl.ds(at + shift, SUB), :]

            flux[r, pl.ds(SUB + at, SUB), :] = through(
                ce[r, pl.ds(at, SUB), :], load(-1), load(0), load(1), load(2)
            )


def lat_divergence(rows, winds):
    north = [through(winds[r], *rows[r : r + 4]) for r in range(len(winds))]
    return [north[r + 1] - north[r] for r in range(len(winds) - 1)]


def sources():
    at, n = lax.axis_index("lat"), lax.axis_size("lat")
    even = lax.rem(at, 2) == 0
    return (even, jnp.logical_not(even), jnp.logical_and(even, at > 0), jnp.logical_and(jnp.logical_not(even), at < n - 1))


def partners(where, ra, rb, span):
    north_a, south_a, south_b, north_b = where
    a, b = ra[span, :], rb[span, :]
    south = jnp.where(south_a, a, jnp.where(south_b, b, 0.0))
    return south, jnp.where(north_a, a, jnp.where(north_b, b, 0.0))


def divergence(q, pair, nrows, b, halo, cn, below, flux):
    at = SUB * b
    here = pl.ds(at, SUB)
    (s0, n0), (s1, n1) = halo(0, at), halo(1, at)
    own = [q[nrows * pair + r, here, :] for r in range(nrows)]
    winds = [below[here, :]] + [cn[r, here, :] for r in range(nrows)]
    north = lat_divergence([s0, s1] + own + [n0, n1], winds)
    div = []
    for r in range(nrows):
        east = flux[r, pl.ds(SUB + at, SUB), :] - flux[r, pl.ds(SUB + at - 1, SUB), :]
        div.append(east + north[r])
    return own, div


def put_side_section(at, nrows, where, ra, rb, corner, side, ntiles, edge_w, edge_e, edge_c, edge_d, out):
    head = sublanes() < SUB // 2

    def shifted(w, e, r, k):
        return jnp.where(head, e[r, pl.ds(SUB + k, SUB), :], w[r, pl.ds(SUB + k, SUB), :])

    def beside(t):
        return side[pl.ds(pl.multiple_of(SUB * t, SUB), SUB), :]

    start = pl.multiple_of(corner + SUB * (at // nrows), SUB)
    south, above = partners(where, ra, rb, pl.ds(start, SUB))
    s0, s1 = south, half_turn(south)
    n0, n1 = above, half_turn(above)
    own = [beside(at + r) for r in range(nrows)]
    last = pl.ds(corner + SUB * (ntiles // nrows), SUB)
    winds = [partners(where, ra, rb, last)[0]]
    winds += [beside(ntiles + nrows + r) for r in range(nrows)]
    north = lat_divergence([s0, s1] + own + [n0, n1], winds)
    for r in range(nrows):
        v = [shifted(edge_w, edge_e, r, k) for k in range(-2, 3)]
        east = through(beside(ntiles + r), *v[1:])
        west = through(shifted(edge_c, edge_d, r, -1), *v[:-1])
        new = own[r] - ((east - west) + north[r])
        out[pl.ds(pl.multiple_of(SUB * (at + r), SUB), SUB), :] = new


def edge_scratch(nrows):
    return [scratch(nrows, 3 * SUB, LANES)] * 4 + [scratch(nrows, LANES + SUB, LANES)]


def first_stage_early(pairs, ntiles, nrows, q, ce, cn, la, lb, ra, rb, section, za, zb, below, side, *edges):
    edge_w, edge_e, edge_c, edge_d, flux = edges
    lat_even, where = is_even("lat"), sources()
    half = LANES // 2
    a = partners(where, ra, rb, pl.ds((2 * pairs + MOVED) * LANES, half))[0]
    turned = pltpu.roll(a, half, 1)
    low = lax.broadcasted_iota(jnp.int32, (half, LANES), 1) < half
    below[pl.ds(0, half), :] = jnp.where(low, a, turned)
    below[pl.ds(half, half), :] = jnp.where(low, turned, a)
    put_side(la, lb, ntiles, side)
    put_corners(lat_even, ntiles, nrows, 2 * pairs * LANES, side, za, zb)
    put_edges(ce, 0, side, side.shape[0] // SUB - 2 * nrows, nrows, edge_c, edge_d)

    def one(p, _):
        def halo(k, shift):
            start = pl.multiple_of((2 * p + k) * LANES, LANES)
            return partners(where, ra, rb, pl.ds(start + shift, SUB))

        put_edges(q, nrows * p, side, nrows * p, nrows, edge_w, edge_e)
        put_fluxes(q, nrows * p, nrows, ce, edge_w, edge_e, edge_c, flux)
        for b in range(LANES // SUB):
            own, div = divergence(q, p, nrows, b, halo, cn, below, flux)
            for r in range(nrows):
                section[nrows * p + r, pl.ds(SUB * b, SUB), :] = own[r] - div[r]
        put_lat_sends(lat_even, section, p, nrows, za, zb)
        return 0

    lax.fori_loop(0, pairs, one, 0)


def first_stage_late(
    pairs, done, nrows, q, ce, cn, side, ra, rb, ra_first, rb_first, below, section, za, zb, *edges
):
    edge_w, edge_e, edge_c, edge_d, flux = edges
    lat_even, where = is_even("lat"), sources()
    put_edges(ce, 0, side, side.shape[0] // SUB - 2 * nrows, nrows, edge_c, edge_d)
    for p in range(pairs):

        def halo(k, shift):
            i = 2 * p + k
            if i < MOVED:
                return partners(where, ra_first, rb_first, pl.ds((2 * done + i) * LANES + shift, SUB))
            return partners(where, ra, rb, pl.ds((i - MOVED) * LANES + shift, SUB))

        put_edges(q, nrows * p, side, nrows * (done + p), nrows, edge_w, edge_e)
        put_fluxes(q, nrows * p, nrows, ce, edge_w, edge_e, edge_c, flux)
        for b in range(LANES // SUB):
            own, div = divergence(q, p, nrows, b, halo, cn, below, flux)
            for r in range(nrows):
                section[nrows * p + r, pl.ds(SUB * b, SUB), :] = own[r] - div[r]
        put_lat_sends(lat_even, section, p, nrows, za, zb)


def put_rows(buffer, pair, rows, nrows):
    levels = LANES // 2
    for r in range(nrows):
        turned = jnp.transpose(jnp.concatenate(rows[r], axis=0))
        for h in range(2):
            buffer[2 * pair + h, pl.ds(r, levels, stride=nrows), :] = turned[levels * h : levels * (h + 1)]


def second_stage_early(
    pairs, later, nrows, q, s, ce, cn, below, ra, rb, side, heating, q_late, s_late,
    out, heat_out, part, buffer, sems, sides, *edges
):
    edge_w, edge_e, edge_c, edge_d, flux = edges
    where = sources()
    heat_copy = pltpu.make_async_copy(heating, heat_out, sems.at[pairs])
    heat_copy.start()
    put_edges(ce, 0, side, side.shape[0] // SUB - 2 * nrows, nrows, edge_c, edge_d)

    ntiles = nrows * (pairs + later)
    for ref, first, n in ((q, 0, pairs), (q_late, pairs, later)):

        def beside(p, _):
            at = nrows * (first + p)
            put_edges(ref, nrows * p, side, at, nrows, edge_w, edge_e)
            put_side_section(
                at, nrows, where, ra, rb, 2 * pairs * LANES, side, ntiles, edge_w, edge_e, edge_c, edge_d, sides
            )
            return 0

        lax.fori_loop(0, n, beside, 0)

    def copy(p):
        return pltpu.make_async_copy(buffer.at[pl.ds(2 * p, 2)], out.at[pl.ds(2 * p, 2)], sems.at[p])

    def one(p, _):
        def halo(k, shift):
            start = pl.multiple_of((2 * p + k) * LANES, LANES)
            return partners(where, ra, rb, pl.ds(start + shift, SUB))

        put_edges(s, nrows * p, sides, nrows * p, nrows, edge_w, edge_e)
        put_fluxes(s, nrows * p, nrows, ce, edge_w, edge_e, edge_c, flux)
        parts = [[] for _ in range(nrows)]
        for b in range(LANES // SUB):
            own, div = divergence(s, p, nrows, b, halo, cn, below, flux)
            for r in range(nrows):
                old = q[nrows * p + r, pl.ds(SUB * b, SUB), :]
                parts[r].append(0.5 * ((old + own[r]) - div[r]))
        put_rows(buffer, p, parts, nrows)

        @pl.when(p == 0)
        def _():
            buffer[0] = buffer[0] + 0.5 * heating[...]

        copy(p).start()
        return 0

    def another(p, _):
        put_edges(s_late, nrows * p, sides, nrows * (pairs + p), nrows, edge_w, edge_e)
        put_fluxes(s_late, nrows * p, nrows, ce, edge_w, edge_e, edge_c, flux)
        for b in range(LANES // SUB):
            here = pl.ds(SUB * b, SUB)
            s0, s1, s2, s3 = own = [s_late[nrows * p + r, here, :] for r in range(nrows)]
            c = [below[here, :]] + [cn[r, here, :] for r in range(nrows)]
            north = [
                c[0] * (7.0 * s0 - s1),
                c[1] * (7.0 * (s0 + s1) - s2),
                through(c[2], *own),
                c[3] * (7.0 * (s2 + s3) - s1),
                c[4] * (7.0 * s3 - s2),
            ]
            for r in range(nrows):
                east = flux[r, pl.ds(SUB * (b + 1), SUB), :] - flux[r, pl.ds(SUB * (b + 1) - 1, SUB), :]
                old = q_late[nrows * p + r, here, :]
                part[nrows * p + r, here, :] = 0.5 * ((old + own[r]) - (east + (north[r + 1] - north[r])))
        return 0

    lax.fori_loop(0, pairs, one, 0)
    lax.fori_loop(0, later, another, 0)
    for p in range(pairs):
        copy(p).wait()
    heat_copy.wait()


def second_stage_late(pairs, done, nrows, part, cn, below, ra, rb, before, out, buffer, sems):
    del before
    where = sources()

    def copy(p):
        return pltpu.make_async_copy(
            buffer.at[pl.ds(2 * p, 2)], out.at[pl.ds(2 * (done + p), 2)], sems.at[p]
        )

    def one(p, _):
        rows = [[] for _ in range(nrows)]
        for b in range(LANES // SUB):
            here = pl.ds(SUB * b, SUB)

            def halo(k):
                start = pl.multiple_of((2 * p + k) * LANES, LANES) + SUB * b
                return partners(where, ra, rb, pl.ds(start, SUB))

            (south_two, north_one), (south_one, north_two) = halo(0), halo(1)
            low = 0.5 * cn[0, here, :] * south_one
            high = 0.5 * cn[2, here, :] * north_one
            bottom = 0.5 * below[here, :] * (7.0 * south_one - south_two)
            top = 0.5 * cn[3, here, :] * (7.0 * north_one - north_two)
            p0, p1, p2, p3 = (part[nrows * p + r, here, :] for r in range(nrows))
            for r, value in enumerate((p0 + (low + bottom), p1 - low, p2 + high, p3 - (top + high))):
                rows[r].append(value)
        put_rows(buffer, p, rows, nrows)
        copy(p).start()
        return 0

    lax.fori_loop(0, pairs, one, 0)
    for p in range(pairs):
        copy(p).wait()


def radiation(
    nat, cosz_in, albedo_in, ext_in, single_in, weight_in, order_in, count_in, after, heat,
    water, depth, save_a, save_b, save_t, save_g, cosz, albedo, ext, single, weight, order, count, sems
):
    del after
    copies = []
    for i, (src, dst) in enumerate(
        (
            (cosz_in, cosz), (albedo_in, albedo), (ext_in, ext), (single_in, single),
            (weight_in, weight), (order_in, order), (count_in, count),
        )
    ):
        copies.append(pltpu.make_async_copy(src, dst, sems.at[i]))
        copies[-1].start()
    nrows, _ = cosz.shape
    levels = nat.shape[1] // nrows
    pairs = ext.shape[0] // 2
    x = nat[1]
    heat[...] = jnp.maximum(x, 0.0) + jnp.log1p(jnp.exp(-jnp.abs(x)))
    total = jnp.zeros((nrows, LANES), jnp.float32)
    depth[0] = jnp.zeros((2 * nrows, LANES), jnp.float32)
    for l in range(levels):
        w = heat[pl.ds(nrows * l, nrows), :]
        total = total + w
        water[l, pl.ds(0, nrows), :] = w
        water[l, pl.ds(nrows, nrows), :] = w
        depth[l + 1, pl.ds(0, nrows), :] = total
        depth[l + 1, pl.ds(nrows, nrows), :] = total
    for copy in copies:
        copy.wait()

    mu = jnp.concatenate([cosz[...], cosz[...]], axis=0)
    floor_albedo = jnp.concatenate([albedo[...], albedo[...]], axis=0)
    first = lax.broadcasted_iota(jnp.int32, (2 * nrows, LANES), 0) < nrows

    def by_band(ref):
        return [jnp.where(first, ref[2 * p], ref[2 * p + 1]) for p in range(pairs)]

    scale = 4.0 / levels
    inv_mu = 1.0 / mu
    ext_of, half_of, weight_of = by_band(ext), by_band(single), by_band(weight)
    beam = [-(e * scale * LOG2E) * inv_mu for e in ext_of]
    diffuse = [-(1.66 * scale * LOG2E) * e for e in ext_of]
    half = [0.5 * s for s in half_of]
    strength = [w * mu for w in weight_of]

    def up(step, carry):
        l = levels - 1 - step
        a_all, b_all, s_all = carry
        w = water[l]
        above = depth[l]
        new_a, new_b, new_s = [], [], []
        for p in range(pairs):
            a, b, s_bot = a_all[p], b_all[p], s_all[p]
            decay = jnp.exp2(diffuse[p] * w)
            s_top = strength[p] * jnp.exp2(beam[p] * above)
            reflect = half[p] - half[p] * decay
            transmit = decay + reflect
            source = half[p] * (s_top - s_bot)
            den = 1.0 - reflect * a
            inv = pl.reciprocal(den, approx=True)
            inv = inv * (2.0 - den * inv)
            t = transmit * inv
            a_here = reflect + transmit * (t * a)
            b_here = t * (a * source + b) + source
            save_t[l, p] = t
            save_g[l, p] = (reflect * b + source) * inv
            save_a[l, p] = 1.0 - a_here
            save_b[l, p] = s_top - b_here
            new_a.append(a_here)
            new_b.append(b_here)
            new_s.append(s_top)
        return tuple(new_a), tuple(new_b), tuple(new_s)

    s_floor = [strength[p] * jnp.exp2(beam[p] * depth[levels]) for p in range(pairs)]
    a_floor = [floor_albedo for _ in range(pairs)]
    b_floor = [floor_albedo * s_floor[p] for p in range(pairs)]
    lax.fori_loop(0, levels, up, (tuple(a_floor), tuple(b_floor), tuple(s_floor)))

    sunlit = []
    column = lax.broadcasted_iota(jnp.int32, (LANES, LANES), 1)
    rank = lax.broadcasted_iota(jnp.int32, (LANES, LANES), 0)
    for r in range(nrows):
        place = jnp.transpose(jnp.broadcast_to(order[r], (LANES, LANES)))
        hit = (place == column) & (rank < count[r])
        sunlit.append(jnp.max(jnp.where(hit, 1.0, 0.0), axis=0, keepdims=True))
    gain = float(levels) * jnp.concatenate(sunlit, axis=0)

    def net_flux(l, d_all):
        net = jnp.zeros((2 * nrows, LANES), jnp.float32)
        for p in range(pairs):
            net = net + (save_b[l, p] + d_all[p] * save_a[l, p])
        return net

    def put(l, absorbed):
        both = absorbed[:nrows] + absorbed[nrows:]
        heat[pl.ds(pl.multiple_of(nrows * l, nrows), nrows), :] = gain * both

    def down(l, carry):
        d_all, net_above = carry
        d_new = tuple(save_t[l - 1, p] * d_all[p] + save_g[l - 1, p] for p in range(pairs))
        net = net_flux(l, d_new)
        put(l - 1, net_above - net)
        return d_new, net

    d_top = tuple(jnp.zeros((2 * nrows, LANES), jnp.float32) for _ in range(pairs))
    d_low, net_low = lax.fori_loop(1, levels, down, (d_top, net_flux(0, d_top)))
    net = jnp.zeros((2 * nrows, LANES), jnp.float32)
    for p in range(pairs):
        d_floor = save_t[levels - 1, p] * d_low[p] + save_g[levels - 1, p]
        net = net + ((s_floor[p] - b_floor[p]) + d_floor * (1.0 - a_floor[p]))
    put(levels - 1, net_low - net)


def in_hbm(x):
    return pltpu.with_memory_space_constraint(x, pltpu.HBM)


def call(kernel, name, out_shape, specs, out_specs, args, scratches, moved=1000, limit=24, **kw):
    return pl.pallas_call(
        kernel,
        out_shape=out_shape,
        in_specs=specs,
        out_specs=out_specs,
        scratch_shapes=scratches,
        compiler_params=pltpu.CompilerParams(vmem_limit_bytes=limit * MIB),
        name=name,
        cost_estimate=pl.CostEstimate(flops=moved, bytes_accessed=moved, transcendentals=0),
        **kw,
    )(*args)


def per_device(
    fields, courant, cos_zenith, albedo, extinction, single_albedo, band_weight, sun_order, sun_count
):
    nfields, levels, nrows, ncols = fields.shape
    flat = fields.reshape(nfields, levels * nrows, ncols)
    wind = courant.reshape(2, levels * nrows, ncols)
    npairs = nfields // 2
    early, late = SPLIT, npairs - SPLIT

    z0 = shape((2 * early + MOVED) * ncols + ncols // 2, LANES)
    tiles0, za, zb, nat, nat_late, nat_wind = call(
        functools.partial(pack_first, early, nrows),
        "pack_first",
        (
            shape(nrows * early, ncols, LANES), z0, z0,
            shape(2 * early, levels * nrows, ncols), shape(2 * late, levels * nrows, ncols),
            shape(2, levels * nrows, ncols),
        ),
        [HBM, HBM],
        (VMEM,) * 6,
        (in_hbm(flat), in_hbm(wind)),
        [pltpu.SemaphoreType.DMA((2 * early + 1 + late,))],
    )
    lat0 = lat_swaps(za, zb)
    ntiles = nrows * npairs
    winds = shape(nrows, ncols, LANES)
    sides = shape(SUB * (ntiles + 2 * nrows), LANES)
    edge = shape(SUB * (ntiles + nrows) // 2, LANES)
    z1 = shape((2 * late - MOVED) * ncols, LANES)
    tiles1, ce, cn, la, lb, za, zb = call(
        functools.partial(pack_middle, late, nrows),
        "pack_middle",
        (shape(nrows * late, ncols, LANES), winds, winds, edge, edge, z1, z1),
        [VMEM] * 3,
        (VMEM,) * 7,
        (nat_late, nat_wind, tiles0),
        [],
    )
    lat1 = lat_swaps(za, zb)
    lon = lon_swaps(la, lb)

    edges = edge_scratch(nrows)
    z0 = shape(2 * early * ncols + SUB * (npairs + 1), LANES)
    section0, za, zb, below, side = call(
        functools.partial(first_stage_early, early, ntiles, nrows),
        "first_stage_early",
        (shape(nrows * early, ncols, LANES), z0, z0, shape(ncols, LANES), sides),
        [VMEM] * 7,
        (VMEM,) * 5,
        (tiles0, ce, cn, *lon, *lat0),
        edges,
        moved=1000_000_000,
    )
    lat2 = lat_swaps(za, zb)
    z1 = shape(2 * late * ncols, LANES)
    section1, za, zb = call(
        functools.partial(first_stage_late, late, early, nrows),
        "first_stage_late",
        (shape(nrows * late, ncols, LANES), z1, z1),
        [VMEM] * 9,
        (VMEM,) * 3,
        (tiles1, ce, cn, side, *lat1, *lat0, below),
        edges,
        moved=12_000_000,
    )
    lat3 = lat_swaps(za, zb)

    pairs = extinction.shape[0] // 2
    store = scratch(levels, pairs, 2 * nrows, ncols)
    heating = call(
        radiation,
        "radiation",
        shape(levels * nrows, ncols),
        [VMEM] + [HBM] * 7 + [VMEM],
        VMEM,
        (
            nat, in_hbm(cos_zenith), in_hbm(albedo), in_hbm(extinction), in_hbm(single_albedo),
            in_hbm(band_weight), in_hbm(sun_order), in_hbm(sun_count.reshape(nrows)), section1,
        ),
        [
            scratch(levels, 2 * nrows, ncols), scratch(levels + 1, 2 * nrows, ncols),
            store, store, store, store,
            scratch(nrows, ncols), scratch(nrows, ncols),
            pltpu.SMEM(extinction.shape, jnp.float32), pltpu.SMEM(extinction.shape, jnp.float32),
            pltpu.SMEM(extinction.shape, jnp.float32), pltpu.VMEM((nrows, 1, ncols), jnp.int32),
            pltpu.SMEM((nrows,), jnp.int32), pltpu.SemaphoreType.DMA((7,)),
        ],
        moved=16_000_000,
    )

    full = shape(nfields, levels * nrows, ncols)
    out, heat_out, part = call(
        functools.partial(second_stage_early, early, late, nrows),
        "second_stage_early",
        (full, shape(levels * nrows, ncols), shape(nrows * late, ncols, LANES)),
        [VMEM] * 11,
        (HBM, HBM, VMEM),
        (tiles0, section0, ce, cn, below, *lat2, side, heating, tiles1, section1),
        [
            scratch(2 * early, levels * nrows, ncols),
            pltpu.SemaphoreType.DMA((early + 1,)),
            scratch(SUB * ntiles, LANES),
            *edges,
        ],
    )
    out = call(
        functools.partial(second_stage_late, late, early, nrows),
        "second_stage_late",
        full,
        [VMEM] * 5 + [HBM],
        HBM,
        (part, cn, below, *lat3, out),
        [scratch(2 * late, levels * nrows, ncols), pltpu.SemaphoreType.DMA((late,))],
        input_output_aliases={5: 0},
    )
    return out.reshape(fields.shape), heat_out.reshape(levels, nrows, ncols)


def solution(mesh):
    in_specs = (
        P(None, None, "lat", "lon"),
        P(None, None, "lat", "lon"),
        P("lat", "lon"),
        P("lat", "lon"),
        P(),
        P(),
        P(),
        P("lat", "lon", None),
        P("lat", "lon"),
    )
    out_specs = (P(None, None, "lat", "lon"), P(None, "lat", "lon"))
    return jax.shard_map(
        per_device, mesh=mesh, in_specs=in_specs, out_specs=out_specs, check_vma=False
    )
```

```python
import functools
import math

import jax
import jax.numpy as jnp
from jax import lax
from jax.experimental import pallas as pl
from jax.experimental.pallas import tpu as pltpu
from jax.sharding import PartitionSpec as P

SPLIT = 2
SUB = 8
LANES = 128
LOG2E = math.log2(math.e)
VMEM = pl.BlockSpec(memory_space=pltpu.VMEM)
HBM = pl.BlockSpec(memory_space=pltpu.HBM)
MIB = 1024 * 1024


def scratch(*dims):
    return pltpu.VMEM(dims, jnp.float32)


def shape(*dims):
    return jax.ShapeDtypeStruct(dims, jnp.float32)


def lon_swaps(first_block, second_block):
    n = lax.axis_size("lon")
    first = [(i, i ^ 1) for i in range(n)]
    second = [(i, (i + 1 if i % 2 else i - 1) % n) for i in range(n)]
    return lax.ppermute(first_block, "lon", first), lax.ppermute(second_block, "lon", second)


def lat_swaps(first_block, second_block):
    nlon, nlat = lax.axis_size("lon"), lax.axis_size("lat")
    second = []
    for i in range(nlon):
        for j in range(nlat):
            k = j + 1 if j % 2 else j - 1
            to = i * nlat + k if 0 <= k < nlat else (i ^ 1) * nlat + j
            second.append((i * nlat + j, to))
    got = lax.ppermute(second_block, ("lon", "lat"), second)
    return lax.ppermute(first_block, "lat", [(j, j ^ 1) for j in range(nlat)]), got


def is_even(axis):
    return lax.rem(lax.axis_index(axis), 2) == 0


def sublanes():
    return lax.broadcasted_iota(jnp.int32, (SUB, LANES), 0)


def lanes():
    return lax.broadcasted_iota(jnp.int32, (SUB, LANES), 1)


def half_turn(block):
    return pltpu.roll(block, SUB // 2, 0)


def native(ref, index, r, nrows):
    levels = ref.shape[1] // nrows
    return ref[index, pl.ds(r, levels, stride=nrows), :]


def tile_of(low, high):
    return jnp.transpose(jnp.concatenate([low, high], axis=0))


def put_lat_sends(even, tiles, pair, nrows, za, zb):
    north = jnp.where(even, 2, 0)
    for k in range(2):
        span = pl.ds(pl.multiple_of((2 * pair + k) * LANES, LANES), LANES)
        za[span, :] = tiles[nrows * pair + north + k]
        zb[span, :] = tiles[nrows * pair + (2 - north) + k]


def take_sides(tile):
    head = sublanes() < SUB // 2
    return jnp.where(head, tile[pl.ds(0, SUB), :], tile[pl.ds(LANES - SUB, SUB), :])


def pack_first(pairs, nrows, fields, courant, tiles, za, zb, nat, nat_late, nat_wind, sems):
    n = 2 * pairs
    first = pltpu.make_async_copy(fields.at[pl.ds(0, n)], nat, sems.at[0])
    wind = pltpu.make_async_copy(courant, nat_wind, sems.at[1])
    late = pltpu.make_async_copy(fields.at[pl.ds(n, nat_late.shape[0])], nat_late, sems.at[2])
    for copy in (first, wind, late):
        copy.start()
    first.wait()
    wind.wait()
    half = LANES // 2
    lane = lax.broadcasted_iota(jnp.int32, (half, LANES), 1)

    def body(up, down):
        for p in range(pairs):
            for r in range(nrows):
                tile = tile_of(native(nat, 2 * p, r, nrows), native(nat, 2 * p + 1, r, nrows))
                tiles[nrows * p + r] = tile
                (up if r >= 2 else down)[pl.ds((2 * p + r % 2) * LANES, LANES), :] = tile
        top = native(nat_wind, 1, nrows - 1, nrows) * (1.0 / 12.0)
        top = tile_of(top, top)
        top = jnp.where(lane < half, top[:half], top[half:])
        for ref in (up, down):
            ref[pl.ds(2 * pairs * LANES, half), :] = top

    even = is_even("lat")
    pl.when(even)(lambda: body(za, zb))
    pl.when(jnp.logical_not(even))(lambda: body(zb, za))
    late.wait()


def pack_middle(pairs, nrows, nat, nat_wind, tiles_first, tiles, ce, cn, la, lb, za, zb):
    up = jnp.where(is_even("lat"), 2, 0)
    for p in range(pairs):
        for r in range(nrows):
            tiles[nrows * p + r] = tile_of(native(nat, 2 * p, r, nrows), native(nat, 2 * p + 1, r, nrows))
    for r in range(nrows):
        east = native(nat_wind, 0, r, nrows) * (1.0 / 12.0)
        north = native(nat_wind, 1, r, nrows) * (1.0 / 12.0)
        ce[r] = tile_of(east, east)
        cn[r] = tile_of(north, north)
    for i in range(2 * pairs):
        p, k = divmod(i, 2)
        span = pl.ds(i * LANES, LANES)
        za[span, :] = tiles[nrows * p + up + k]
        zb[span, :] = tiles[nrows * p + (2 - up) + k]
    even = is_even("lon")
    head, low = sublanes() < SUB // 2, lanes() < LANES // 2
    blocks = [take_sides(ref.at[t]) for ref in (tiles_first, tiles) for t in range(ref.shape[0])]
    blocks += [jnp.where(low, take_sides(ce.at[r]), take_sides(cn.at[r])) for r in range(nrows)]
    for i in range(0, len(blocks), 2):
        one, two = blocks[i : i + 2]
        east = jnp.where(head, half_turn(one), two)
        west = jnp.where(head, one, half_turn(two))
        span = pl.ds(SUB * (i // 2), SUB)
        la[span, :] = jnp.where(even, east, west)
        lb[span, :] = jnp.where(even, west, east)


def put_side(la, lb, ntiles, side):
    lon_even = is_even("lon")
    head, low = sublanes() < SUB // 2, lanes() < LANES // 2
    blocks = []
    for i in range(la.shape[0] // SUB):
        span = pl.ds(SUB * i, SUB)
        a, b = la[span, :], lb[span, :]
        east, west = jnp.where(lon_even, a, b), jnp.where(lon_even, b, a)
        blocks += [jnp.where(head, east, half_turn(west)), jnp.where(head, half_turn(east), west)]
    winds = blocks[ntiles:]
    turned = [pltpu.roll(wind, LANES // 2, 1) for wind in winds]
    blocks[ntiles:] = [jnp.where(low, x, y) for x, y in zip(winds, turned)]
    blocks += [jnp.where(low, y, x) for x, y in zip(winds, turned)]
    for t, value in enumerate(blocks):
        side[pl.ds(SUB * t, SUB), :] = value


def put_corners(lat_even, ntiles, nrows, at, side, za, zb):
    row = sublanes()
    outer = (row < 2) | (row >= SUB - 2)
    north = jnp.where(lat_even, 2, 0)

    def corner(p, first):
        start = pl.multiple_of(SUB * (nrows * p + first), SUB)
        one, two = side[pl.ds(start, SUB), :], side[pl.ds(start + SUB, SUB), :]
        return jnp.where(outer, one, half_turn(two))

    npairs = ntiles // nrows
    for p in range(npairs):
        to = pl.ds(at + SUB * p, SUB)
        za[to, :] = corner(p, north)
        zb[to, :] = corner(p, 2 - north)
    to = pl.ds(at + SUB * npairs, SUB)
    top = side[pl.ds(SUB * (ntiles + 2 * nrows - 1), SUB), :]
    za[to, :] = top
    zb[to, :] = top


def put_edges(q, first, side, at, nrows, edge_w, edge_e):
    for r in range(nrows):
        beside = side[pl.ds(pl.multiple_of(SUB * (at + r), SUB), SUB), :]
        edge_w[r, pl.ds(SUB, SUB), :] = beside
        edge_w[r, pl.ds(2 * SUB, SUB), :] = q[first + r, pl.ds(0, SUB), :]
        edge_e[r, pl.ds(0, SUB), :] = q[first + r, pl.ds(LANES - SUB, SUB), :]
        edge_e[r, pl.ds(SUB, SUB), :] = beside


def through(c, before, left, right, after):
    return c * (7.0 * (left + right) - (before + after))


def put_fluxes(q, first, nrows, ce, edge_w, edge_e, edge_c, flux):
    for r in range(nrows):
        window = [edge_w[r, pl.ds(SUB + k, SUB), :] for k in range(4)]
        flux[r, pl.ds(1, SUB), :] = through(edge_c[r, pl.ds(SUB + 1, SUB), :], *window)
        for b in range(LANES // SUB):
            at = SUB * b

            def load(shift):
                if at + shift < 0:
                    return edge_w[r, pl.ds(2 * SUB + shift, SUB), :]
                if at + shift + SUB > LANES:
                    return edge_e[r, pl.ds(shift, SUB), :]
                return q[first + r, pl.ds(at + shift, SUB), :]

            flux[r, pl.ds(SUB + at, SUB), :] = through(
                ce[r, pl.ds(at, SUB), :], load(-1), load(0), load(1), load(2)
            )


def lat_divergence(rows, winds):
    north = [through(winds[r], *rows[r : r + 4]) for r in range(len(winds))]
    return [north[r + 1] - north[r] for r in range(len(winds) - 1)]


def sources():
    at, n = lax.axis_index("lat"), lax.axis_size("lat")
    even = lax.rem(at, 2) == 0
    return (even, jnp.logical_not(even), jnp.logical_and(even, at > 0), jnp.logical_and(jnp.logical_not(even), at < n - 1))


def partners(where, ra, rb, span):
    north_a, south_a, south_b, north_b = where
    a, b = ra[span, :], rb[span, :]
    south = jnp.where(south_a, a, jnp.where(south_b, b, 0.0))
    return south, jnp.where(north_a, a, jnp.where(north_b, b, 0.0))


def divergence(q, pair, nrows, b, halo, cn, below, flux):
    at = SUB * b
    here = pl.ds(at, SUB)
    (s0, n0), (s1, n1) = halo(0, at), halo(1, at)
    own = [q[nrows * pair + r, here, :] for r in range(nrows)]
    winds = [below[here, :]] + [cn[r, here, :] for r in range(nrows)]
    north = lat_divergence([s0, s1] + own + [n0, n1], winds)
    div = []
    for r in range(nrows):
        east = flux[r, pl.ds(SUB + at, SUB), :] - flux[r, pl.ds(SUB + at - 1, SUB), :]
        div.append(east + north[r])
    return own, div


def put_side_section(at, nrows, where, ra, rb, corner, side, ntiles, edge_w, edge_e, edge_c, edge_d, out):
    head = sublanes() < SUB // 2

    def shifted(w, e, r, k):
        return jnp.where(head, e[r, pl.ds(SUB + k, SUB), :], w[r, pl.ds(SUB + k, SUB), :])

    def beside(t):
        return side[pl.ds(pl.multiple_of(SUB * t, SUB), SUB), :]

    start = pl.multiple_of(corner + SUB * (at // nrows), SUB)
    south, above = partners(where, ra, rb, pl.ds(start, SUB))
    s0, s1 = south, half_turn(south)
    n0, n1 = above, half_turn(above)
    own = [beside(at + r) for r in range(nrows)]
    last = pl.ds(corner + SUB * (ntiles // nrows), SUB)
    winds = [partners(where, ra, rb, last)[0]]
    winds += [beside(ntiles + nrows + r) for r in range(nrows)]
    north = lat_divergence([s0, s1] + own + [n0, n1], winds)
    for r in range(nrows):
        v = [shifted(edge_w, edge_e, r, k) for k in range(-2, 3)]
        east = through(beside(ntiles + r), *v[1:])
        west = through(shifted(edge_c, edge_d, r, -1), *v[:-1])
        new = own[r] - ((east - west) + north[r])
        out[pl.ds(pl.multiple_of(SUB * (at + r), SUB), SUB), :] = new


def edge_scratch(nrows):
    return [scratch(nrows, 3 * SUB, LANES)] * 4 + [scratch(nrows, LANES + SUB, LANES)]


def first_stage_early(pairs, ntiles, nrows, q, ce, cn, la, lb, ra, rb, section, za, zb, below, side, *edges):
    edge_w, edge_e, edge_c, edge_d, flux = edges
    lat_even, where = is_even("lat"), sources()
    half = LANES // 2
    a = partners(where, ra, rb, pl.ds(2 * pairs * LANES, half))[0]
    turned = pltpu.roll(a, half, 1)
    low = lax.broadcasted_iota(jnp.int32, (half, LANES), 1) < half
    below[pl.ds(0, half), :] = jnp.where(low, a, turned)
    below[pl.ds(half, half), :] = jnp.where(low, turned, a)
    put_side(la, lb, ntiles, side)
    put_corners(lat_even, ntiles, nrows, 2 * pairs * LANES, side, za, zb)
    put_edges(ce, 0, side, side.shape[0] // SUB - 2 * nrows, nrows, edge_c, edge_d)

    def one(p, _):
        def halo(k, shift):
            start = pl.multiple_of((2 * p + k) * LANES, LANES)
            return partners(where, ra, rb, pl.ds(start + shift, SUB))

        put_edges(q, nrows * p, side, nrows * p, nrows, edge_w, edge_e)
        put_fluxes(q, nrows * p, nrows, ce, edge_w, edge_e, edge_c, flux)
        for b in range(LANES // SUB):
            own, div = divergence(q, p, nrows, b, halo, cn, below, flux)
            for r in range(nrows):
                section[nrows * p + r, pl.ds(SUB * b, SUB), :] = own[r] - div[r]
        put_lat_sends(lat_even, section, p, nrows, za, zb)
        return 0

    lax.fori_loop(0, pairs, one, 0)


def first_stage_late(
    pairs, done, nrows, q, ce, cn, side, ra, rb, below, section, za, zb, *edges
):
    edge_w, edge_e, edge_c, edge_d, flux = edges
    lat_even, where = is_even("lat"), sources()
    put_edges(ce, 0, side, side.shape[0] // SUB - 2 * nrows, nrows, edge_c, edge_d)
    for p in range(pairs):

        def halo(k, shift):
            return partners(where, ra, rb, pl.ds((2 * p + k) * LANES + shift, SUB))

        put_edges(q, nrows * p, side, nrows * (done + p), nrows, edge_w, edge_e)
        put_fluxes(q, nrows * p, nrows, ce, edge_w, edge_e, edge_c, flux)
        for b in range(LANES // SUB):
            own, div = divergence(q, p, nrows, b, halo, cn, below, flux)
            for r in range(nrows):
                section[nrows * p + r, pl.ds(SUB * b, SUB), :] = own[r] - div[r]
        put_lat_sends(lat_even, section, p, nrows, za, zb)


def put_rows(buffer, pair, rows, nrows):
    levels = LANES // 2
    for r in range(nrows):
        turned = jnp.transpose(jnp.concatenate(rows[r], axis=0))
        for h in range(2):
            buffer[2 * pair + h, pl.ds(r, levels, stride=nrows), :] = turned[levels * h : levels * (h + 1)]


def second_stage_early(
    pairs, later, nrows, q, s, ce, cn, below, ra, rb, side, heating, q_late, s_late,
    out, heat_out, part, buffer, sems, sides, *edges
):
    edge_w, edge_e, edge_c, edge_d, flux = edges
    where = sources()
    heat_copy = pltpu.make_async_copy(heating, heat_out, sems.at[pairs])
    heat_copy.start()
    put_edges(ce, 0, side, side.shape[0] // SUB - 2 * nrows, nrows, edge_c, edge_d)

    ntiles = nrows * (pairs + later)
    for ref, first, n in ((q, 0, pairs), (q_late, pairs, later)):

        def beside(p, _):
            at = nrows * (first + p)
            put_edges(ref, nrows * p, side, at, nrows, edge_w, edge_e)
            put_side_section(
                at, nrows, where, ra, rb, 2 * pairs * LANES, side, ntiles, edge_w, edge_e, edge_c, edge_d, sides
            )
            return 0

        lax.fori_loop(0, n, beside, 0)

    def copy(p):
        return pltpu.make_async_copy(buffer.at[pl.ds(2 * p, 2)], out.at[pl.ds(2 * p, 2)], sems.at[p])

    def one(p, _):
        def halo(k, shift):
            start = pl.multiple_of((2 * p + k) * LANES, LANES)
            return partners(where, ra, rb, pl.ds(start + shift, SUB))

        put_edges(s, nrows * p, sides, nrows * p, nrows, edge_w, edge_e)
        put_fluxes(s, nrows * p, nrows, ce, edge_w, edge_e, edge_c, flux)
        parts = [[] for _ in range(nrows)]
        for b in range(LANES // SUB):
            own, div = divergence(s, p, nrows, b, halo, cn, below, flux)
            for r in range(nrows):
                old = q[nrows * p + r, pl.ds(SUB * b, SUB), :]
                parts[r].append(0.5 * ((old + own[r]) - div[r]))
        put_rows(buffer, p, parts, nrows)

        @pl.when(p == 0)
        def _():
            buffer[0] = buffer[0] + 0.5 * heating[...]

        copy(p).start()
        return 0

    def another(p, _):
        put_edges(s_late, nrows * p, sides, nrows * (pairs + p), nrows, edge_w, edge_e)
        put_fluxes(s_late, nrows * p, nrows, ce, edge_w, edge_e, edge_c, flux)
        for b in range(LANES // SUB):
            here = pl.ds(SUB * b, SUB)
            s0, s1, s2, s3 = own = [s_late[nrows * p + r, here, :] for r in range(nrows)]
            c = [below[here, :]] + [cn[r, here, :] for r in range(nrows)]
            north = [
                c[0] * (7.0 * s0 - s1),
                c[1] * (7.0 * (s0 + s1) - s2),
                through(c[2], *own),
                c[3] * (7.0 * (s2 + s3) - s1),
                c[4] * (7.0 * s3 - s2),
            ]
            for r in range(nrows):
                east = flux[r, pl.ds(SUB * (b + 1), SUB), :] - flux[r, pl.ds(SUB * (b + 1) - 1, SUB), :]
                old = q_late[nrows * p + r, here, :]
                part[nrows * p + r, here, :] = 0.5 * ((old + own[r]) - (east + (north[r + 1] - north[r])))
        return 0

    lax.fori_loop(0, pairs, one, 0)
    lax.fori_loop(0, later, another, 0)
    for p in range(pairs):
        copy(p).wait()
    heat_copy.wait()


def second_stage_late(pairs, done, nrows, part, cn, below, ra, rb, before, out, buffer, sems):
    del before
    where = sources()

    def copy(p):
        return pltpu.make_async_copy(
            buffer.at[pl.ds(2 * p, 2)], out.at[pl.ds(2 * (done + p), 2)], sems.at[p]
        )

    def one(p):
        rows = [[] for _ in range(nrows)]
        for b in range(LANES // SUB):
            here = pl.ds(SUB * b, SUB)

            def halo(k):
                start = (2 * p + k) * LANES + SUB * b
                return partners(where, ra, rb, pl.ds(start, SUB))

            (south_two, north_one), (south_one, north_two) = halo(0), halo(1)
            low = 0.5 * cn[0, here, :] * south_one
            high = 0.5 * cn[2, here, :] * north_one
            bottom = 0.5 * below[here, :] * (7.0 * south_one - south_two)
            top = 0.5 * cn[3, here, :] * (7.0 * north_one - north_two)
            p0, p1, p2, p3 = (part[nrows * p + r, here, :] for r in range(nrows))
            for r, value in enumerate((p0 + (low + bottom), p1 - low, p2 + high, p3 - (top + high))):
                rows[r].append(value)
        put_rows(buffer, p, rows, nrows)
        copy(p).start()

    for p in range(pairs):
        one(p)
    for p in range(pairs):
        copy(p).wait()


def radiation(
    nat, cosz_in, albedo_in, ext_in, single_in, weight_in, order_in, count_in, after, heat,
    water, depth, save_a, save_b, save_t, save_g, cosz, albedo, ext, single, weight, order, count, sems
):
    del after
    copies = []
    for i, (src, dst) in enumerate(
        (
            (cosz_in, cosz), (albedo_in, albedo), (ext_in, ext), (single_in, single),
            (weight_in, weight), (order_in, order), (count_in, count),
        )
    ):
        copies.append(pltpu.make_async_copy(src, dst, sems.at[i]))
        copies[-1].start()
    nrows, _ = cosz.shape
    levels = nat.shape[1] // nrows
    pairs = ext.shape[0] // 2
    x = nat[1]
    heat[...] = jnp.maximum(x, 0.0) + jnp.log1p(jnp.exp(-jnp.abs(x)))
    total = jnp.zeros((nrows, LANES), jnp.float32)
    depth[0] = jnp.zeros((2 * nrows, LANES), jnp.float32)
    for l in range(levels):
        w = heat[pl.ds(nrows * l, nrows), :]
        total = total + w
        water[l, pl.ds(0, nrows), :] = w
        water[l, pl.ds(nrows, nrows), :] = w
        depth[l + 1, pl.ds(0, nrows), :] = total
        depth[l + 1, pl.ds(nrows, nrows), :] = total
    for copy in copies:
        copy.wait()

    mu = jnp.concatenate([cosz[...], cosz[...]], axis=0)
    floor_albedo = jnp.concatenate([albedo[...], albedo[...]], axis=0)
    first = lax.broadcasted_iota(jnp.int32, (2 * nrows, LANES), 0) < nrows

    def by_band(ref):
        return [jnp.where(first, ref[2 * p], ref[2 * p + 1]) for p in range(pairs)]

    scale = 4.0 / levels
    inv_mu = 1.0 / mu
    ext_of, half_of, weight_of = by_band(ext), by_band(single), by_band(weight)
    beam = [-(e * scale * LOG2E) * inv_mu for e in ext_of]
    diffuse = [-(1.66 * scale * LOG2E) * e for e in ext_of]
    half = [0.5 * s for s in half_of]
    strength = [w * mu for w in weight_of]

    def up(step, carry):
        l = levels - 1 - step
        a_all, b_all, s_all = carry
        w = water[l]
        above = depth[l]
        new_a, new_b, new_s = [], [], []
        for p in range(pairs):
            a, b, s_bot = a_all[p], b_all[p], s_all[p]
            decay = jnp.exp2(diffuse[p] * w)
            s_top = strength[p] * jnp.exp2(beam[p] * above)
            reflect = half[p] - half[p] * decay
            transmit = decay + reflect
            source = half[p] * (s_top - s_bot)
            den = 1.0 - reflect * a
            inv = pl.reciprocal(den, approx=True)
            inv = inv * (2.0 - den * inv)
            t = transmit * inv
            a_here = reflect + transmit * (t * a)
            b_here = t * (a * source + b) + source
            save_t[l, p] = t
            save_g[l, p] = (reflect * b + source) * inv
            save_a[l, p] = 1.0 - a_here
            save_b[l, p] = s_top - b_here
            new_a.append(a_here)
            new_b.append(b_here)
            new_s.append(s_top)
        return tuple(new_a), tuple(new_b), tuple(new_s)

    s_floor = [strength[p] * jnp.exp2(beam[p] * depth[levels]) for p in range(pairs)]
    a_floor = [floor_albedo for _ in range(pairs)]
    b_floor = [floor_albedo * s_floor[p] for p in range(pairs)]
    lax.fori_loop(0, levels, up, (tuple(a_floor), tuple(b_floor), tuple(s_floor)))

    sunlit = []
    column = lax.broadcasted_iota(jnp.int32, (LANES, LANES), 1)
    rank = lax.broadcasted_iota(jnp.int32, (LANES, LANES), 0)
    for r in range(nrows):
        place = jnp.transpose(jnp.broadcast_to(order[r], (LANES, LANES)))
        hit = (place == column) & (rank < count[r])
        sunlit.append(jnp.max(jnp.where(hit, 1.0, 0.0), axis=0, keepdims=True))
    gain = float(levels) * jnp.concatenate(sunlit, axis=0)

    def net_flux(l, d_all):
        net = jnp.zeros((2 * nrows, LANES), jnp.float32)
        for p in range(pairs):
            net = net + (save_b[l, p] + d_all[p] * save_a[l, p])
        return net

    def put(l, absorbed):
        both = absorbed[:nrows] + absorbed[nrows:]
        heat[pl.ds(pl.multiple_of(nrows * l, nrows), nrows), :] = gain * both

    def down(l, carry):
        d_all, net_above = carry
        d_new = tuple(save_t[l - 1, p] * d_all[p] + save_g[l - 1, p] for p in range(pairs))
        net = net_flux(l, d_new)
        put(l - 1, net_above - net)
        return d_new, net

    d_top = tuple(jnp.zeros((2 * nrows, LANES), jnp.float32) for _ in range(pairs))
    d_low, net_low = lax.fori_loop(1, levels, down, (d_top, net_flux(0, d_top)))
    net = jnp.zeros((2 * nrows, LANES), jnp.float32)
    for p in range(pairs):
        d_floor = save_t[levels - 1, p] * d_low[p] + save_g[levels - 1, p]
        net = net + ((s_floor[p] - b_floor[p]) + d_floor * (1.0 - a_floor[p]))
    put(levels - 1, net_low - net)


def in_hbm(x):
    return pltpu.with_memory_space_constraint(x, pltpu.HBM)


def call(kernel, name, out_shape, specs, out_specs, args, scratches, moved=1000, limit=24, **kw):
    return pl.pallas_call(
        kernel,
        out_shape=out_shape,
        in_specs=specs,
        out_specs=out_specs,
        scratch_shapes=scratches,
        compiler_params=pltpu.CompilerParams(vmem_limit_bytes=limit * MIB),
        name=name,
        cost_estimate=pl.CostEstimate(flops=moved, bytes_accessed=moved, transcendentals=0),
        **kw,
    )(*args)


def per_device(
    fields, courant, cos_zenith, albedo, extinction, single_albedo, band_weight, sun_order, sun_count
):
    nfields, levels, nrows, ncols = fields.shape
    flat = fields.reshape(nfields, levels * nrows, ncols)
    wind = courant.reshape(2, levels * nrows, ncols)
    npairs = nfields // 2
    early, late = SPLIT, npairs - SPLIT

    z0 = shape(2 * early * ncols + ncols // 2, LANES)
    tiles0, za, zb, nat, nat_late, nat_wind = call(
        functools.partial(pack_first, early, nrows),
        "pack_first",
        (
            shape(nrows * early, ncols, LANES), z0, z0,
            shape(2 * early, levels * nrows, ncols), shape(2 * late, levels * nrows, ncols),
            shape(2, levels * nrows, ncols),
        ),
        [HBM, HBM],
        (VMEM,) * 6,
        (in_hbm(flat), in_hbm(wind)),
        [pltpu.SemaphoreType.DMA((3,))],
    )
    lat0 = lat_swaps(za, zb)
    ntiles = nrows * npairs
    winds = shape(nrows, ncols, LANES)
    sides = shape(SUB * (ntiles + 2 * nrows), LANES)
    edge = shape(SUB * (ntiles + nrows) // 2, LANES)
    z1 = shape(2 * late * ncols, LANES)
    tiles1, ce, cn, la, lb, za, zb = call(
        functools.partial(pack_middle, late, nrows),
        "pack_middle",
        (shape(nrows * late, ncols, LANES), winds, winds, edge, edge, z1, z1),
        [VMEM] * 3,
        (VMEM,) * 7,
        (nat_late, nat_wind, tiles0),
        [],
    )
    lat1 = lat_swaps(za, zb)
    lon = lon_swaps(la, lb)

    edges = edge_scratch(nrows)
    z0 = shape(2 * early * ncols + SUB * (npairs + 1), LANES)
    section0, za, zb, below, side = call(
        functools.partial(first_stage_early, early, ntiles, nrows),
        "first_stage_early",
        (shape(nrows * early, ncols, LANES), z0, z0, shape(ncols, LANES), sides),
        [VMEM] * 7,
        (VMEM,) * 5,
        (tiles0, ce, cn, *lon, *lat0),
        edges,
        moved=1000_000_000,
    )
    lat2 = lat_swaps(za, zb)
    z1 = shape(2 * late * ncols, LANES)
    section1, za, zb = call(
        functools.partial(first_stage_late, late, early, nrows),
        "first_stage_late",
        (shape(nrows * late, ncols, LANES), z1, z1),
        [VMEM] * 7,
        (VMEM,) * 3,
        (tiles1, ce, cn, side, *lat1, below),
        edges,
        moved=12_000_000,
    )
    lat3 = lat_swaps(za, zb)

    pairs = extinction.shape[0] // 2
    store = scratch(levels, pairs, 2 * nrows, ncols)
    heating = call(
        radiation,
        "radiation",
        shape(levels * nrows, ncols),
        [VMEM] + [HBM] * 7 + [VMEM],
        VMEM,
        (
            nat, in_hbm(cos_zenith), in_hbm(albedo), in_hbm(extinction), in_hbm(single_albedo),
            in_hbm(band_weight), in_hbm(sun_order), in_hbm(sun_count.reshape(nrows)), section1,
        ),
        [
            scratch(levels, 2 * nrows, ncols), scratch(levels + 1, 2 * nrows, ncols),
            store, store, store, store,
            scratch(nrows, ncols), scratch(nrows, ncols),
            pltpu.SMEM(extinction.shape, jnp.float32), pltpu.SMEM(extinction.shape, jnp.float32),
            pltpu.SMEM(extinction.shape, jnp.float32), pltpu.VMEM((nrows, 1, ncols), jnp.int32),
            pltpu.SMEM((nrows,), jnp.int32), pltpu.SemaphoreType.DMA((7,)),
        ],
        moved=16_000_000,
    )

    full = shape(nfields, levels * nrows, ncols)
    out, heat_out, part = call(
        functools.partial(second_stage_early, early, late, nrows),
        "second_stage_early",
        (full, shape(levels * nrows, ncols), shape(nrows * late, ncols, LANES)),
        [VMEM] * 11,
        (HBM, HBM, VMEM),
        (tiles0, section0, ce, cn, below, *lat2, side, heating, tiles1, section1),
        [
            scratch(2 * early, levels * nrows, ncols),
            pltpu.SemaphoreType.DMA((early + 1,)),
            scratch(SUB * ntiles, LANES),
            *edges,
        ],
    )
    out = call(
        functools.partial(second_stage_late, late, early, nrows),
        "second_stage_late",
        full,
        [VMEM] * 5 + [HBM],
        HBM,
        (part, cn, below, *lat3, out),
        [scratch(2 * late, levels * nrows, ncols), pltpu.SemaphoreType.DMA((late,))],
        input_output_aliases={5: 0},
    )
    return out.reshape(fields.shape), heat_out.reshape(levels, nrows, ncols)


def solution(mesh):
    in_specs = (
        P(None, None, "lat", "lon"),
        P(None, None, "lat", "lon"),
        P("lat", "lon"),
        P("lat", "lon"),
        P(),
        P(),
        P(),
        P("lat", "lon", None),
        P("lat", "lon"),
    )
    out_specs = (P(None, None, "lat", "lon"), P(None, "lat", "lon"))
    return jax.shard_map(
        per_device, mesh=mesh, in_specs=in_specs, out_specs=out_specs, check_vma=False
    )
```

```python
import functools
import math

import jax
import jax.numpy as jnp
from jax import lax
from jax.experimental import pallas as pl
from jax.experimental.pallas import tpu as pltpu
from jax.sharding import PartitionSpec as P

SPLIT = 2
SUB = 8
LANES = 128
LOG2E = math.log2(math.e)
VMEM = pl.BlockSpec(memory_space=pltpu.VMEM)
HBM = pl.BlockSpec(memory_space=pltpu.HBM)
MIB = 1024 * 1024


def scratch(*dims):
    return pltpu.VMEM(dims, jnp.float32)


def shape(*dims):
    return jax.ShapeDtypeStruct(dims, jnp.float32)


def lon_swaps(first_block, second_block):
    n = lax.axis_size("lon")
    first = [(i, i ^ 1) for i in range(n)]
    second = [(i, (i + 1 if i % 2 else i - 1) % n) for i in range(n)]
    return lax.ppermute(first_block, "lon", first), lax.ppermute(second_block, "lon", second)


def lat_swaps(first_block, second_block):
    nlon, nlat = lax.axis_size("lon"), lax.axis_size("lat")
    second = []
    for i in range(nlon):
        for j in range(nlat):
            k = j + 1 if j % 2 else j - 1
            to = i * nlat + k if 0 <= k < nlat else (i ^ 1) * nlat + j
            second.append((i * nlat + j, to))
    got = lax.ppermute(second_block, ("lon", "lat"), second)
    return lax.ppermute(first_block, "lat", [(j, j ^ 1) for j in range(nlat)]), got


def is_even(axis):
    return lax.rem(lax.axis_index(axis), 2) == 0


def sublanes():
    return lax.broadcasted_iota(jnp.int32, (SUB, LANES), 0)


def lanes():
    return lax.broadcasted_iota(jnp.int32, (SUB, LANES), 1)


def half_turn(block):
    return pltpu.roll(block, SUB // 2, 0)


def native(ref, index, r, nrows):
    levels = ref.shape[1] // nrows
    return ref[index, pl.ds(r, levels, stride=nrows), :]


def tile_of(low, high):
    return jnp.transpose(jnp.concatenate([low, high], axis=0))


def put_lat_sends(even, tiles, pair, nrows, za, zb):
    north = jnp.where(even, 2, 0)
    for k in range(2):
        span = pl.ds(pl.multiple_of((2 * pair + k) * LANES, LANES), LANES)
        za[span, :] = tiles[nrows * pair + north + k]
        zb[span, :] = tiles[nrows * pair + (2 - north) + k]


def take_sides(tile):
    head = sublanes() < SUB // 2
    return jnp.where(head, tile[pl.ds(0, SUB), :], tile[pl.ds(LANES - SUB, SUB), :])


def pack_first(pairs, nrows, fields, courant, tiles, za, zb, nat, nat_late, nat_wind, sems):
    n = 2 * pairs
    first = pltpu.make_async_copy(fields.at[pl.ds(0, n)], nat, sems.at[0])
    wind = pltpu.make_async_copy(courant, nat_wind, sems.at[1])
    late = pltpu.make_async_copy(fields.at[pl.ds(n, nat_late.shape[0])], nat_late, sems.at[2])
    for copy in (first, wind, late):
        copy.start()
    first.wait()
    wind.wait()
    half = LANES // 2
    lane = lax.broadcasted_iota(jnp.int32, (half, LANES), 1)

    def body(up, down):
        for p in range(pairs):
            for r in range(nrows):
                tile = tile_of(native(nat, 2 * p, r, nrows), native(nat, 2 * p + 1, r, nrows))
                tiles[nrows * p + r] = tile
                (up if r >= 2 else down)[pl.ds((2 * p + r % 2) * LANES, LANES), :] = tile
        top = native(nat_wind, 1, nrows - 1, nrows) * (1.0 / 12.0)
        top = tile_of(top, top)
        top = jnp.where(lane < half, top[:half], top[half:])
        for ref in (up, down):
            ref[pl.ds(2 * pairs * LANES, half), :] = top

    even = is_even("lat")
    pl.when(even)(lambda: body(za, zb))
    pl.when(jnp.logical_not(even))(lambda: body(zb, za))
    late.wait()


def pack_middle(pairs, nrows, nat, nat_wind, tiles_first, tiles, ce, cn, la, lb, za, zb):
    up = jnp.where(is_even("lat"), 2, 0)
    for p in range(pairs):
        for r in range(nrows):
            tiles[nrows * p + r] = tile_of(native(nat, 2 * p, r, nrows), native(nat, 2 * p + 1, r, nrows))
    for r in range(nrows):
        east = native(nat_wind, 0, r, nrows) * (1.0 / 12.0)
        north = native(nat_wind, 1, r, nrows) * (1.0 / 12.0)
        ce[r] = tile_of(east, east)
        cn[r] = tile_of(north, north)
    for i in range(2 * pairs):
        p, k = divmod(i, 2)
        span = pl.ds(i * LANES, LANES)
        za[span, :] = tiles[nrows * p + up + k]
        zb[span, :] = tiles[nrows * p + (2 - up) + k]
    even = is_even("lon")
    head, low = sublanes() < SUB // 2, lanes() < LANES // 2
    blocks = [take_sides(ref.at[t]) for ref in (tiles_first, tiles) for t in range(ref.shape[0])]
    blocks += [jnp.where(low, take_sides(ce.at[r]), take_sides(cn.at[r])) for r in range(nrows)]
    for i in range(0, len(blocks), 2):
        one, two = blocks[i : i + 2]
        east = jnp.where(head, half_turn(one), two)
        west = jnp.where(head, one, half_turn(two))
        span = pl.ds(SUB * (i // 2), SUB)
        la[span, :] = jnp.where(even, east, west)
        lb[span, :] = jnp.where(even, west, east)


def put_side(la, lb, ntiles, side):
    lon_even = is_even("lon")
    head, low = sublanes() < SUB // 2, lanes() < LANES // 2
    blocks = []
    for i in range(la.shape[0] // SUB):
        span = pl.ds(SUB * i, SUB)
        a, b = la[span, :], lb[span, :]
        east, west = jnp.where(lon_even, a, b), jnp.where(lon_even, b, a)
        blocks += [jnp.where(head, east, half_turn(west)), jnp.where(head, half_turn(east), west)]
    winds = blocks[ntiles:]
    turned = [pltpu.roll(wind, LANES // 2, 1) for wind in winds]
    blocks[ntiles:] = [jnp.where(low, x, y) for x, y in zip(winds, turned)]
    blocks += [jnp.where(low, y, x) for x, y in zip(winds, turned)]
    for t, value in enumerate(blocks):
        side[pl.ds(SUB * t, SUB), :] = value


def put_corners(lat_even, ntiles, nrows, at, side, za, zb):
    row = sublanes()
    outer = (row < 2) | (row >= SUB - 2)
    north = jnp.where(lat_even, 2, 0)

    def corner(p, first):
        start = pl.multiple_of(SUB * (nrows * p + first), SUB)
        one, two = side[pl.ds(start, SUB), :], side[pl.ds(start + SUB, SUB), :]
        return jnp.where(outer, one, half_turn(two))

    npairs = ntiles // nrows
    for p in range(npairs):
        to = pl.ds(at + SUB * p, SUB)
        za[to, :] = corner(p, north)
        zb[to, :] = corner(p, 2 - north)
    to = pl.ds(at + SUB * npairs, SUB)
    top = side[pl.ds(SUB * (ntiles + 2 * nrows - 1), SUB), :]
    za[to, :] = top
    zb[to, :] = top


def put_edges(q, first, side, at, nrows, edge_w, edge_e):
    for r in range(nrows):
        beside = side[pl.ds(pl.multiple_of(SUB * (at + r), SUB), SUB), :]
        edge_w[r, pl.ds(SUB, SUB), :] = beside
        edge_w[r, pl.ds(2 * SUB, SUB), :] = q[first + r, pl.ds(0, SUB), :]
        edge_e[r, pl.ds(0, SUB), :] = q[first + r, pl.ds(LANES - SUB, SUB), :]
        edge_e[r, pl.ds(SUB, SUB), :] = beside


def through(c, before, left, right, after):
    return c * (7.0 * (left + right) - (before + after))


def put_fluxes(q, first, nrows, ce, edge_w, edge_e, edge_c, flux):
    for r in range(nrows):
        window = [edge_w[r, pl.ds(SUB + k, SUB), :] for k in range(4)]
        flux[r, pl.ds(1, SUB), :] = through(edge_c[r, pl.ds(SUB + 1, SUB), :], *window)
        for b in range(LANES // SUB):
            at = SUB * b

            def load(shift):
                if at + shift < 0:
                    return edge_w[r, pl.ds(2 * SUB + shift, SUB), :]
                if at + shift + SUB > LANES:
                    return edge_e[r, pl.ds(shift, SUB), :]
                return q[first + r, pl.ds(at + shift, SUB), :]

            flux[r, pl.ds(SUB + at, SUB), :] = through(
                ce[r, pl.ds(at, SUB), :], load(-1), load(0), load(1), load(2)
            )


def lat_divergence(rows, winds):
    north = [through(winds[r], *rows[r : r + 4]) for r in range(len(winds))]
    return [north[r + 1] - north[r] for r in range(len(winds) - 1)]


def sources():
    at, n = lax.axis_index("lat"), lax.axis_size("lat")
    even = lax.rem(at, 2) == 0
    return (even, jnp.logical_not(even), jnp.logical_and(even, at > 0), jnp.logical_and(jnp.logical_not(even), at < n - 1))


def partners(where, ra, rb, span):
    north_a, south_a, south_b, north_b = where
    a, b = ra[span, :], rb[span, :]
    south = jnp.where(south_a, a, jnp.where(south_b, b, 0.0))
    return south, jnp.where(north_a, a, jnp.where(north_b, b, 0.0))


def divergence(q, pair, nrows, b, halo, cn, below, flux):
    at = SUB * b
    here = pl.ds(at, SUB)
    (s0, n0), (s1, n1) = halo(0, at), halo(1, at)
    own = [q[nrows * pair + r, here, :] for r in range(nrows)]
    winds = [below[here, :]] + [cn[r, here, :] for r in range(nrows)]
    north = lat_divergence([s0, s1] + own + [n0, n1], winds)
    div = []
    for r in range(nrows):
        east = flux[r, pl.ds(SUB + at, SUB), :] - flux[r, pl.ds(SUB + at - 1, SUB), :]
        div.append(east + north[r])
    return own, div


def put_side_section(at, nrows, where, ra, rb, corner, side, ntiles, edge_w, edge_e, edge_c, edge_d, out):
    head = sublanes() < SUB // 2

    def shifted(w, e, r, k):
        return jnp.where(head, e[r, pl.ds(SUB + k, SUB), :], w[r, pl.ds(SUB + k, SUB), :])

    def beside(t):
        return side[pl.ds(pl.multiple_of(SUB * t, SUB), SUB), :]

    start = pl.multiple_of(corner + SUB * (at // nrows), SUB)
    south, above = partners(where, ra, rb, pl.ds(start, SUB))
    s0, s1 = south, half_turn(south)
    n0, n1 = above, half_turn(above)
    own = [beside(at + r) for r in range(nrows)]
    last = pl.ds(corner + SUB * (ntiles // nrows), SUB)
    winds = [partners(where, ra, rb, last)[0]]
    winds += [beside(ntiles + nrows + r) for r in range(nrows)]
    north = lat_divergence([s0, s1] + own + [n0, n1], winds)
    for r in range(nrows):
        v = [shifted(edge_w, edge_e, r, k) for k in range(-2, 3)]
        east = through(beside(ntiles + r), *v[1:])
        west = through(shifted(edge_c, edge_d, r, -1), *v[:-1])
        new = own[r] - ((east - west) + north[r])
        out[pl.ds(pl.multiple_of(SUB * (at + r), SUB), SUB), :] = new


def edge_scratch(nrows):
    return [scratch(nrows, 3 * SUB, LANES)] * 4 + [scratch(nrows, LANES + SUB, LANES)]


def first_stage_early(pairs, ntiles, nrows, q, ce, cn, la, lb, ra, rb, section, za, zb, below, side, *edges):
    edge_w, edge_e, edge_c, edge_d, flux = edges
    lat_even, where = is_even("lat"), sources()
    half = LANES // 2
    a = partners(where, ra, rb, pl.ds(2 * pairs * LANES, half))[0]
    turned = pltpu.roll(a, half, 1)
    low = lax.broadcasted_iota(jnp.int32, (half, LANES), 1) < half
    below[pl.ds(0, half), :] = jnp.where(low, a, turned)
    below[pl.ds(half, half), :] = jnp.where(low, turned, a)
    put_side(la, lb, ntiles, side)
    put_corners(lat_even, ntiles, nrows, 2 * pairs * LANES, side, za, zb)
    put_edges(ce, 0, side, side.shape[0] // SUB - 2 * nrows, nrows, edge_c, edge_d)

    def one(p, _):
        def halo(k, shift):
            start = pl.multiple_of((2 * p + k) * LANES, LANES)
            return partners(where, ra, rb, pl.ds(start + shift, SUB))

        put_edges(q, nrows * p, side, nrows * p, nrows, edge_w, edge_e)
        put_fluxes(q, nrows * p, nrows, ce, edge_w, edge_e, edge_c, flux)
        for b in range(LANES // SUB):
            own, div = divergence(q, p, nrows, b, halo, cn, below, flux)
            for r in range(nrows):
                section[nrows * p + r, pl.ds(SUB * b, SUB), :] = own[r] - div[r]
        put_lat_sends(lat_even, section, p, nrows, za, zb)
        return 0

    lax.fori_loop(0, pairs, one, 0)


def first_stage_late(
    pairs, done, nrows, q, ce, cn, side, ra, rb, below, section, za, zb, *edges
):
    edge_w, edge_e, edge_c, edge_d, flux = edges
    lat_even, where = is_even("lat"), sources()
    put_edges(ce, 0, side, side.shape[0] // SUB - 2 * nrows, nrows, edge_c, edge_d)
    for p in range(pairs):

        def halo(k, shift):
            return partners(where, ra, rb, pl.ds((2 * p + k) * LANES + shift, SUB))

        put_edges(q, nrows * p, side, nrows * (done + p), nrows, edge_w, edge_e)
        put_fluxes(q, nrows * p, nrows, ce, edge_w, edge_e, edge_c, flux)
        for b in range(LANES // SUB):
            own, div = divergence(q, p, nrows, b, halo, cn, below, flux)
            for r in range(nrows):
                section[nrows * p + r, pl.ds(SUB * b, SUB), :] = own[r] - div[r]
        put_lat_sends(lat_even, section, p, nrows, za, zb)


def put_rows(buffer, pair, rows, nrows):
    levels = LANES // 2
    for r in range(nrows):
        turned = jnp.transpose(jnp.concatenate(rows[r], axis=0))
        for h in range(2):
            buffer[2 * pair + h, pl.ds(r, levels, stride=nrows), :] = turned[levels * h : levels * (h + 1)]


def second_stage_early(
    pairs, later, nrows, q, s, ce, cn, below, ra, rb, side, heating, q_late, s_late,
    out, heat_out, part, buffer, sems, sides, *edges
):
    edge_w, edge_e, edge_c, edge_d, flux = edges
    where = sources()
    heat_copy = pltpu.make_async_copy(heating, heat_out, sems.at[pairs])
    heat_copy.start()
    put_edges(ce, 0, side, side.shape[0] // SUB - 2 * nrows, nrows, edge_c, edge_d)

    ntiles = nrows * (pairs + later)
    for ref, first, n in ((q, 0, pairs), (q_late, pairs, later)):

        def beside(p, _):
            at = nrows * (first + p)
            put_edges(ref, nrows * p, side, at, nrows, edge_w, edge_e)
            put_side_section(
                at, nrows, where, ra, rb, 2 * pairs * LANES, side, ntiles, edge_w, edge_e, edge_c, edge_d, sides
            )
            return 0

        lax.fori_loop(0, n, beside, 0)

    def copy(p):
        return pltpu.make_async_copy(buffer.at[pl.ds(2 * p, 2)], out.at[pl.ds(2 * p, 2)], sems.at[p])

    def one(p, _):
        def halo(k, shift):
            start = pl.multiple_of((2 * p + k) * LANES, LANES)
            return partners(where, ra, rb, pl.ds(start + shift, SUB))

        put_edges(s, nrows * p, sides, nrows * p, nrows, edge_w, edge_e)
        put_fluxes(s, nrows * p, nrows, ce, edge_w, edge_e, edge_c, flux)
        parts = [[] for _ in range(nrows)]
        for b in range(LANES // SUB):
            own, div = divergence(s, p, nrows, b, halo, cn, below, flux)
            for r in range(nrows):
                old = q[nrows * p + r, pl.ds(SUB * b, SUB), :]
                parts[r].append(0.5 * ((old + own[r]) - div[r]))
        put_rows(buffer, p, parts, nrows)

        @pl.when(p == 0)
        def _():
            buffer[0] = buffer[0] + 0.5 * heating[...]

        copy(p).start()
        return 0

    def another(p, _):
        put_edges(s_late, nrows * p, sides, nrows * (pairs + p), nrows, edge_w, edge_e)
        put_fluxes(s_late, nrows * p, nrows, ce, edge_w, edge_e, edge_c, flux)
        for b in range(LANES // SUB):
            here = pl.ds(SUB * b, SUB)
            s0, s1, s2, s3 = own = [s_late[nrows * p + r, here, :] for r in range(nrows)]
            c = [below[here, :]] + [cn[r, here, :] for r in range(nrows)]
            north = [
                c[0] * (7.0 * s0 - s1),
                c[1] * (7.0 * (s0 + s1) - s2),
                through(c[2], *own),
                c[3] * (7.0 * (s2 + s3) - s1),
                c[4] * (7.0 * s3 - s2),
            ]
            for r in range(nrows):
                east = flux[r, pl.ds(SUB * (b + 1), SUB), :] - flux[r, pl.ds(SUB * (b + 1) - 1, SUB), :]
                old = q_late[nrows * p + r, here, :]
                part[nrows * p + r, here, :] = 0.5 * ((old + own[r]) - (east + (north[r + 1] - north[r])))
        return 0

    lax.fori_loop(0, pairs, one, 0)
    lax.fori_loop(0, later, another, 0)
    for p in range(pairs):
        copy(p).wait()
    heat_copy.wait()


def second_stage_late(pairs, done, nrows, part, cn, below, ra, rb, before, out, buffer, sems):
    del before
    where = sources()

    def copy(p):
        return pltpu.make_async_copy(
            buffer.at[pl.ds(2 * p, 2)], out.at[pl.ds(2 * (done + p), 2)], sems.at[p]
        )

    def one(p):
        rows = [[] for _ in range(nrows)]
        for b in range(LANES // SUB):
            here = pl.ds(SUB * b, SUB)

            def halo(k):
                start = (2 * p + k) * LANES + SUB * b
                return partners(where, ra, rb, pl.ds(start, SUB))

            (south_two, north_one), (south_one, north_two) = halo(0), halo(1)
            low = 0.5 * cn[0, here, :] * south_one
            high = 0.5 * cn[2, here, :] * north_one
            bottom = 0.5 * below[here, :] * (7.0 * south_one - south_two)
            top = 0.5 * cn[3, here, :] * (7.0 * north_one - north_two)
            p0, p1, p2, p3 = (part[nrows * p + r, here, :] for r in range(nrows))
            for r, value in enumerate((p0 + (low + bottom), p1 - low, p2 + high, p3 - (top + high))):
                rows[r].append(value)
        put_rows(buffer, p, rows, nrows)
        copy(p).start()

    for p in range(pairs):
        one(p)
    for p in range(pairs):
        copy(p).wait()


def radiation(
    nat, cosz_in, albedo_in, ext_in, single_in, weight_in, order_in, count_in, after, heat,
    water, depth, save_c, save_d, save_t, save_g, cosz, albedo, ext, single, weight, order, count, sems
):
    del after
    copies = []
    for i, (src, dst) in enumerate(
        (
            (cosz_in, cosz), (albedo_in, albedo), (ext_in, ext), (single_in, single),
            (weight_in, weight), (order_in, order), (count_in, count),
        )
    ):
        copies.append(pltpu.make_async_copy(src, dst, sems.at[i]))
        copies[-1].start()
    nrows, _ = cosz.shape
    levels = nat.shape[1] // nrows
    pairs = ext.shape[0] // 2
    x = nat[1]
    heat[...] = jnp.maximum(x, 0.0) + jnp.log1p(jnp.exp(-jnp.abs(x)))
    total = jnp.zeros((nrows, LANES), jnp.float32)
    depth[0] = jnp.zeros((2 * nrows, LANES), jnp.float32)
    for l in range(levels):
        w = heat[pl.ds(nrows * l, nrows), :]
        total = total + w
        water[l, pl.ds(0, nrows), :] = w
        water[l, pl.ds(nrows, nrows), :] = w
        depth[l + 1, pl.ds(0, nrows), :] = total
        depth[l + 1, pl.ds(nrows, nrows), :] = total
    for copy in copies:
        copy.wait()

    mu = jnp.concatenate([cosz[...], cosz[...]], axis=0)
    floor_albedo = jnp.concatenate([albedo[...], albedo[...]], axis=0)
    first = lax.broadcasted_iota(jnp.int32, (2 * nrows, LANES), 0) < nrows

    def by_band(ref):
        return [jnp.where(first, ref[2 * p], ref[2 * p + 1]) for p in range(pairs)]

    scale = 4.0 / levels
    inv_mu = 1.0 / mu
    ext_of, single_of, weight_of = by_band(ext), by_band(single), by_band(weight)
    beam = [-(e * scale * LOG2E) * inv_mu for e in ext_of]
    diffuse = [-(1.66 * scale * LOG2E) * e for e in ext_of]
    half = [0.5 * s for s in single_of]
    strength = [weight_of[p] * mu * (1.0 - single_of[p]) for p in range(pairs)]

    def up(step, carry):
        l = levels - 1 - step
        a_all, b_all, s_all = carry
        w = water[l]
        above = depth[l]
        new_a, new_b, new_s = [], [], []
        known = jnp.zeros((2 * nrows, LANES), jnp.float32)
        for p in range(pairs):
            a, b, s_bot = a_all[p], b_all[p], s_all[p]
            decay = jnp.exp2(diffuse[p] * w)
            s_top = strength[p] * jnp.exp2(beam[p] * above)
            lost = 1.0 - decay
            reflect = half[p] * lost
            transmit = decay + reflect
            taken = s_top - s_bot
            source = half[p] * taken
            den = 1.0 - reflect * a
            inv = pl.reciprocal(den, approx=True)
            inv = inv * (2.0 - den * inv)
            t = transmit * inv
            ta = t * a
            g = (reflect * b + source) * inv
            save_t[l, p] = t
            save_g[l, p] = g
            save_d[l, p] = lost + lost * ta
            known = known + (lost * (a * g + b) + taken)
            new_a.append(reflect + transmit * ta)
            new_b.append(t * (a * source + b) + source)
            new_s.append(s_top)
        save_c[l] = known
        return tuple(new_a), tuple(new_b), tuple(new_s)

    s_floor = [strength[p] * jnp.exp2(beam[p] * depth[levels]) for p in range(pairs)]
    a_floor = [floor_albedo for _ in range(pairs)]
    b_floor = [floor_albedo * s_floor[p] for p in range(pairs)]
    lax.fori_loop(0, levels, up, (tuple(a_floor), tuple(b_floor), tuple(s_floor)))

    sunlit = []
    column = lax.broadcasted_iota(jnp.int32, (LANES, LANES), 1)
    rank = lax.broadcasted_iota(jnp.int32, (LANES, LANES), 0)
    for r in range(nrows):
        place = jnp.transpose(jnp.broadcast_to(order[r], (LANES, LANES)))
        hit = (place == column) & (rank < count[r])
        sunlit.append(jnp.max(jnp.where(hit, 1.0, 0.0), axis=0, keepdims=True))
    gain = float(levels) * jnp.concatenate(sunlit, axis=0)

    def down(l, d_all):
        absorbed = save_c[l]
        for p in range(pairs):
            absorbed = absorbed + save_d[l, p] * d_all[p]
        both = absorbed[:nrows] + absorbed[nrows:]
        heat[pl.ds(pl.multiple_of(nrows * l, nrows), nrows), :] = gain * both
        return tuple(save_t[l, p] * d_all[p] + save_g[l, p] for p in range(pairs))

    d_top = tuple(jnp.zeros((2 * nrows, LANES), jnp.float32) for _ in range(pairs))
    lax.fori_loop(0, levels, down, d_top, unroll=4)


def in_hbm(x):
    return pltpu.with_memory_space_constraint(x, pltpu.HBM)


def call(kernel, name, out_shape, specs, out_specs, args, scratches, moved=1000, limit=24, **kw):
    return pl.pallas_call(
        kernel,
        out_shape=out_shape,
        in_specs=specs,
        out_specs=out_specs,
        scratch_shapes=scratches,
        compiler_params=pltpu.CompilerParams(vmem_limit_bytes=limit * MIB),
        name=name,
        cost_estimate=pl.CostEstimate(flops=moved, bytes_accessed=moved, transcendentals=0),
        **kw,
    )(*args)


def per_device(
    fields, courant, cos_zenith, albedo, extinction, single_albedo, band_weight, sun_order, sun_count
):
    nfields, levels, nrows, ncols = fields.shape
    flat = fields.reshape(nfields, levels * nrows, ncols)
    wind = courant.reshape(2, levels * nrows, ncols)
    npairs = nfields // 2
    early, late = SPLIT, npairs - SPLIT

    z0 = shape(2 * early * ncols + ncols // 2, LANES)
    tiles0, za, zb, nat, nat_late, nat_wind = call(
        functools.partial(pack_first, early, nrows),
        "pack_first",
        (
            shape(nrows * early, ncols, LANES), z0, z0,
            shape(2 * early, levels * nrows, ncols), shape(2 * late, levels * nrows, ncols),
            shape(2, levels * nrows, ncols),
        ),
        [HBM, HBM],
        (VMEM,) * 6,
        (in_hbm(flat), in_hbm(wind)),
        [pltpu.SemaphoreType.DMA((3,))],
    )
    lat0 = lat_swaps(za, zb)
    ntiles = nrows * npairs
    winds = shape(nrows, ncols, LANES)
    sides = shape(SUB * (ntiles + 2 * nrows), LANES)
    edge = shape(SUB * (ntiles + nrows) // 2, LANES)
    z1 = shape(2 * late * ncols, LANES)
    tiles1, ce, cn, la, lb, za, zb = call(
        functools.partial(pack_middle, late, nrows),
        "pack_middle",
        (shape(nrows * late, ncols, LANES), winds, winds, edge, edge, z1, z1),
        [VMEM] * 3,
        (VMEM,) * 7,
        (nat_late, nat_wind, tiles0),
        [],
    )
    lat1 = lat_swaps(za, zb)
    lon = lon_swaps(la, lb)

    edges = edge_scratch(nrows)
    z0 = shape(2 * early * ncols + SUB * (npairs + 1), LANES)
    section0, za, zb, below, side = call(
        functools.partial(first_stage_early, early, ntiles, nrows),
        "first_stage_early",
        (shape(nrows * early, ncols, LANES), z0, z0, shape(ncols, LANES), sides),
        [VMEM] * 7,
        (VMEM,) * 5,
        (tiles0, ce, cn, *lon, *lat0),
        edges,
        moved=1000_000_000,
    )
    lat2 = lat_swaps(za, zb)
    z1 = shape(2 * late * ncols, LANES)
    section1, za, zb = call(
        functools.partial(first_stage_late, late, early, nrows),
        "first_stage_late",
        (shape(nrows * late, ncols, LANES), z1, z1),
        [VMEM] * 7,
        (VMEM,) * 3,
        (tiles1, ce, cn, side, *lat1, below),
        edges,
        moved=12_000_000,
    )
    lat3 = lat_swaps(za, zb)

    pairs = extinction.shape[0] // 2
    store = scratch(levels, pairs, 2 * nrows, ncols)
    heating = call(
        radiation,
        "radiation",
        shape(levels * nrows, ncols),
        [VMEM] + [HBM] * 7 + [VMEM],
        VMEM,
        (
            nat, in_hbm(cos_zenith), in_hbm(albedo), in_hbm(extinction), in_hbm(single_albedo),
            in_hbm(band_weight), in_hbm(sun_order), in_hbm(sun_count.reshape(nrows)), section1,
        ),
        [
            scratch(levels, 2 * nrows, ncols), scratch(levels + 1, 2 * nrows, ncols),
            scratch(levels, 2 * nrows, ncols), store, store, store,
            scratch(nrows, ncols), scratch(nrows, ncols),
            pltpu.SMEM(extinction.shape, jnp.float32), pltpu.SMEM(extinction.shape, jnp.float32),
            pltpu.SMEM(extinction.shape, jnp.float32), pltpu.VMEM((nrows, 1, ncols), jnp.int32),
            pltpu.SMEM((nrows,), jnp.int32), pltpu.SemaphoreType.DMA((7,)),
        ],
        moved=16_000_000,
    )

    full = shape(nfields, levels * nrows, ncols)
    out, heat_out, part = call(
        functools.partial(second_stage_early, early, late, nrows),
        "second_stage_early",
        (full, shape(levels * nrows, ncols), shape(nrows * late, ncols, LANES)),
        [VMEM] * 11,
        (HBM, HBM, VMEM),
        (tiles0, section0, ce, cn, below, *lat2, side, heating, tiles1, section1),
        [
            scratch(2 * early, levels * nrows, ncols),
            pltpu.SemaphoreType.DMA((early + 1,)),
            scratch(SUB * ntiles, LANES),
            *edges,
        ],
    )
    out = call(
        functools.partial(second_stage_late, late, early, nrows),
        "second_stage_late",
        full,
        [VMEM] * 5 + [HBM],
        HBM,
        (part, cn, below, *lat3, out),
        [scratch(2 * late, levels * nrows, ncols), pltpu.SemaphoreType.DMA((late,))],
        input_output_aliases={5: 0},
    )
    return out.reshape(fields.shape), heat_out.reshape(levels, nrows, ncols)


def solution(mesh):
    in_specs = (
        P(None, None, "lat", "lon"),
        P(None, None, "lat", "lon"),
        P("lat", "lon"),
        P("lat", "lon"),
        P(),
        P(),
        P(),
        P("lat", "lon", None),
        P("lat", "lon"),
    )
    out_specs = (P(None, None, "lat", "lon"), P(None, "lat", "lon"))
    return jax.shard_map(
        per_device, mesh=mesh, in_specs=in_specs, out_specs=out_specs, check_vma=False
    )
```

```python
import functools
import math

import jax
import jax.numpy as jnp
from jax import lax
from jax.experimental import pallas as pl
from jax.experimental.pallas import tpu as pltpu
from jax.sharding import PartitionSpec as P

SPLIT = 2
SUB = 8
LANES = 128
LOG2E = math.log2(math.e)
VMEM = pl.BlockSpec(memory_space=pltpu.VMEM)
HBM = pl.BlockSpec(memory_space=pltpu.HBM)
MIB = 1024 * 1024


def scratch(*dims):
    return pltpu.VMEM(dims, jnp.float32)


def shape(*dims):
    return jax.ShapeDtypeStruct(dims, jnp.float32)


def lon_swaps(first_block, second_block):
    n = lax.axis_size("lon")
    first = [(i, i ^ 1) for i in range(n)]
    second = [(i, (i + 1 if i % 2 else i - 1) % n) for i in range(n)]
    return lax.ppermute(first_block, "lon", first), lax.ppermute(second_block, "lon", second)


def lat_swaps(first_block, second_block):
    nlon, nlat = lax.axis_size("lon"), lax.axis_size("lat")
    second = []
    for i in range(nlon):
        for j in range(nlat):
            k = j + 1 if j % 2 else j - 1
            to = i * nlat + k if 0 <= k < nlat else (i ^ 1) * nlat + j
            second.append((i * nlat + j, to))
    got = lax.ppermute(second_block, ("lon", "lat"), second)
    return lax.ppermute(first_block, "lat", [(j, j ^ 1) for j in range(nlat)]), got


def is_even(axis):
    return lax.rem(lax.axis_index(axis), 2) == 0


def sublanes():
    return lax.broadcasted_iota(jnp.int32, (SUB, LANES), 0)


def lanes():
    return lax.broadcasted_iota(jnp.int32, (SUB, LANES), 1)


def half_turn(block):
    return pltpu.roll(block, SUB // 2, 0)


def native(ref, index, r, nrows):
    levels = ref.shape[1] // nrows
    return ref[index, pl.ds(r, levels, stride=nrows), :]


def tile_of(low, high):
    return jnp.transpose(jnp.concatenate([low, high], axis=0))


def put_lat_sends(even, tiles, pair, nrows, za, zb):
    north = jnp.where(even, 2, 0)
    for k in range(2):
        span = pl.ds(pl.multiple_of((2 * pair + k) * LANES, LANES), LANES)
        za[span, :] = tiles[nrows * pair + north + k]
        zb[span, :] = tiles[nrows * pair + (2 - north) + k]


def take_sides(tile):
    head = sublanes() < SUB // 2
    return jnp.where(head, tile[pl.ds(0, SUB), :], tile[pl.ds(LANES - SUB, SUB), :])


def pack_first(pairs, nrows, fields, courant, tiles, za, zb, nat, nat_late, nat_wind, sems):
    n = 2 * pairs
    first = [
        pltpu.make_async_copy(fields.at[pl.ds(2 * p, 2)], nat.at[pl.ds(2 * p, 2)], sems.at[p]) for p in range(pairs)
    ]
    north = pltpu.make_async_copy(courant.at[pl.ds(1, 1)], nat_wind.at[pl.ds(1, 1)], sems.at[pairs])
    late = pltpu.make_async_copy(fields.at[pl.ds(n, nat_late.shape[0])], nat_late, sems.at[pairs + 1])
    east = pltpu.make_async_copy(courant.at[pl.ds(0, 1)], nat_wind.at[pl.ds(0, 1)], sems.at[pairs + 2])
    for copy in first + [north, late, east]:
        copy.start()
    half = LANES // 2
    even = is_even("lat")

    def body(p, up, down):
        for r in range(nrows):
            tile = tile_of(native(nat, 2 * p, r, nrows), native(nat, 2 * p + 1, r, nrows))
            tiles[nrows * p + r] = tile
            (up if r >= 2 else down)[pl.ds((2 * p + r % 2) * LANES, LANES), :] = tile
        if p < pairs - 1:
            return
        lane = lax.broadcasted_iota(jnp.int32, (half, LANES), 1)
        top = native(nat_wind, 1, nrows - 1, nrows) * (1.0 / 12.0)
        top = tile_of(top, top)
        top = jnp.where(lane < half, top[:half], top[half:])
        for ref in (up, down):
            ref[pl.ds(2 * pairs * LANES, half), :] = top

    for p in range(pairs):
        first[p].wait()
        if p == pairs - 1:
            north.wait()
        pl.when(even)(functools.partial(body, p, za, zb))
        pl.when(jnp.logical_not(even))(functools.partial(body, p, zb, za))
    late.wait()
    east.wait()


def pack_middle(pairs, nrows, nat, nat_wind, tiles_first, tiles, ce, cn, la, lb, za, zb):
    up = jnp.where(is_even("lat"), 2, 0)
    for p in range(pairs):
        for r in range(nrows):
            tiles[nrows * p + r] = tile_of(native(nat, 2 * p, r, nrows), native(nat, 2 * p + 1, r, nrows))
    for r in range(nrows):
        east = native(nat_wind, 0, r, nrows) * (1.0 / 12.0)
        north = native(nat_wind, 1, r, nrows) * (1.0 / 12.0)
        ce[r] = tile_of(east, east)
        cn[r] = tile_of(north, north)
    for i in range(2 * pairs):
        p, k = divmod(i, 2)
        span = pl.ds(i * LANES, LANES)
        za[span, :] = tiles[nrows * p + up + k]
        zb[span, :] = tiles[nrows * p + (2 - up) + k]
    even = is_even("lon")
    head, low = sublanes() < SUB // 2, lanes() < LANES // 2
    blocks = [take_sides(ref.at[t]) for ref in (tiles_first, tiles) for t in range(ref.shape[0])]
    blocks += [jnp.where(low, take_sides(ce.at[r]), take_sides(cn.at[r])) for r in range(nrows)]
    for i in range(0, len(blocks), 2):
        one, two = blocks[i : i + 2]
        east = jnp.where(head, half_turn(one), two)
        west = jnp.where(head, one, half_turn(two))
        span = pl.ds(SUB * (i // 2), SUB)
        la[span, :] = jnp.where(even, east, west)
        lb[span, :] = jnp.where(even, west, east)


def put_side(la, lb, ntiles, side):
    lon_even = is_even("lon")
    head, low = sublanes() < SUB // 2, lanes() < LANES // 2
    blocks = []
    for i in range(la.shape[0] // SUB):
        span = pl.ds(SUB * i, SUB)
        a, b = la[span, :], lb[span, :]
        east, west = jnp.where(lon_even, a, b), jnp.where(lon_even, b, a)
        blocks += [jnp.where(head, east, half_turn(west)), jnp.where(head, half_turn(east), west)]
    winds = blocks[ntiles:]
    turned = [pltpu.roll(wind, LANES // 2, 1) for wind in winds]
    blocks[ntiles:] = [jnp.where(low, x, y) for x, y in zip(winds, turned)]
    blocks += [jnp.where(low, y, x) for x, y in zip(winds, turned)]
    for t, value in enumerate(blocks):
        side[pl.ds(SUB * t, SUB), :] = value


def put_corners(lat_even, ntiles, nrows, at, side, za, zb):
    row = sublanes()
    outer = (row < 2) | (row >= SUB - 2)
    north = jnp.where(lat_even, 2, 0)

    def corner(p, first):
        start = pl.multiple_of(SUB * (nrows * p + first), SUB)
        one, two = side[pl.ds(start, SUB), :], side[pl.ds(start + SUB, SUB), :]
        return jnp.where(outer, one, half_turn(two))

    npairs = ntiles // nrows
    for p in range(npairs):
        to = pl.ds(at + SUB * p, SUB)
        za[to, :] = corner(p, north)
        zb[to, :] = corner(p, 2 - north)
    to = pl.ds(at + SUB * npairs, SUB)
    top = side[pl.ds(SUB * (ntiles + 2 * nrows - 1), SUB), :]
    za[to, :] = top
    zb[to, :] = top


def put_edges(q, first, side, at, nrows, edge_w, edge_e):
    for r in range(nrows):
        beside = side[pl.ds(pl.multiple_of(SUB * (at + r), SUB), SUB), :]
        edge_w[r, pl.ds(SUB, SUB), :] = beside
        edge_w[r, pl.ds(2 * SUB, SUB), :] = q[first + r, pl.ds(0, SUB), :]
        edge_e[r, pl.ds(0, SUB), :] = q[first + r, pl.ds(LANES - SUB, SUB), :]
        edge_e[r, pl.ds(SUB, SUB), :] = beside


def through(c, before, left, right, after):
    return c * (7.0 * (left + right) - (before + after))


def put_fluxes(q, first, nrows, ce, edge_w, edge_e, edge_c, flux):
    for r in range(nrows):
        window = [edge_w[r, pl.ds(SUB + k, SUB), :] for k in range(4)]
        flux[r, pl.ds(1, SUB), :] = through(edge_c[r, pl.ds(SUB + 1, SUB), :], *window)
        for b in range(LANES // SUB):
            at = SUB * b

            def load(shift):
                if at + shift < 0:
                    return edge_w[r, pl.ds(2 * SUB + shift, SUB), :]
                if at + shift + SUB > LANES:
                    return edge_e[r, pl.ds(shift, SUB), :]
                return q[first + r, pl.ds(at + shift, SUB), :]

            flux[r, pl.ds(SUB + at, SUB), :] = through(
                ce[r, pl.ds(at, SUB), :], load(-1), load(0), load(1), load(2)
            )


def lat_divergence(rows, winds):
    north = [through(winds[r], *rows[r : r + 4]) for r in range(len(winds))]
    return [north[r + 1] - north[r] for r in range(len(winds) - 1)]


def sources():
    at, n = lax.axis_index("lat"), lax.axis_size("lat")
    even = lax.rem(at, 2) == 0
    return (even, jnp.logical_not(even), jnp.logical_and(even, at > 0), jnp.logical_and(jnp.logical_not(even), at < n - 1))


def partners(where, ra, rb, span):
    north_a, south_a, south_b, north_b = where
    a, b = ra[span, :], rb[span, :]
    south = jnp.where(south_a, a, jnp.where(south_b, b, 0.0))
    return south, jnp.where(north_a, a, jnp.where(north_b, b, 0.0))


def divergence(q, pair, nrows, b, halo, cn, below, flux):
    at = SUB * b
    here = pl.ds(at, SUB)
    (s0, n0), (s1, n1) = halo(0, at), halo(1, at)
    own = [q[nrows * pair + r, here, :] for r in range(nrows)]
    winds = [below[here, :]] + [cn[r, here, :] for r in range(nrows)]
    north = lat_divergence([s0, s1] + own + [n0, n1], winds)
    div = []
    for r in range(nrows):
        east = flux[r, pl.ds(SUB + at, SUB), :] - flux[r, pl.ds(SUB + at - 1, SUB), :]
        div.append(east + north[r])
    return own, div


def put_side_section(at, nrows, where, ra, rb, corner, side, ntiles, edge_w, edge_e, edge_c, edge_d, out):
    head = sublanes() < SUB // 2

    def shifted(w, e, r, k):
        return jnp.where(head, e[r, pl.ds(SUB + k, SUB), :], w[r, pl.ds(SUB + k, SUB), :])

    def beside(t):
        return side[pl.ds(pl.multiple_of(SUB * t, SUB), SUB), :]

    start = pl.multiple_of(corner + SUB * (at // nrows), SUB)
    south, above = partners(where, ra, rb, pl.ds(start, SUB))
    s0, s1 = south, half_turn(south)
    n0, n1 = above, half_turn(above)
    own = [beside(at + r) for r in range(nrows)]
    last = pl.ds(corner + SUB * (ntiles // nrows), SUB)
    winds = [partners(where, ra, rb, last)[0]]
    winds += [beside(ntiles + nrows + r) for r in range(nrows)]
    north = lat_divergence([s0, s1] + own + [n0, n1], winds)
    for r in range(nrows):
        v = [shifted(edge_w, edge_e, r, k) for k in range(-2, 3)]
        east = through(beside(ntiles + r), *v[1:])
        west = through(shifted(edge_c, edge_d, r, -1), *v[:-1])
        new = own[r] - ((east - west) + north[r])
        out[pl.ds(pl.multiple_of(SUB * (at + r), SUB), SUB), :] = new


def edge_scratch(nrows):
    return [scratch(nrows, 3 * SUB, LANES)] * 4 + [scratch(nrows, LANES + SUB, LANES)]


def first_stage_early(pairs, ntiles, nrows, q, ce, cn, la, lb, ra, rb, section, za, zb, below, side, *edges):
    edge_w, edge_e, edge_c, edge_d, flux = edges
    lat_even, where = is_even("lat"), sources()
    half = LANES // 2
    a = partners(where, ra, rb, pl.ds(2 * pairs * LANES, half))[0]
    turned = pltpu.roll(a, half, 1)
    low = lax.broadcasted_iota(jnp.int32, (half, LANES), 1) < half
    below[pl.ds(0, half), :] = jnp.where(low, a, turned)
    below[pl.ds(half, half), :] = jnp.where(low, turned, a)
    put_side(la, lb, ntiles, side)
    put_corners(lat_even, ntiles, nrows, 2 * pairs * LANES, side, za, zb)
    put_edges(ce, 0, side, side.shape[0] // SUB - 2 * nrows, nrows, edge_c, edge_d)

    def one(p, _):
        def halo(k, shift):
            start = pl.multiple_of((2 * p + k) * LANES, LANES)
            return partners(where, ra, rb, pl.ds(start + shift, SUB))

        put_edges(q, nrows * p, side, nrows * p, nrows, edge_w, edge_e)
        put_fluxes(q, nrows * p, nrows, ce, edge_w, edge_e, edge_c, flux)
        for b in range(LANES // SUB):
            own, div = divergence(q, p, nrows, b, halo, cn, below, flux)
            for r in range(nrows):
                section[nrows * p + r, pl.ds(SUB * b, SUB), :] = own[r] - div[r]
        put_lat_sends(lat_even, section, p, nrows, za, zb)
        return 0

    lax.fori_loop(0, pairs, one, 0)


def first_stage_late(
    pairs, done, nrows, q, ce, cn, side, ra, rb, below, section, za, zb, *edges
):
    edge_w, edge_e, edge_c, edge_d, flux = edges
    lat_even, where = is_even("lat"), sources()
    put_edges(ce, 0, side, side.shape[0] // SUB - 2 * nrows, nrows, edge_c, edge_d)
    for p in range(pairs):

        def halo(k, shift):
            return partners(where, ra, rb, pl.ds((2 * p + k) * LANES + shift, SUB))

        put_edges(q, nrows * p, side, nrows * (done + p), nrows, edge_w, edge_e)
        put_fluxes(q, nrows * p, nrows, ce, edge_w, edge_e, edge_c, flux)
        for b in range(LANES // SUB):
            own, div = divergence(q, p, nrows, b, halo, cn, below, flux)
            for r in range(nrows):
                section[nrows * p + r, pl.ds(SUB * b, SUB), :] = own[r] - div[r]
        put_lat_sends(lat_even, section, p, nrows, za, zb)


def put_rows(buffer, pair, rows, nrows):
    levels = LANES // 2
    for r in range(nrows):
        turned = jnp.transpose(jnp.concatenate(rows[r], axis=0))
        for h in range(2):
            buffer[2 * pair + h, pl.ds(r, levels, stride=nrows), :] = turned[levels * h : levels * (h + 1)]


def second_stage_early(
    pairs, later, nrows, q, s, ce, cn, below, ra, rb, side, heating, q_late, s_late,
    out, heat_out, part, buffer, sems, sides, *edges
):
    edge_w, edge_e, edge_c, edge_d, flux = edges
    where = sources()
    heat_copy = pltpu.make_async_copy(heating, heat_out, sems.at[pairs])
    heat_copy.start()
    put_edges(ce, 0, side, side.shape[0] // SUB - 2 * nrows, nrows, edge_c, edge_d)

    ntiles = nrows * (pairs + later)
    for ref, first, n in ((q, 0, pairs), (q_late, pairs, later)):

        def beside(p, _):
            at = nrows * (first + p)
            put_edges(ref, nrows * p, side, at, nrows, edge_w, edge_e)
            put_side_section(
                at, nrows, where, ra, rb, 2 * pairs * LANES, side, ntiles, edge_w, edge_e, edge_c, edge_d, sides
            )
            return 0

        lax.fori_loop(0, n, beside, 0)

    def copy(p):
        return pltpu.make_async_copy(buffer.at[pl.ds(2 * p, 2)], out.at[pl.ds(2 * p, 2)], sems.at[p])

    def one(p, _):
        def halo(k, shift):
            start = pl.multiple_of((2 * p + k) * LANES, LANES)
            return partners(where, ra, rb, pl.ds(start + shift, SUB))

        put_edges(s, nrows * p, sides, nrows * p, nrows, edge_w, edge_e)
        put_fluxes(s, nrows * p, nrows, ce, edge_w, edge_e, edge_c, flux)
        parts = [[] for _ in range(nrows)]
        for b in range(LANES // SUB):
            own, div = divergence(s, p, nrows, b, halo, cn, below, flux)
            for r in range(nrows):
                old = q[nrows * p + r, pl.ds(SUB * b, SUB), :]
                parts[r].append(0.5 * ((old + own[r]) - div[r]))
        put_rows(buffer, p, parts, nrows)

        @pl.when(p == 0)
        def _():
            buffer[0] = buffer[0] + 0.5 * heating[...]

        copy(p).start()
        return 0

    def another(p, _):
        put_edges(s_late, nrows * p, sides, nrows * (pairs + p), nrows, edge_w, edge_e)
        put_fluxes(s_late, nrows * p, nrows, ce, edge_w, edge_e, edge_c, flux)
        for b in range(LANES // SUB):
            here = pl.ds(SUB * b, SUB)
            s0, s1, s2, s3 = own = [s_late[nrows * p + r, here, :] for r in range(nrows)]
            c = [below[here, :]] + [cn[r, here, :] for r in range(nrows)]
            north = [
                c[0] * (7.0 * s0 - s1),
                c[1] * (7.0 * (s0 + s1) - s2),
                through(c[2], *own),
                c[3] * (7.0 * (s2 + s3) - s1),
                c[4] * (7.0 * s3 - s2),
            ]
            for r in range(nrows):
                east = flux[r, pl.ds(SUB * (b + 1), SUB), :] - flux[r, pl.ds(SUB * (b + 1) - 1, SUB), :]
                old = q_late[nrows * p + r, here, :]
                part[nrows * p + r, here, :] = 0.5 * ((old + own[r]) - (east + (north[r + 1] - north[r])))
        return 0

    lax.fori_loop(0, pairs, one, 0)
    lax.fori_loop(0, later, another, 0)
    for p in range(pairs):
        copy(p).wait()
    heat_copy.wait()


def second_stage_late(pairs, done, nrows, part, cn, below, ra, rb, before, out, buffer, sems):
    del before
    where = sources()

    def copy(p):
        return pltpu.make_async_copy(
            buffer.at[pl.ds(2 * p, 2)], out.at[pl.ds(2 * (done + p), 2)], sems.at[p]
        )

    def one(p):
        rows = [[] for _ in range(nrows)]
        for b in range(LANES // SUB):
            here = pl.ds(SUB * b, SUB)

            def halo(k):
                start = (2 * p + k) * LANES + SUB * b
                return partners(where, ra, rb, pl.ds(start, SUB))

            (south_two, north_one), (south_one, north_two) = halo(0), halo(1)
            low = 0.5 * cn[0, here, :] * south_one
            high = 0.5 * cn[2, here, :] * north_one
            bottom = 0.5 * below[here, :] * (7.0 * south_one - south_two)
            top = 0.5 * cn[3, here, :] * (7.0 * north_one - north_two)
            p0, p1, p2, p3 = (part[nrows * p + r, here, :] for r in range(nrows))
            for r, value in enumerate((p0 + (low + bottom), p1 - low, p2 + high, p3 - (top + high))):
                rows[r].append(value)
        put_rows(buffer, p, rows, nrows)
        copy(p).start()

    for p in range(pairs):
        one(p)
    for p in range(pairs):
        copy(p).wait()


def radiation(
    nat, cosz_in, albedo_in, ext_in, single_in, weight_in, order_in, count_in, after, heat,
    water, depth, save_c, save_d, save_t, save_g, cosz, albedo, ext, single, weight, order, count, sems
):
    del after
    copies = []
    for i, (src, dst) in enumerate(
        (
            (cosz_in, cosz), (albedo_in, albedo), (ext_in, ext), (single_in, single),
            (weight_in, weight), (order_in, order), (count_in, count),
        )
    ):
        copies.append(pltpu.make_async_copy(src, dst, sems.at[i]))
        copies[-1].start()
    nrows, _ = cosz.shape
    levels = nat.shape[1] // nrows
    pairs = ext.shape[0] // 2
    x = nat[1]
    heat[...] = jnp.maximum(x, 0.0) + jnp.log1p(jnp.exp(-jnp.abs(x)))
    total = jnp.zeros((nrows, LANES), jnp.float32)
    depth[0] = jnp.zeros((2 * nrows, LANES), jnp.float32)
    for l in range(levels):
        w = heat[pl.ds(nrows * l, nrows), :]
        total = total + w
        water[l, pl.ds(0, nrows), :] = w
        water[l, pl.ds(nrows, nrows), :] = w
        depth[l + 1, pl.ds(0, nrows), :] = total
        depth[l + 1, pl.ds(nrows, nrows), :] = total
    for copy in copies:
        copy.wait()

    mu = jnp.concatenate([cosz[...], cosz[...]], axis=0)
    floor_albedo = jnp.concatenate([albedo[...], albedo[...]], axis=0)
    first = lax.broadcasted_iota(jnp.int32, (2 * nrows, LANES), 0) < nrows

    def by_band(ref):
        return [jnp.where(first, ref[2 * p], ref[2 * p + 1]) for p in range(pairs)]

    scale = 4.0 / levels
    inv_mu = 1.0 / mu
    ext_of, single_of, weight_of = by_band(ext), by_band(single), by_band(weight)
    beam = [-(e * scale * LOG2E) * inv_mu for e in ext_of]
    diffuse = [-(1.66 * scale * LOG2E) * e for e in ext_of]
    half = [0.5 * s for s in single_of]
    strength = [weight_of[p] * mu * (1.0 - single_of[p]) for p in range(pairs)]

    def up(step, carry):
        l = levels - 1 - step
        a_all, b_all, s_all = carry
        w = water[l]
        above = depth[l]
        new_a, new_b, new_s = [], [], []
        known = jnp.zeros((2 * nrows, LANES), jnp.float32)
        for p in range(pairs):
            a, b, s_bot = a_all[p], b_all[p], s_all[p]
            decay = jnp.exp2(diffuse[p] * w)
            s_top = strength[p] * jnp.exp2(beam[p] * above)
            lost = 1.0 - decay
            reflect = half[p] * lost
            transmit = decay + reflect
            taken = s_top - s_bot
            source = half[p] * taken
            den = 1.0 - reflect * a
            inv = pl.reciprocal(den, approx=True)
            inv = inv * (2.0 - den * inv)
            t = transmit * inv
            ta = t * a
            g = (reflect * b + source) * inv
            save_t[l, p] = t
            save_g[l, p] = g
            save_d[l, p] = lost + lost * ta
            known = known + (lost * (a * g + b) + taken)
            new_a.append(reflect + transmit * ta)
            new_b.append(t * (a * source + b) + source)
            new_s.append(s_top)
        save_c[l] = known
        return tuple(new_a), tuple(new_b), tuple(new_s)

    s_floor = [strength[p] * jnp.exp2(beam[p] * depth[levels]) for p in range(pairs)]
    a_floor = [floor_albedo for _ in range(pairs)]
    b_floor = [floor_albedo * s_floor[p] for p in range(pairs)]
    lax.fori_loop(0, levels, up, (tuple(a_floor), tuple(b_floor), tuple(s_floor)))

    sunlit = []
    column = lax.broadcasted_iota(jnp.int32, (LANES, LANES), 1)
    rank = lax.broadcasted_iota(jnp.int32, (LANES, LANES), 0)
    for r in range(nrows):
        place = jnp.transpose(jnp.broadcast_to(order[r], (LANES, LANES)))
        hit = (place == column) & (rank < count[r])
        sunlit.append(jnp.max(jnp.where(hit, 1.0, 0.0), axis=0, keepdims=True))
    gain = float(levels) * jnp.concatenate(sunlit, axis=0)

    def down(l, d_all):
        absorbed = save_c[l]
        for p in range(pairs):
            absorbed = absorbed + save_d[l, p] * d_all[p]
        both = absorbed[:nrows] + absorbed[nrows:]
        heat[pl.ds(pl.multiple_of(nrows * l, nrows), nrows), :] = gain * both
        return tuple(save_t[l, p] * d_all[p] + save_g[l, p] for p in range(pairs))

    d_top = tuple(jnp.zeros((2 * nrows, LANES), jnp.float32) for _ in range(pairs))
    lax.fori_loop(0, levels, down, d_top, unroll=4)


def in_hbm(x):
    return pltpu.with_memory_space_constraint(x, pltpu.HBM)


def call(kernel, name, out_shape, specs, out_specs, args, scratches, moved=1000, limit=24, **kw):
    return pl.pallas_call(
        kernel,
        out_shape=out_shape,
        in_specs=specs,
        out_specs=out_specs,
        scratch_shapes=scratches,
        compiler_params=pltpu.CompilerParams(vmem_limit_bytes=limit * MIB),
        name=name,
        cost_estimate=pl.CostEstimate(flops=moved, bytes_accessed=moved, transcendentals=0),
        **kw,
    )(*args)


def per_device(
    fields, courant, cos_zenith, albedo, extinction, single_albedo, band_weight, sun_order, sun_count
):
    nfields, levels, nrows, ncols = fields.shape
    flat = fields.reshape(nfields, levels * nrows, ncols)
    wind = courant.reshape(2, levels * nrows, ncols)
    npairs = nfields // 2
    early, late = SPLIT, npairs - SPLIT

    z0 = shape(2 * early * ncols + ncols // 2, LANES)
    tiles0, za, zb, nat, nat_late, nat_wind = call(
        functools.partial(pack_first, early, nrows),
        "pack_first",
        (
            shape(nrows * early, ncols, LANES), z0, z0,
            shape(2 * early, levels * nrows, ncols), shape(2 * late, levels * nrows, ncols),
            shape(2, levels * nrows, ncols),
        ),
        [HBM, HBM],
        (VMEM,) * 6,
        (in_hbm(flat), in_hbm(wind)),
        [pltpu.SemaphoreType.DMA((early + 3,))],
    )
    lat0 = lat_swaps(za, zb)
    ntiles = nrows * npairs
    winds = shape(nrows, ncols, LANES)
    sides = shape(SUB * (ntiles + 2 * nrows), LANES)
    edge = shape(SUB * (ntiles + nrows) // 2, LANES)
    z1 = shape(2 * late * ncols, LANES)
    tiles1, ce, cn, la, lb, za, zb = call(
        functools.partial(pack_middle, late, nrows),
        "pack_middle",
        (shape(nrows * late, ncols, LANES), winds, winds, edge, edge, z1, z1),
        [VMEM] * 3,
        (VMEM,) * 7,
        (nat_late, nat_wind, tiles0),
        [],
    )
    lat1 = lat_swaps(za, zb)
    lon = lon_swaps(la, lb)

    edges = edge_scratch(nrows)
    z0 = shape(2 * early * ncols + SUB * (npairs + 1), LANES)
    section0, za, zb, below, side = call(
        functools.partial(first_stage_early, early, ntiles, nrows),
        "first_stage_early",
        (shape(nrows * early, ncols, LANES), z0, z0, shape(ncols, LANES), sides),
        [VMEM] * 7,
        (VMEM,) * 5,
        (tiles0, ce, cn, *lon, *lat0),
        edges,
        moved=1000_000_000,
    )
    lat2 = lat_swaps(za, zb)
    z1 = shape(2 * late * ncols, LANES)
    section1, za, zb = call(
        functools.partial(first_stage_late, late, early, nrows),
        "first_stage_late",
        (shape(nrows * late, ncols, LANES), z1, z1),
        [VMEM] * 7,
        (VMEM,) * 3,
        (tiles1, ce, cn, side, *lat1, below),
        edges,
        moved=12_000_000,
    )
    lat3 = lat_swaps(za, zb)

    pairs = extinction.shape[0] // 2
    store = scratch(levels, pairs, 2 * nrows, ncols)
    heating = call(
        radiation,
        "radiation",
        shape(levels * nrows, ncols),
        [VMEM] + [HBM] * 7 + [VMEM],
        VMEM,
        (
            nat, in_hbm(cos_zenith), in_hbm(albedo), in_hbm(extinction), in_hbm(single_albedo),
            in_hbm(band_weight), in_hbm(sun_order), in_hbm(sun_count.reshape(nrows)), section1,
        ),
        [
            scratch(levels, 2 * nrows, ncols), scratch(levels + 1, 2 * nrows, ncols),
            scratch(levels, 2 * nrows, ncols), store, store, store,
            scratch(nrows, ncols), scratch(nrows, ncols),
            pltpu.SMEM(extinction.shape, jnp.float32), pltpu.SMEM(extinction.shape, jnp.float32),
            pltpu.SMEM(extinction.shape, jnp.float32), pltpu.VMEM((nrows, 1, ncols), jnp.int32),
            pltpu.SMEM((nrows,), jnp.int32), pltpu.SemaphoreType.DMA((7,)),
        ],
        moved=16_000_000,
    )

    full = shape(nfields, levels * nrows, ncols)
    out, heat_out, part = call(
        functools.partial(second_stage_early, early, late, nrows),
        "second_stage_early",
        (full, shape(levels * nrows, ncols), shape(nrows * late, ncols, LANES)),
        [VMEM] * 11,
        (HBM, HBM, VMEM),
        (tiles0, section0, ce, cn, below, *lat2, side, heating, tiles1, section1),
        [
            scratch(2 * early, levels * nrows, ncols),
            pltpu.SemaphoreType.DMA((early + 1,)),
            scratch(SUB * ntiles, LANES),
            *edges,
        ],
    )
    out = call(
        functools.partial(second_stage_late, late, early, nrows),
        "second_stage_late",
        full,
        [VMEM] * 5 + [HBM],
        HBM,
        (part, cn, below, *lat3, out),
        [scratch(2 * late, levels * nrows, ncols), pltpu.SemaphoreType.DMA((late,))],
        input_output_aliases={5: 0},
    )
    return out.reshape(fields.shape), heat_out.reshape(levels, nrows, ncols)


def solution(mesh):
    in_specs = (
        P(None, None, "lat", "lon"),
        P(None, None, "lat", "lon"),
        P("lat", "lon"),
        P("lat", "lon"),
        P(),
        P(),
        P(),
        P("lat", "lon", None),
        P("lat", "lon"),
    )
    out_specs = (P(None, None, "lat", "lon"), P(None, "lat", "lon"))
    return jax.shard_map(
        per_device, mesh=mesh, in_specs=in_specs, out_specs=out_specs, check_vma=False
    )
```

```python
import functools
import math

import jax
import jax.numpy as jnp
from jax import lax
from jax.experimental import pallas as pl
from jax.experimental.pallas import tpu as pltpu
from jax.sharding import PartitionSpec as P

SPLIT = 2
SUB = 8
LANES = 128
LOG2E = math.log2(math.e)
VMEM = pl.BlockSpec(memory_space=pltpu.VMEM)
HBM = pl.BlockSpec(memory_space=pltpu.HBM)
MIB = 1024 * 1024


def scratch(*dims):
    return pltpu.VMEM(dims, jnp.float32)


def shape(*dims):
    return jax.ShapeDtypeStruct(dims, jnp.float32)


def lon_swaps(first_block, second_block):
    n = lax.axis_size("lon")
    first = [(i, i ^ 1) for i in range(n)]
    second = [(i, (i + 1 if i % 2 else i - 1) % n) for i in range(n)]
    return lax.ppermute(first_block, "lon", first), lax.ppermute(second_block, "lon", second)


def lat_swaps(first_block, second_block):
    nlon, nlat = lax.axis_size("lon"), lax.axis_size("lat")
    second = []
    for i in range(nlon):
        for j in range(nlat):
            k = j + 1 if j % 2 else j - 1
            to = i * nlat + k if 0 <= k < nlat else (i ^ 1) * nlat + j
            second.append((i * nlat + j, to))
    got = lax.ppermute(second_block, ("lon", "lat"), second)
    return lax.ppermute(first_block, "lat", [(j, j ^ 1) for j in range(nlat)]), got


def is_even(axis):
    return lax.rem(lax.axis_index(axis), 2) == 0


def sublanes():
    return lax.broadcasted_iota(jnp.int32, (SUB, LANES), 0)


def lanes():
    return lax.broadcasted_iota(jnp.int32, (SUB, LANES), 1)


def half_turn(block):
    return pltpu.roll(block, SUB // 2, 0)


def native(ref, index, r, nrows):
    levels = ref.shape[1] // nrows
    return ref[index, pl.ds(r, levels, stride=nrows), :]


def tile_of(low, high):
    return jnp.transpose(jnp.concatenate([low, high], axis=0))


def put_lat_sends(even, tiles, pair, nrows, za, zb):
    north = jnp.where(even, 2, 0)
    for k in range(2):
        span = pl.ds(pl.multiple_of((2 * pair + k) * LANES, LANES), LANES)
        za[span, :] = tiles[nrows * pair + north + k]
        zb[span, :] = tiles[nrows * pair + (2 - north) + k]


def take_sides(tile):
    head = sublanes() < SUB // 2
    return jnp.where(head, tile[pl.ds(0, SUB), :], tile[pl.ds(LANES - SUB, SUB), :])


def pack_first(pairs, nrows, fields, courant, tiles, za, zb, nat, nat_late, nat_wind, sems):
    n = 2 * pairs
    first = [
        pltpu.make_async_copy(fields.at[pl.ds(2 * p, 2)], nat.at[pl.ds(2 * p, 2)], sems.at[p]) for p in range(pairs)
    ]
    north = pltpu.make_async_copy(courant.at[pl.ds(1, 1)], nat_wind.at[pl.ds(1, 1)], sems.at[pairs])
    late = pltpu.make_async_copy(fields.at[pl.ds(n, nat_late.shape[0])], nat_late, sems.at[pairs + 1])
    east = pltpu.make_async_copy(courant.at[pl.ds(0, 1)], nat_wind.at[pl.ds(0, 1)], sems.at[pairs + 2])
    for copy in first + [north, late, east]:
        copy.start()
    half = LANES // 2
    even = is_even("lat")

    def body(p, up, down):
        for r in range(nrows):
            tile = tile_of(native(nat, 2 * p, r, nrows), native(nat, 2 * p + 1, r, nrows))
            tiles[nrows * p + r] = tile
            (up if r >= 2 else down)[pl.ds((2 * p + r % 2) * LANES, LANES), :] = tile
        if p < pairs - 1:
            return
        lane = lax.broadcasted_iota(jnp.int32, (half, LANES), 1)
        top = native(nat_wind, 1, nrows - 1, nrows) * (1.0 / 12.0)
        top = tile_of(top, top)
        top = jnp.where(lane < half, top[:half], top[half:])
        for ref in (up, down):
            ref[pl.ds(2 * pairs * LANES, half), :] = top

    for p in range(pairs):
        first[p].wait()
        if p == pairs - 1:
            north.wait()
        pl.when(even)(functools.partial(body, p, za, zb))
        pl.when(jnp.logical_not(even))(functools.partial(body, p, zb, za))
    late.wait()
    east.wait()


def pack_middle(pairs, nrows, nat, nat_wind, tiles_first, tiles, ce, cn, la, lb, za, zb):
    up = jnp.where(is_even("lat"), 2, 0)
    for p in range(pairs):
        for r in range(nrows):
            tiles[nrows * p + r] = tile_of(native(nat, 2 * p, r, nrows), native(nat, 2 * p + 1, r, nrows))
    for r in range(nrows):
        east = native(nat_wind, 0, r, nrows) * (1.0 / 12.0)
        north = native(nat_wind, 1, r, nrows) * (1.0 / 12.0)
        ce[r] = tile_of(east, east)
        cn[r] = tile_of(north, north)
    for i in range(2 * pairs):
        p, k = divmod(i, 2)
        span = pl.ds(i * LANES, LANES)
        za[span, :] = tiles[nrows * p + up + k]
        zb[span, :] = tiles[nrows * p + (2 - up) + k]
    even = is_even("lon")
    head, low = sublanes() < SUB // 2, lanes() < LANES // 2
    blocks = [take_sides(ref.at[t]) for ref in (tiles_first, tiles) for t in range(ref.shape[0])]
    blocks += [jnp.where(low, take_sides(ce.at[r]), take_sides(cn.at[r])) for r in range(nrows)]
    for i in range(0, len(blocks), 2):
        one, two = blocks[i : i + 2]
        east = jnp.where(head, half_turn(one), two)
        west = jnp.where(head, one, half_turn(two))
        span = pl.ds(SUB * (i // 2), SUB)
        la[span, :] = jnp.where(even, east, west)
        lb[span, :] = jnp.where(even, west, east)


def put_side(la, lb, ntiles, side):
    lon_even = is_even("lon")
    head, low = sublanes() < SUB // 2, lanes() < LANES // 2
    blocks = []
    for i in range(la.shape[0] // SUB):
        span = pl.ds(SUB * i, SUB)
        a, b = la[span, :], lb[span, :]
        east, west = jnp.where(lon_even, a, b), jnp.where(lon_even, b, a)
        blocks += [jnp.where(head, east, half_turn(west)), jnp.where(head, half_turn(east), west)]
    winds = blocks[ntiles:]
    turned = [pltpu.roll(wind, LANES // 2, 1) for wind in winds]
    blocks[ntiles:] = [jnp.where(low, x, y) for x, y in zip(winds, turned)]
    blocks += [jnp.where(low, y, x) for x, y in zip(winds, turned)]
    for t, value in enumerate(blocks):
        side[pl.ds(SUB * t, SUB), :] = value


def put_corners(lat_even, ntiles, nrows, at, side, za, zb):
    row = sublanes()
    outer = (row < 2) | (row >= SUB - 2)
    north = jnp.where(lat_even, 2, 0)

    def corner(p, first):
        start = pl.multiple_of(SUB * (nrows * p + first), SUB)
        one, two = side[pl.ds(start, SUB), :], side[pl.ds(start + SUB, SUB), :]
        return jnp.where(outer, one, half_turn(two))

    npairs = ntiles // nrows
    for p in range(npairs):
        to = pl.ds(at + SUB * p, SUB)
        za[to, :] = corner(p, north)
        zb[to, :] = corner(p, 2 - north)
    to = pl.ds(at + SUB * npairs, SUB)
    top = side[pl.ds(SUB * (ntiles + 2 * nrows - 1), SUB), :]
    za[to, :] = top
    zb[to, :] = top


def put_edges(q, first, side, at, nrows, edge_w, edge_e):
    for r in range(nrows):
        beside = side[pl.ds(pl.multiple_of(SUB * (at + r), SUB), SUB), :]
        edge_w[r, pl.ds(SUB, SUB), :] = beside
        edge_w[r, pl.ds(2 * SUB, SUB), :] = q[first + r, pl.ds(0, SUB), :]
        edge_e[r, pl.ds(0, SUB), :] = q[first + r, pl.ds(LANES - SUB, SUB), :]
        edge_e[r, pl.ds(SUB, SUB), :] = beside


def through(c, before, left, right, after):
    return c * (7.0 * (left + right) - (before + after))


def put_fluxes(q, first, nrows, ce, edge_w, edge_e, edge_c, flux):
    for r in range(nrows):
        window = [edge_w[r, pl.ds(SUB + k, SUB), :] for k in range(4)]
        flux[r, pl.ds(1, SUB), :] = through(edge_c[r, pl.ds(SUB + 1, SUB), :], *window)
        for b in range(LANES // SUB):
            at = SUB * b

            def load(shift):
                if at + shift < 0:
                    return edge_w[r, pl.ds(2 * SUB + shift, SUB), :]
                if at + shift + SUB > LANES:
                    return edge_e[r, pl.ds(shift, SUB), :]
                return q[first + r, pl.ds(at + shift, SUB), :]

            flux[r, pl.ds(SUB + at, SUB), :] = through(
                ce[r, pl.ds(at, SUB), :], load(-1), load(0), load(1), load(2)
            )


def lat_divergence(rows, winds):
    north = [through(winds[r], *rows[r : r + 4]) for r in range(len(winds))]
    return [north[r + 1] - north[r] for r in range(len(winds) - 1)]


def sources():
    at, n = lax.axis_index("lat"), lax.axis_size("lat")
    even = lax.rem(at, 2) == 0
    return (even, jnp.logical_not(even), jnp.logical_and(even, at > 0), jnp.logical_and(jnp.logical_not(even), at < n - 1))


def partners(where, ra, rb, span):
    north_a, south_a, south_b, north_b = where
    a, b = ra[span, :], rb[span, :]
    south = jnp.where(south_a, a, jnp.where(south_b, b, 0.0))
    return south, jnp.where(north_a, a, jnp.where(north_b, b, 0.0))


def divergence(q, pair, nrows, b, halo, cn, below, flux):
    at = SUB * b
    here = pl.ds(at, SUB)
    (s0, n0), (s1, n1) = halo(0, at), halo(1, at)
    own = [q[nrows * pair + r, here, :] for r in range(nrows)]
    winds = [below[here, :]] + [cn[r, here, :] for r in range(nrows)]
    north = lat_divergence([s0, s1] + own + [n0, n1], winds)
    div = []
    for r in range(nrows):
        east = flux[r, pl.ds(SUB + at, SUB), :] - flux[r, pl.ds(SUB + at - 1, SUB), :]
        div.append(east + north[r])
    return own, div


def put_side_section(at, nrows, where, ra, rb, corner, side, ntiles, edge_w, edge_e, edge_c, edge_d, out):
    head = sublanes() < SUB // 2

    def shifted(w, e, r, k):
        return jnp.where(head, e[r, pl.ds(SUB + k, SUB), :], w[r, pl.ds(SUB + k, SUB), :])

    def beside(t):
        return side[pl.ds(pl.multiple_of(SUB * t, SUB), SUB), :]

    start = pl.multiple_of(corner + SUB * (at // nrows), SUB)
    south, above = partners(where, ra, rb, pl.ds(start, SUB))
    s0, s1 = south, half_turn(south)
    n0, n1 = above, half_turn(above)
    own = [beside(at + r) for r in range(nrows)]
    last = pl.ds(corner + SUB * (ntiles // nrows), SUB)
    winds = [partners(where, ra, rb, last)[0]]
    winds += [beside(ntiles + nrows + r) for r in range(nrows)]
    north = lat_divergence([s0, s1] + own + [n0, n1], winds)
    for r in range(nrows):
        v = [shifted(edge_w, edge_e, r, k) for k in range(-2, 3)]
        east = through(beside(ntiles + r), *v[1:])
        west = through(shifted(edge_c, edge_d, r, -1), *v[:-1])
        new = own[r] - ((east - west) + north[r])
        out[pl.ds(pl.multiple_of(SUB * (at + r), SUB), SUB), :] = new


def edge_scratch(nrows):
    return [scratch(nrows, 3 * SUB, LANES)] * 4 + [scratch(nrows, LANES + SUB, LANES)]


def first_stage_early(pairs, ntiles, nrows, q, ce, cn, la, lb, ra, rb, section, za, zb, below, side, *edges):
    edge_w, edge_e, edge_c, edge_d, flux = edges
    lat_even, where = is_even("lat"), sources()
    half = LANES // 2
    a = partners(where, ra, rb, pl.ds(2 * pairs * LANES, half))[0]
    turned = pltpu.roll(a, half, 1)
    low = lax.broadcasted_iota(jnp.int32, (half, LANES), 1) < half
    below[pl.ds(0, half), :] = jnp.where(low, a, turned)
    below[pl.ds(half, half), :] = jnp.where(low, turned, a)
    put_side(la, lb, ntiles, side)
    put_corners(lat_even, ntiles, nrows, 2 * pairs * LANES, side, za, zb)
    put_edges(ce, 0, side, side.shape[0] // SUB - 2 * nrows, nrows, edge_c, edge_d)

    def one(p, _):
        def halo(k, shift):
            start = pl.multiple_of((2 * p + k) * LANES, LANES)
            return partners(where, ra, rb, pl.ds(start + shift, SUB))

        put_edges(q, nrows * p, side, nrows * p, nrows, edge_w, edge_e)
        put_fluxes(q, nrows * p, nrows, ce, edge_w, edge_e, edge_c, flux)
        for b in range(LANES // SUB):
            own, div = divergence(q, p, nrows, b, halo, cn, below, flux)
            for r in range(nrows):
                section[nrows * p + r, pl.ds(SUB * b, SUB), :] = own[r] - div[r]
        put_lat_sends(lat_even, section, p, nrows, za, zb)
        return 0

    lax.fori_loop(0, pairs, one, 0)


def first_stage_late(
    pairs, done, nrows, q, ce, cn, side, ra, rb, below, section, za, zb, *edges
):
    edge_w, edge_e, edge_c, edge_d, flux = edges
    lat_even, where = is_even("lat"), sources()
    put_edges(ce, 0, side, side.shape[0] // SUB - 2 * nrows, nrows, edge_c, edge_d)
    for p in range(pairs):

        def halo(k, shift):
            return partners(where, ra, rb, pl.ds((2 * p + k) * LANES + shift, SUB))

        put_edges(q, nrows * p, side, nrows * (done + p), nrows, edge_w, edge_e)
        put_fluxes(q, nrows * p, nrows, ce, edge_w, edge_e, edge_c, flux)
        for b in range(LANES // SUB):
            own, div = divergence(q, p, nrows, b, halo, cn, below, flux)
            for r in range(nrows):
                section[nrows * p + r, pl.ds(SUB * b, SUB), :] = own[r] - div[r]
        up = jnp.where(lat_even, 2, 0)
        for k in range(2):
            span = pl.ds((2 * p + k) * LANES, LANES)
            za[span, :] = jnp.transpose(section[nrows * p + up + k])
            zb[span, :] = jnp.transpose(section[nrows * p + (2 - up) + k])


def put_rows(buffer, pair, rows, nrows):
    levels = LANES // 2
    for r in range(nrows):
        turned = jnp.transpose(jnp.concatenate(rows[r], axis=0))
        for h in range(2):
            buffer[2 * pair + h, pl.ds(r, levels, stride=nrows), :] = turned[levels * h : levels * (h + 1)]


def second_stage_early(
    pairs, later, nrows, q, s, ce, cn, below, ra, rb, side, heating, q_late, s_late,
    out, heat_out, part, winds, buffer, sems, sides, *edges
):
    edge_w, edge_e, edge_c, edge_d, flux = edges
    where = sources()
    heat_copy = pltpu.make_async_copy(heating, heat_out, sems.at[pairs])
    heat_copy.start()
    put_edges(ce, 0, side, side.shape[0] // SUB - 2 * nrows, nrows, edge_c, edge_d)

    ntiles = nrows * (pairs + later)
    for ref, first, n in ((q, 0, pairs), (q_late, pairs, later)):

        def beside(p, _):
            at = nrows * (first + p)
            put_edges(ref, nrows * p, side, at, nrows, edge_w, edge_e)
            put_side_section(
                at, nrows, where, ra, rb, 2 * pairs * LANES, side, ntiles, edge_w, edge_e, edge_c, edge_d, sides
            )
            return 0

        lax.fori_loop(0, n, beside, 0)

    def copy(p):
        return pltpu.make_async_copy(buffer.at[pl.ds(2 * p, 2)], out.at[pl.ds(2 * p, 2)], sems.at[p])

    def one(p, _):
        def halo(k, shift):
            start = pl.multiple_of((2 * p + k) * LANES, LANES)
            return partners(where, ra, rb, pl.ds(start + shift, SUB))

        put_edges(s, nrows * p, sides, nrows * p, nrows, edge_w, edge_e)
        put_fluxes(s, nrows * p, nrows, ce, edge_w, edge_e, edge_c, flux)
        parts = [[] for _ in range(nrows)]
        for b in range(LANES // SUB):
            own, div = divergence(s, p, nrows, b, halo, cn, below, flux)
            for r in range(nrows):
                old = q[nrows * p + r, pl.ds(SUB * b, SUB), :]
                parts[r].append(0.5 * ((old + own[r]) - div[r]))
        put_rows(buffer, p, parts, nrows)

        @pl.when(p == 0)
        def _():
            buffer[0] = buffer[0] + 0.5 * heating[...]

        copy(p).start()
        return 0

    def another(p, _):
        put_edges(s_late, nrows * p, sides, nrows * (pairs + p), nrows, edge_w, edge_e)
        put_fluxes(s_late, nrows * p, nrows, ce, edge_w, edge_e, edge_c, flux)
        rows = [[] for _ in range(nrows)]
        for b in range(LANES // SUB):
            here = pl.ds(SUB * b, SUB)
            s0, s1, s2, s3 = own = [s_late[nrows * p + r, here, :] for r in range(nrows)]
            c = [below[here, :]] + [cn[r, here, :] for r in range(nrows)]
            north = [
                c[0] * (7.0 * s0 - s1),
                c[1] * (7.0 * (s0 + s1) - s2),
                through(c[2], *own),
                c[3] * (7.0 * (s2 + s3) - s1),
                c[4] * (7.0 * s3 - s2),
            ]
            for r in range(nrows):
                east = flux[r, pl.ds(SUB * (b + 1), SUB), :] - flux[r, pl.ds(SUB * (b + 1) - 1, SUB), :]
                old = q_late[nrows * p + r, here, :]
                rows[r].append(0.5 * ((old + own[r]) - (east + (north[r + 1] - north[r]))))
        put_rows(part, p, rows, nrows)
        return 0

    lax.fori_loop(0, pairs, one, 0)
    lax.fori_loop(0, later, another, 0)
    for i, tile in enumerate((cn[0], cn[2], below[...], cn[3])):
        winds[i] = 0.5 * jnp.transpose(tile)[: LANES // 2]
    for p in range(pairs):
        copy(p).wait()
    heat_copy.wait()


def second_stage_late(pairs, done, nrows, part, winds, ra, rb, before, out, buffer, sems):
    del before
    where = sources()
    levels = LANES // 2

    def copy(p):
        return pltpu.make_async_copy(
            buffer.at[pl.ds(2 * p, 2)], out.at[pl.ds(2 * (done + p), 2)], sems.at[p]
        )

    for p in range(pairs):
        for h in range(2):
            for b in range(levels // SUB):
                here = pl.ds(SUB * b, SUB)

                def halo(k):
                    return partners(where, ra, rb, pl.ds((2 * p + k) * LANES + levels * h + SUB * b, SUB))

                (south_two, north_one), (south_one, north_two) = halo(0), halo(1)
                low = winds[0, here, :] * south_one
                high = winds[1, here, :] * north_one
                bottom = winds[2, here, :] * (7.0 * south_one - south_two)
                top = winds[3, here, :] * (7.0 * north_one - north_two)
                for r, more in enumerate((low + bottom, -low, high, -(top + high))):
                    rows = pl.ds(nrows * SUB * b + r, SUB, stride=nrows)
                    buffer[2 * p + h, rows, :] = part[2 * p + h, rows, :] + more
        copy(p).start()
    for p in range(pairs):
        copy(p).wait()


def radiation(
    nat, cosz_in, albedo_in, ext_in, single_in, weight_in, order_in, count_in, after, heat,
    water, depth, save_c, save_d, save_t, save_g, cosz, albedo, ext, single, weight, order, count, sems
):
    del after
    copies = []
    for i, (src, dst) in enumerate(
        (
            (cosz_in, cosz), (albedo_in, albedo), (ext_in, ext), (single_in, single),
            (weight_in, weight), (order_in, order), (count_in, count),
        )
    ):
        copies.append(pltpu.make_async_copy(src, dst, sems.at[i]))
        copies[-1].start()
    nrows, _ = cosz.shape
    levels = nat.shape[1] // nrows
    pairs = ext.shape[0] // 2
    x = nat[1]
    heat[...] = jnp.maximum(x, 0.0) + jnp.log1p(jnp.exp(-jnp.abs(x)))
    total = jnp.zeros((nrows, LANES), jnp.float32)
    depth[0] = jnp.zeros((2 * nrows, LANES), jnp.float32)
    for l in range(levels):
        w = heat[pl.ds(nrows * l, nrows), :]
        total = total + w
        water[l, pl.ds(0, nrows), :] = w
        water[l, pl.ds(nrows, nrows), :] = w
        depth[l + 1, pl.ds(0, nrows), :] = total
        depth[l + 1, pl.ds(nrows, nrows), :] = total
    for copy in copies:
        copy.wait()

    mu = jnp.concatenate([cosz[...], cosz[...]], axis=0)
    floor_albedo = jnp.concatenate([albedo[...], albedo[...]], axis=0)
    first = lax.broadcasted_iota(jnp.int32, (2 * nrows, LANES), 0) < nrows

    def by_band(ref):
        return [jnp.where(first, ref[2 * p], ref[2 * p + 1]) for p in range(pairs)]

    scale = 4.0 / levels
    inv_mu = 1.0 / mu
    ext_of, single_of, weight_of = by_band(ext), by_band(single), by_band(weight)
    beam = [-(e * scale * LOG2E) * inv_mu for e in ext_of]
    diffuse = [-(1.66 * scale * LOG2E) * e for e in ext_of]
    half = [0.5 * s for s in single_of]
    strength = [weight_of[p] * mu * (1.0 - single_of[p]) for p in range(pairs)]

    def up(step, carry):
        l = levels - 1 - step
        a_all, b_all, s_all = carry
        w = water[l]
        above = depth[l]
        new_a, new_b, new_s = [], [], []
        known = jnp.zeros((2 * nrows, LANES), jnp.float32)
        for p in range(pairs):
            a, b, s_bot = a_all[p], b_all[p], s_all[p]
            decay = jnp.exp2(diffuse[p] * w)
            s_top = strength[p] * jnp.exp2(beam[p] * above)
            lost = 1.0 - decay
            reflect = half[p] * lost
            transmit = decay + reflect
            taken = s_top - s_bot
            source = half[p] * taken
            den = 1.0 - reflect * a
            inv = pl.reciprocal(den, approx=True)
            inv = inv * (2.0 - den * inv)
            t = transmit * inv
            ta = t * a
            g = (reflect * b + source) * inv
            save_t[l, p] = t
            save_g[l, p] = g
            save_d[l, p] = lost + lost * ta
            known = known + (lost * (a * g + b) + taken)
            new_a.append(reflect + transmit * ta)
            new_b.append(t * (a * source + b) + source)
            new_s.append(s_top)
        save_c[l] = known
        return tuple(new_a), tuple(new_b), tuple(new_s)

    s_floor = [strength[p] * jnp.exp2(beam[p] * depth[levels]) for p in range(pairs)]
    a_floor = [floor_albedo for _ in range(pairs)]
    b_floor = [floor_albedo * s_floor[p] for p in range(pairs)]
    lax.fori_loop(0, levels, up, (tuple(a_floor), tuple(b_floor), tuple(s_floor)))

    sunlit = []
    column = lax.broadcasted_iota(jnp.int32, (LANES, LANES), 1)
    rank = lax.broadcasted_iota(jnp.int32, (LANES, LANES), 0)
    for r in range(nrows):
        place = jnp.transpose(jnp.broadcast_to(order[r], (LANES, LANES)))
        hit = (place == column) & (rank < count[r])
        sunlit.append(jnp.max(jnp.where(hit, 1.0, 0.0), axis=0, keepdims=True))
    gain = float(levels) * jnp.concatenate(sunlit, axis=0)

    def down(l, d_all):
        absorbed = save_c[l]
        for p in range(pairs):
            absorbed = absorbed + save_d[l, p] * d_all[p]
        both = absorbed[:nrows] + absorbed[nrows:]
        heat[pl.ds(pl.multiple_of(nrows * l, nrows), nrows), :] = gain * both
        return tuple(save_t[l, p] * d_all[p] + save_g[l, p] for p in range(pairs))

    d_top = tuple(jnp.zeros((2 * nrows, LANES), jnp.float32) for _ in range(pairs))
    lax.fori_loop(0, levels, down, d_top, unroll=4)


def in_hbm(x):
    return pltpu.with_memory_space_constraint(x, pltpu.HBM)


def call(kernel, name, out_shape, specs, out_specs, args, scratches, moved=1000, limit=24, **kw):
    return pl.pallas_call(
        kernel,
        out_shape=out_shape,
        in_specs=specs,
        out_specs=out_specs,
        scratch_shapes=scratches,
        compiler_params=pltpu.CompilerParams(vmem_limit_bytes=limit * MIB),
        name=name,
        cost_estimate=pl.CostEstimate(flops=moved, bytes_accessed=moved, transcendentals=0),
        **kw,
    )(*args)


def per_device(
    fields, courant, cos_zenith, albedo, extinction, single_albedo, band_weight, sun_order, sun_count
):
    nfields, levels, nrows, ncols = fields.shape
    flat = fields.reshape(nfields, levels * nrows, ncols)
    wind = courant.reshape(2, levels * nrows, ncols)
    npairs = nfields // 2
    early, late = SPLIT, npairs - SPLIT

    z0 = shape(2 * early * ncols + ncols // 2, LANES)
    tiles0, za, zb, nat, nat_late, nat_wind = call(
        functools.partial(pack_first, early, nrows),
        "pack_first",
        (
            shape(nrows * early, ncols, LANES), z0, z0,
            shape(2 * early, levels * nrows, ncols), shape(2 * late, levels * nrows, ncols),
            shape(2, levels * nrows, ncols),
        ),
        [HBM, HBM],
        (VMEM,) * 6,
        (in_hbm(flat), in_hbm(wind)),
        [pltpu.SemaphoreType.DMA((early + 3,))],
    )
    lat0 = lat_swaps(za, zb)
    ntiles = nrows * npairs
    winds = shape(nrows, ncols, LANES)
    sides = shape(SUB * (ntiles + 2 * nrows), LANES)
    edge = shape(SUB * (ntiles + nrows) // 2, LANES)
    z1 = shape(2 * late * ncols, LANES)
    tiles1, ce, cn, la, lb, za, zb = call(
        functools.partial(pack_middle, late, nrows),
        "pack_middle",
        (shape(nrows * late, ncols, LANES), winds, winds, edge, edge, z1, z1),
        [VMEM] * 3,
        (VMEM,) * 7,
        (nat_late, nat_wind, tiles0),
        [],
    )
    lat1 = lat_swaps(za, zb)
    lon = lon_swaps(la, lb)

    edges = edge_scratch(nrows)
    z0 = shape(2 * early * ncols + SUB * (npairs + 1), LANES)
    section0, za, zb, below, side = call(
        functools.partial(first_stage_early, early, ntiles, nrows),
        "first_stage_early",
        (shape(nrows * early, ncols, LANES), z0, z0, shape(ncols, LANES), sides),
        [VMEM] * 7,
        (VMEM,) * 5,
        (tiles0, ce, cn, *lon, *lat0),
        edges,
        moved=1000_000_000,
    )
    lat2 = lat_swaps(za, zb)
    z1 = shape(2 * late * ncols, LANES)
    section1, za, zb = call(
        functools.partial(first_stage_late, late, early, nrows),
        "first_stage_late",
        (shape(nrows * late, ncols, LANES), z1, z1),
        [VMEM] * 7,
        (VMEM,) * 3,
        (tiles1, ce, cn, side, *lat1, below),
        edges,
        moved=12_000_000,
    )
    lat3 = lat_swaps(za, zb)

    pairs = extinction.shape[0] // 2
    store = scratch(levels, pairs, 2 * nrows, ncols)
    heating = call(
        radiation,
        "radiation",
        shape(levels * nrows, ncols),
        [VMEM] + [HBM] * 7 + [VMEM],
        VMEM,
        (
            nat, in_hbm(cos_zenith), in_hbm(albedo), in_hbm(extinction), in_hbm(single_albedo),
            in_hbm(band_weight), in_hbm(sun_order), in_hbm(sun_count.reshape(nrows)), section1,
        ),
        [
            scratch(levels, 2 * nrows, ncols), scratch(levels + 1, 2 * nrows, ncols),
            scratch(levels, 2 * nrows, ncols), store, store, store,
            scratch(nrows, ncols), scratch(nrows, ncols),
            pltpu.SMEM(extinction.shape, jnp.float32), pltpu.SMEM(extinction.shape, jnp.float32),
            pltpu.SMEM(extinction.shape, jnp.float32), pltpu.VMEM((nrows, 1, ncols), jnp.int32),
            pltpu.SMEM((nrows,), jnp.int32), pltpu.SemaphoreType.DMA((7,)),
        ],
        moved=16_000_000,
    )

    full = shape(nfields, levels * nrows, ncols)
    out, heat_out, part, half_winds = call(
        functools.partial(second_stage_early, early, late, nrows),
        "second_stage_early",
        (full, shape(levels * nrows, ncols), shape(2 * late, levels * nrows, ncols), shape(nrows, levels, ncols)),
        [VMEM] * 11,
        (HBM, HBM, VMEM, VMEM),
        (tiles0, section0, ce, cn, below, *lat2, side, heating, tiles1, section1),
        [
            scratch(2 * early, levels * nrows, ncols),
            pltpu.SemaphoreType.DMA((early + 1,)),
            scratch(SUB * ntiles, LANES),
            *edges,
        ],
    )
    out = call(
        functools.partial(second_stage_late, late, early, nrows),
        "second_stage_late",
        full,
        [VMEM] * 4 + [HBM],
        HBM,
        (part, half_winds, *lat3, out),
        [scratch(2 * late, levels * nrows, ncols), pltpu.SemaphoreType.DMA((late,))],
        input_output_aliases={4: 0},
    )
    return out.reshape(fields.shape), heat_out.reshape(levels, nrows, ncols)


def solution(mesh):
    in_specs = (
        P(None, None, "lat", "lon"),
        P(None, None, "lat", "lon"),
        P("lat", "lon"),
        P("lat", "lon"),
        P(),
        P(),
        P(),
        P("lat", "lon", None),
        P("lat", "lon"),
    )
    out_specs = (P(None, None, "lat", "lon"), P(None, "lat", "lon"))
    return jax.shard_map(
        per_device, mesh=mesh, in_specs=in_specs, out_specs=out_specs, check_vma=False
    )
```

```python
import functools
import math

import jax
import jax.numpy as jnp
from jax import lax
from jax.experimental import pallas as pl
from jax.experimental.pallas import tpu as pltpu
from jax.sharding import PartitionSpec as P

SPLIT = 2
SUB = 8
LANES = 128
LOG2E = math.log2(math.e)
VMEM = pl.BlockSpec(memory_space=pltpu.VMEM)
HBM = pl.BlockSpec(memory_space=pltpu.HBM)
MIB = 1024 * 1024


def scratch(*dims):
    return pltpu.VMEM(dims, jnp.float32)


def shape(*dims):
    return jax.ShapeDtypeStruct(dims, jnp.float32)


def lon_swaps(first_block, second_block):
    n = lax.axis_size("lon")
    first = [(i, i ^ 1) for i in range(n)]
    second = [(i, (i + 1 if i % 2 else i - 1) % n) for i in range(n)]
    return lax.ppermute(first_block, "lon", first), lax.ppermute(second_block, "lon", second)


def lat_swaps(first_block, second_block):
    nlon, nlat = lax.axis_size("lon"), lax.axis_size("lat")
    second = []
    for i in range(nlon):
        for j in range(nlat):
            k = j + 1 if j % 2 else j - 1
            to = i * nlat + k if 0 <= k < nlat else (i ^ 1) * nlat + j
            second.append((i * nlat + j, to))
    got = lax.ppermute(second_block, ("lon", "lat"), second)
    return lax.ppermute(first_block, "lat", [(j, j ^ 1) for j in range(nlat)]), got


def is_even(axis):
    return lax.rem(lax.axis_index(axis), 2) == 0


def sublanes():
    return lax.broadcasted_iota(jnp.int32, (SUB, LANES), 0)


def lanes():
    return lax.broadcasted_iota(jnp.int32, (SUB, LANES), 1)


def half_turn(block):
    return pltpu.roll(block, SUB // 2, 0)


def native(ref, index, r, nrows):
    levels = ref.shape[1] // nrows
    return ref[index, pl.ds(r, levels, stride=nrows), :]


def tile_of(low, high):
    return jnp.transpose(jnp.concatenate([low, high], axis=0))


def put_lat_sends(even, tiles, pair, nrows, za, zb):
    north = jnp.where(even, 2, 0)
    for k in range(2):
        span = pl.ds(pl.multiple_of((2 * pair + k) * LANES, LANES), LANES)
        za[span, :] = tiles[nrows * pair + north + k]
        zb[span, :] = tiles[nrows * pair + (2 - north) + k]


def take_sides(tile):
    head = sublanes() < SUB // 2
    return jnp.where(head, tile[pl.ds(0, SUB), :], tile[pl.ds(LANES - SUB, SUB), :])


def pack_first(pairs, nrows, fields, courant, tiles, za, zb, nat, nat_late, nat_wind, sems):
    n = 2 * pairs
    first = [
        pltpu.make_async_copy(fields.at[pl.ds(2 * p, 2)], nat.at[pl.ds(2 * p, 2)], sems.at[p]) for p in range(pairs)
    ]
    north = pltpu.make_async_copy(courant.at[pl.ds(1, 1)], nat_wind.at[pl.ds(1, 1)], sems.at[pairs])
    late = pltpu.make_async_copy(fields.at[pl.ds(n, nat_late.shape[0])], nat_late, sems.at[pairs + 1])
    east = pltpu.make_async_copy(courant.at[pl.ds(0, 1)], nat_wind.at[pl.ds(0, 1)], sems.at[pairs + 2])
    for copy in first + [north, late, east]:
        copy.start()
    half = LANES // 2
    even = is_even("lat")

    def body(p, up, down):
        for r in range(nrows):
            tile = tile_of(native(nat, 2 * p, r, nrows), native(nat, 2 * p + 1, r, nrows))
            tiles[nrows * p + r] = tile
            (up if r >= 2 else down)[pl.ds((2 * p + r % 2) * LANES, LANES), :] = tile
        if p < pairs - 1:
            return
        lane = lax.broadcasted_iota(jnp.int32, (half, LANES), 1)
        top = native(nat_wind, 1, nrows - 1, nrows) * (1.0 / 12.0)
        top = tile_of(top, top)
        top = jnp.where(lane < half, top[:half], top[half:])
        for ref in (up, down):
            ref[pl.ds(2 * pairs * LANES, half), :] = top

    for p in range(pairs):
        first[p].wait()
        if p == pairs - 1:
            north.wait()
        pl.when(even)(functools.partial(body, p, za, zb))
        pl.when(jnp.logical_not(even))(functools.partial(body, p, zb, za))
    late.wait()
    east.wait()


def pack_middle(pairs, nrows, nat, nat_wind, tiles_first, tiles, ce, cn, la, lb, za, zb):
    up = jnp.where(is_even("lat"), 2, 0)
    for p in range(pairs):
        for r in range(nrows):
            tiles[nrows * p + r] = tile_of(native(nat, 2 * p, r, nrows), native(nat, 2 * p + 1, r, nrows))
    for r in range(nrows):
        east = native(nat_wind, 0, r, nrows) * (1.0 / 12.0)
        north = native(nat_wind, 1, r, nrows) * (1.0 / 12.0)
        ce[r] = tile_of(east, east)
        cn[r] = tile_of(north, north)
    for i in range(2 * pairs):
        p, k = divmod(i, 2)
        span = pl.ds(i * LANES, LANES)
        za[span, :] = tiles[nrows * p + up + k]
        zb[span, :] = tiles[nrows * p + (2 - up) + k]
    even = is_even("lon")
    head, low = sublanes() < SUB // 2, lanes() < LANES // 2
    blocks = [take_sides(ref.at[t]) for ref in (tiles_first, tiles) for t in range(ref.shape[0])]
    blocks += [jnp.where(low, take_sides(ce.at[r]), take_sides(cn.at[r])) for r in range(nrows)]
    for i in range(0, len(blocks), 2):
        one, two = blocks[i : i + 2]
        east = jnp.where(head, half_turn(one), two)
        west = jnp.where(head, one, half_turn(two))
        span = pl.ds(SUB * (i // 2), SUB)
        la[span, :] = jnp.where(even, east, west)
        lb[span, :] = jnp.where(even, west, east)


def put_side(la, lb, ntiles, side):
    lon_even = is_even("lon")
    head, low = sublanes() < SUB // 2, lanes() < LANES // 2
    blocks = []
    for i in range(la.shape[0] // SUB):
        span = pl.ds(SUB * i, SUB)
        a, b = la[span, :], lb[span, :]
        east, west = jnp.where(lon_even, a, b), jnp.where(lon_even, b, a)
        blocks += [jnp.where(head, east, half_turn(west)), jnp.where(head, half_turn(east), west)]
    winds = blocks[ntiles:]
    turned = [pltpu.roll(wind, LANES // 2, 1) for wind in winds]
    blocks[ntiles:] = [jnp.where(low, x, y) for x, y in zip(winds, turned)]
    blocks += [jnp.where(low, y, x) for x, y in zip(winds, turned)]
    for t, value in enumerate(blocks):
        side[pl.ds(SUB * t, SUB), :] = value


def put_corners(lat_even, ntiles, nrows, at, side, za, zb):
    row = sublanes()
    outer = (row < 2) | (row >= SUB - 2)
    north = jnp.where(lat_even, 2, 0)

    def corner(p, first):
        start = pl.multiple_of(SUB * (nrows * p + first), SUB)
        one, two = side[pl.ds(start, SUB), :], side[pl.ds(start + SUB, SUB), :]
        return jnp.where(outer, one, half_turn(two))

    npairs = ntiles // nrows
    for p in range(npairs):
        to = pl.ds(at + SUB * p, SUB)
        za[to, :] = corner(p, north)
        zb[to, :] = corner(p, 2 - north)
    to = pl.ds(at + SUB * npairs, SUB)
    top = side[pl.ds(SUB * (ntiles + 2 * nrows - 1), SUB), :]
    za[to, :] = top
    zb[to, :] = top


def put_edges(q, first, side, at, nrows, edge_w, edge_e):
    for r in range(nrows):
        beside = side[pl.ds(pl.multiple_of(SUB * (at + r), SUB), SUB), :]
        edge_w[r, pl.ds(SUB, SUB), :] = beside
        edge_w[r, pl.ds(2 * SUB, SUB), :] = q[first + r, pl.ds(0, SUB), :]
        edge_e[r, pl.ds(0, SUB), :] = q[first + r, pl.ds(LANES - SUB, SUB), :]
        edge_e[r, pl.ds(SUB, SUB), :] = beside


def through(c, before, left, right, after):
    return c * (7.0 * (left + right) - (before + after))


def put_fluxes(q, first, nrows, ce, edge_w, edge_e, edge_c, flux):
    for r in range(nrows):
        window = [edge_w[r, pl.ds(SUB + k, SUB), :] for k in range(4)]
        flux[r, pl.ds(1, SUB), :] = through(edge_c[r, pl.ds(SUB + 1, SUB), :], *window)
        for b in range(LANES // SUB):
            at = SUB * b

            def load(shift):
                if at + shift < 0:
                    return edge_w[r, pl.ds(2 * SUB + shift, SUB), :]
                if at + shift + SUB > LANES:
                    return edge_e[r, pl.ds(shift, SUB), :]
                return q[first + r, pl.ds(at + shift, SUB), :]

            flux[r, pl.ds(SUB + at, SUB), :] = through(
                ce[r, pl.ds(at, SUB), :], load(-1), load(0), load(1), load(2)
            )


def lat_divergence(rows, winds):
    north = [through(winds[r], *rows[r : r + 4]) for r in range(len(winds))]
    return [north[r + 1] - north[r] for r in range(len(winds) - 1)]


def sources():
    at, n = lax.axis_index("lat"), lax.axis_size("lat")
    even = lax.rem(at, 2) == 0
    return (even, jnp.logical_not(even), jnp.logical_and(even, at > 0), jnp.logical_and(jnp.logical_not(even), at < n - 1))


def partners(where, ra, rb, span):
    north_a, south_a, south_b, north_b = where
    a, b = ra[span, :], rb[span, :]
    south = jnp.where(south_a, a, jnp.where(south_b, b, 0.0))
    return south, jnp.where(north_a, a, jnp.where(north_b, b, 0.0))


def divergence(q, pair, nrows, b, halo, cn, below, flux):
    at = SUB * b
    here = pl.ds(at, SUB)
    (s0, n0), (s1, n1) = halo(0, at), halo(1, at)
    own = [q[nrows * pair + r, here, :] for r in range(nrows)]
    winds = [below[here, :]] + [cn[r, here, :] for r in range(nrows)]
    north = lat_divergence([s0, s1] + own + [n0, n1], winds)
    div = []
    for r in range(nrows):
        east = flux[r, pl.ds(SUB + at, SUB), :] - flux[r, pl.ds(SUB + at - 1, SUB), :]
        div.append(east + north[r])
    return own, div


def put_side_section(at, nrows, where, ra, rb, corner, side, ntiles, edge_w, edge_e, edge_c, edge_d, out):
    head = sublanes() < SUB // 2

    def shifted(w, e, r, k):
        return jnp.where(head, e[r, pl.ds(SUB + k, SUB), :], w[r, pl.ds(SUB + k, SUB), :])

    def beside(t):
        return side[pl.ds(pl.multiple_of(SUB * t, SUB), SUB), :]

    start = pl.multiple_of(corner + SUB * (at // nrows), SUB)
    south, above = partners(where, ra, rb, pl.ds(start, SUB))
    s0, s1 = south, half_turn(south)
    n0, n1 = above, half_turn(above)
    own = [beside(at + r) for r in range(nrows)]
    last = pl.ds(corner + SUB * (ntiles // nrows), SUB)
    winds = [partners(where, ra, rb, last)[0]]
    winds += [beside(ntiles + nrows + r) for r in range(nrows)]
    north = lat_divergence([s0, s1] + own + [n0, n1], winds)
    for r in range(nrows):
        v = [shifted(edge_w, edge_e, r, k) for k in range(-2, 3)]
        east = through(beside(ntiles + r), *v[1:])
        west = through(shifted(edge_c, edge_d, r, -1), *v[:-1])
        new = own[r] - ((east - west) + north[r])
        out[pl.ds(pl.multiple_of(SUB * (at + r), SUB), SUB), :] = new


def edge_scratch(nrows):
    return [scratch(nrows, 3 * SUB, LANES)] * 4 + [scratch(nrows, LANES + SUB, LANES)]


def first_stage_early(pairs, ntiles, nrows, q, ce, cn, la, lb, ra, rb, section, za, zb, below, side, *edges):
    edge_w, edge_e, edge_c, edge_d, flux = edges
    lat_even, where = is_even("lat"), sources()
    half = LANES // 2
    a = partners(where, ra, rb, pl.ds(2 * pairs * LANES, half))[0]
    turned = pltpu.roll(a, half, 1)
    low = lax.broadcasted_iota(jnp.int32, (half, LANES), 1) < half
    below[pl.ds(0, half), :] = jnp.where(low, a, turned)
    below[pl.ds(half, half), :] = jnp.where(low, turned, a)
    put_side(la, lb, ntiles, side)
    put_corners(lat_even, ntiles, nrows, 2 * pairs * LANES, side, za, zb)
    put_edges(ce, 0, side, side.shape[0] // SUB - 2 * nrows, nrows, edge_c, edge_d)

    def one(p, _):
        def halo(k, shift):
            start = pl.multiple_of((2 * p + k) * LANES, LANES)
            return partners(where, ra, rb, pl.ds(start + shift, SUB))

        put_edges(q, nrows * p, side, nrows * p, nrows, edge_w, edge_e)
        put_fluxes(q, nrows * p, nrows, ce, edge_w, edge_e, edge_c, flux)
        for b in range(LANES // SUB):
            own, div = divergence(q, p, nrows, b, halo, cn, below, flux)
            for r in range(nrows):
                section[nrows * p + r, pl.ds(SUB * b, SUB), :] = own[r] - div[r]
        put_lat_sends(lat_even, section, p, nrows, za, zb)
        return 0

    lax.fori_loop(0, pairs, one, 0)


def first_stage_late(
    pairs, done, nrows, q, ce, cn, side, ra, rb, below, section, za, zb, *edges
):
    edge_w, edge_e, edge_c, edge_d, flux = edges
    lat_even, where = is_even("lat"), sources()
    put_edges(ce, 0, side, side.shape[0] // SUB - 2 * nrows, nrows, edge_c, edge_d)
    for p in range(pairs):

        def halo(k, shift):
            return partners(where, ra, rb, pl.ds((2 * p + k) * LANES + shift, SUB))

        put_edges(q, nrows * p, side, nrows * (done + p), nrows, edge_w, edge_e)
        put_fluxes(q, nrows * p, nrows, ce, edge_w, edge_e, edge_c, flux)
        for b in range(LANES // SUB):
            own, div = divergence(q, p, nrows, b, halo, cn, below, flux)
            for r in range(nrows):
                section[nrows * p + r, pl.ds(SUB * b, SUB), :] = own[r] - div[r]
        up = jnp.where(lat_even, 2, 0)
        for k in range(2):
            span = pl.ds((2 * p + k) * LANES, LANES)
            za[span, :] = jnp.transpose(section[nrows * p + up + k])
            zb[span, :] = jnp.transpose(section[nrows * p + (2 - up) + k])


def put_rows(buffer, pair, rows, nrows):
    levels = LANES // 2
    for r in range(nrows):
        turned = jnp.transpose(jnp.concatenate(rows[r], axis=0))
        for h in range(2):
            buffer[2 * pair + h, pl.ds(r, levels, stride=nrows), :] = turned[levels * h : levels * (h + 1)]


def second_stage_early(
    pairs, later, nrows, q, s, ce, cn, below, ra, rb, side, heating, q_late, s_late,
    out, heat_out, part, winds, buffer, sems, sides, *edges
):
    edge_w, edge_e, edge_c, edge_d, flux = edges
    where = sources()
    heat_copy = pltpu.make_async_copy(heating, heat_out, sems.at[pairs])
    heat_copy.start()
    put_edges(ce, 0, side, side.shape[0] // SUB - 2 * nrows, nrows, edge_c, edge_d)

    ntiles = nrows * (pairs + later)
    for ref, first, n in ((q, 0, pairs), (q_late, pairs, later)):

        def beside(p, _):
            at = nrows * (first + p)
            put_edges(ref, nrows * p, side, at, nrows, edge_w, edge_e)
            put_side_section(
                at, nrows, where, ra, rb, 2 * pairs * LANES, side, ntiles, edge_w, edge_e, edge_c, edge_d, sides
            )
            return 0

        lax.fori_loop(0, n, beside, 0)

    def copy(p):
        return pltpu.make_async_copy(buffer.at[pl.ds(2 * p, 2)], out.at[pl.ds(2 * p, 2)], sems.at[p])

    def one(p, _):
        def halo(k, shift):
            start = pl.multiple_of((2 * p + k) * LANES, LANES)
            return partners(where, ra, rb, pl.ds(start + shift, SUB))

        put_edges(s, nrows * p, sides, nrows * p, nrows, edge_w, edge_e)
        put_fluxes(s, nrows * p, nrows, ce, edge_w, edge_e, edge_c, flux)
        parts = [[] for _ in range(nrows)]
        for b in range(LANES // SUB):
            own, div = divergence(s, p, nrows, b, halo, cn, below, flux)
            for r in range(nrows):
                old = q[nrows * p + r, pl.ds(SUB * b, SUB), :]
                parts[r].append(0.5 * ((old + own[r]) - div[r]))
        put_rows(buffer, p, parts, nrows)

        @pl.when(p == 0)
        def _():
            buffer[0] = buffer[0] + 0.5 * heating[...]

        copy(p).start()
        return 0

    def another(p, _):
        put_edges(s_late, nrows * p, sides, nrows * (pairs + p), nrows, edge_w, edge_e)
        put_fluxes(s_late, nrows * p, nrows, ce, edge_w, edge_e, edge_c, flux)
        rows = [[] for _ in range(nrows)]
        for b in range(LANES // SUB):
            here = pl.ds(SUB * b, SUB)
            s0, s1, s2, s3 = own = [s_late[nrows * p + r, here, :] for r in range(nrows)]
            c = [below[here, :]] + [cn[r, here, :] for r in range(nrows)]
            north = [
                c[0] * (7.0 * s0 - s1),
                c[1] * (7.0 * (s0 + s1) - s2),
                through(c[2], *own),
                c[3] * (7.0 * (s2 + s3) - s1),
                c[4] * (7.0 * s3 - s2),
            ]
            for r in range(nrows):
                east = flux[r, pl.ds(SUB * (b + 1), SUB), :] - flux[r, pl.ds(SUB * (b + 1) - 1, SUB), :]
                old = q_late[nrows * p + r, here, :]
                rows[r].append(0.5 * ((old + own[r]) - (east + (north[r + 1] - north[r]))))
        put_rows(part, p, rows, nrows)
        return 0

    lax.fori_loop(0, pairs, one, 0)
    lax.fori_loop(0, later, another, 0)
    for i, tile in enumerate((cn[0], cn[2], below[...], cn[3])):
        winds[i] = 0.5 * jnp.transpose(tile)[: LANES // 2]
    for p in range(pairs):
        copy(p).wait()
    heat_copy.wait()


def second_stage_late(pairs, done, nrows, part, winds, ra, rb, before, out, buffer, sems):
    del before
    levels = LANES // 2

    def copy(p):
        return pltpu.make_async_copy(
            buffer.at[pl.ds(2 * p, 2)], out.at[pl.ds(2 * (done + p), 2)], sems.at[p]
        )

    def finish(south, north):
        for p in range(pairs):
            for h in range(2):
                for b in range(levels // SUB):
                    here = pl.ds(SUB * b, SUB)
                    one, two = (pl.ds((2 * p + k) * LANES + levels * h + SUB * b, SUB) for k in range(2))
                    more = [None] * nrows
                    if south is not None:
                        low = winds[0, here, :] * south[two, :]
                        more[0] = low + winds[2, here, :] * (7.0 * south[two, :] - south[one, :])
                        more[1] = -low
                    if north is not None:
                        high = winds[1, here, :] * north[one, :]
                        more[2] = high
                        more[3] = -(winds[3, here, :] * (7.0 * north[one, :] - north[two, :]) + high)
                    for r in range(nrows):
                        rows = pl.ds(nrows * SUB * b + r, SUB, stride=nrows)
                        value = part[2 * p + h, rows, :]
                        buffer[2 * p + h, rows, :] = value if more[r] is None else value + more[r]
            copy(p).start()
        for p in range(pairs):
            copy(p).wait()

    at, n = lax.axis_index("lat"), lax.axis_size("lat")
    even, inner = is_even("lat"), jnp.logical_and(at > 0, at < n - 1)
    pl.when(at == 0)(lambda: finish(None, ra))
    pl.when(at == n - 1)(lambda: finish(ra, None))
    pl.when(jnp.logical_and(inner, even))(lambda: finish(rb, ra))
    pl.when(jnp.logical_and(inner, jnp.logical_not(even)))(lambda: finish(ra, rb))


def radiation(
    nat, cosz_in, albedo_in, ext_in, single_in, weight_in, order_in, count_in, after, heat,
    water, depth, save_c, save_d, save_t, save_g, cosz, albedo, ext, single, weight, order, count, sems
):
    del after
    copies = []
    for i, (src, dst) in enumerate(
        (
            (cosz_in, cosz), (albedo_in, albedo), (ext_in, ext), (single_in, single),
            (weight_in, weight), (order_in, order), (count_in, count),
        )
    ):
        copies.append(pltpu.make_async_copy(src, dst, sems.at[i]))
        copies[-1].start()
    nrows, _ = cosz.shape
    levels = nat.shape[1] // nrows
    pairs = ext.shape[0] // 2
    x = nat[1]
    heat[...] = jnp.maximum(x, 0.0) + jnp.log1p(jnp.exp(-jnp.abs(x)))
    total = jnp.zeros((nrows, LANES), jnp.float32)
    depth[0] = jnp.zeros((2 * nrows, LANES), jnp.float32)
    for l in range(levels):
        w = heat[pl.ds(nrows * l, nrows), :]
        total = total + w
        water[l, pl.ds(0, nrows), :] = w
        water[l, pl.ds(nrows, nrows), :] = w
        depth[l + 1, pl.ds(0, nrows), :] = total
        depth[l + 1, pl.ds(nrows, nrows), :] = total
    for copy in copies:
        copy.wait()

    mu = jnp.concatenate([cosz[...], cosz[...]], axis=0)
    floor_albedo = jnp.concatenate([albedo[...], albedo[...]], axis=0)
    first = lax.broadcasted_iota(jnp.int32, (2 * nrows, LANES), 0) < nrows

    def by_band(ref):
        return [jnp.where(first, ref[2 * p], ref[2 * p + 1]) for p in range(pairs)]

    scale = 4.0 / levels
    inv_mu = 1.0 / mu
    ext_of, single_of, weight_of = by_band(ext), by_band(single), by_band(weight)
    beam = [-(e * scale * LOG2E) * inv_mu for e in ext_of]
    diffuse = [-(1.66 * scale * LOG2E) * e for e in ext_of]
    half = [0.5 * s for s in single_of]
    strength = [weight_of[p] * mu * (1.0 - single_of[p]) for p in range(pairs)]

    def up(step, carry):
        l = levels - 1 - step
        a_all, b_all, s_all = carry
        w = water[l]
        above = depth[l]
        new_a, new_b, new_s = [], [], []
        known = jnp.zeros((2 * nrows, LANES), jnp.float32)
        for p in range(pairs):
            a, b, s_bot = a_all[p], b_all[p], s_all[p]
            decay = jnp.exp2(diffuse[p] * w)
            s_top = strength[p] * jnp.exp2(beam[p] * above)
            lost = 1.0 - decay
            reflect = half[p] * lost
            transmit = decay + reflect
            taken = s_top - s_bot
            source = half[p] * taken
            den = 1.0 - reflect * a
            inv = pl.reciprocal(den, approx=True)
            inv = inv * (2.0 - den * inv)
            t = transmit * inv
            ta = t * a
            g = (reflect * b + source) * inv
            save_t[l, p] = t
            save_g[l, p] = g
            save_d[l, p] = lost + lost * ta
            known = known + (lost * (a * g + b) + taken)
            new_a.append(reflect + transmit * ta)
            new_b.append(t * (a * source + b) + source)
            new_s.append(s_top)
        save_c[l] = known
        return tuple(new_a), tuple(new_b), tuple(new_s)

    s_floor = [strength[p] * jnp.exp2(beam[p] * depth[levels]) for p in range(pairs)]
    a_floor = [floor_albedo for _ in range(pairs)]
    b_floor = [floor_albedo * s_floor[p] for p in range(pairs)]
    lax.fori_loop(0, levels, up, (tuple(a_floor), tuple(b_floor), tuple(s_floor)))

    sunlit = []
    column = lax.broadcasted_iota(jnp.int32, (LANES, LANES), 1)
    rank = lax.broadcasted_iota(jnp.int32, (LANES, LANES), 0)
    for r in range(nrows):
        place = jnp.transpose(jnp.broadcast_to(order[r], (LANES, LANES)))
        hit = (place == column) & (rank < count[r])
        sunlit.append(jnp.max(jnp.where(hit, 1.0, 0.0), axis=0, keepdims=True))
    gain = float(levels) * jnp.concatenate(sunlit, axis=0)

    def down(l, d_all):
        absorbed = save_c[l]
        for p in range(pairs):
            absorbed = absorbed + save_d[l, p] * d_all[p]
        both = absorbed[:nrows] + absorbed[nrows:]
        heat[pl.ds(pl.multiple_of(nrows * l, nrows), nrows), :] = gain * both
        return tuple(save_t[l, p] * d_all[p] + save_g[l, p] for p in range(pairs))

    d_top = tuple(jnp.zeros((2 * nrows, LANES), jnp.float32) for _ in range(pairs))
    lax.fori_loop(0, levels, down, d_top, unroll=4)


def in_hbm(x):
    return pltpu.with_memory_space_constraint(x, pltpu.HBM)


def call(kernel, name, out_shape, specs, out_specs, args, scratches, moved=1000, limit=24, **kw):
    return pl.pallas_call(
        kernel,
        out_shape=out_shape,
        in_specs=specs,
        out_specs=out_specs,
        scratch_shapes=scratches,
        compiler_params=pltpu.CompilerParams(vmem_limit_bytes=limit * MIB),
        name=name,
        cost_estimate=pl.CostEstimate(flops=moved, bytes_accessed=moved, transcendentals=0),
        **kw,
    )(*args)


def per_device(
    fields, courant, cos_zenith, albedo, extinction, single_albedo, band_weight, sun_order, sun_count
):
    nfields, levels, nrows, ncols = fields.shape
    flat = fields.reshape(nfields, levels * nrows, ncols)
    wind = courant.reshape(2, levels * nrows, ncols)
    npairs = nfields // 2
    early, late = SPLIT, npairs - SPLIT

    z0 = shape(2 * early * ncols + ncols // 2, LANES)
    tiles0, za, zb, nat, nat_late, nat_wind = call(
        functools.partial(pack_first, early, nrows),
        "pack_first",
        (
            shape(nrows * early, ncols, LANES), z0, z0,
            shape(2 * early, levels * nrows, ncols), shape(2 * late, levels * nrows, ncols),
            shape(2, levels * nrows, ncols),
        ),
        [HBM, HBM],
        (VMEM,) * 6,
        (in_hbm(flat), in_hbm(wind)),
        [pltpu.SemaphoreType.DMA((early + 3,))],
    )
    lat0 = lat_swaps(za, zb)
    ntiles = nrows * npairs
    winds = shape(nrows, ncols, LANES)
    sides = shape(SUB * (ntiles + 2 * nrows), LANES)
    edge = shape(SUB * (ntiles + nrows) // 2, LANES)
    z1 = shape(2 * late * ncols, LANES)
    tiles1, ce, cn, la, lb, za, zb = call(
        functools.partial(pack_middle, late, nrows),
        "pack_middle",
        (shape(nrows * late, ncols, LANES), winds, winds, edge, edge, z1, z1),
        [VMEM] * 3,
        (VMEM,) * 7,
        (nat_late, nat_wind, tiles0),
        [],
    )
    lat1 = lat_swaps(za, zb)
    lon = lon_swaps(la, lb)

    edges = edge_scratch(nrows)
    z0 = shape(2 * early * ncols + SUB * (npairs + 1), LANES)
    section0, za, zb, below, side = call(
        functools.partial(first_stage_early, early, ntiles, nrows),
        "first_stage_early",
        (shape(nrows * early, ncols, LANES), z0, z0, shape(ncols, LANES), sides),
        [VMEM] * 7,
        (VMEM,) * 5,
        (tiles0, ce, cn, *lon, *lat0),
        edges,
        moved=1000_000_000,
    )
    lat2 = lat_swaps(za, zb)
    z1 = shape(2 * late * ncols, LANES)
    section1, za, zb = call(
        functools.partial(first_stage_late, late, early, nrows),
        "first_stage_late",
        (shape(nrows * late, ncols, LANES), z1, z1),
        [VMEM] * 7,
        (VMEM,) * 3,
        (tiles1, ce, cn, side, *lat1, below),
        edges,
        moved=12_000_000,
    )
    lat3 = lat_swaps(za, zb)

    pairs = extinction.shape[0] // 2
    store = scratch(levels, pairs, 2 * nrows, ncols)
    heating = call(
        radiation,
        "radiation",
        shape(levels * nrows, ncols),
        [VMEM] + [HBM] * 7 + [VMEM],
        VMEM,
        (
            nat, in_hbm(cos_zenith), in_hbm(albedo), in_hbm(extinction), in_hbm(single_albedo),
            in_hbm(band_weight), in_hbm(sun_order), in_hbm(sun_count.reshape(nrows)), section1,
        ),
        [
            scratch(levels, 2 * nrows, ncols), scratch(levels + 1, 2 * nrows, ncols),
            scratch(levels, 2 * nrows, ncols), store, store, store,
            scratch(nrows, ncols), scratch(nrows, ncols),
            pltpu.SMEM(extinction.shape, jnp.float32), pltpu.SMEM(extinction.shape, jnp.float32),
            pltpu.SMEM(extinction.shape, jnp.float32), pltpu.VMEM((nrows, 1, ncols), jnp.int32),
            pltpu.SMEM((nrows,), jnp.int32), pltpu.SemaphoreType.DMA((7,)),
        ],
        moved=16_000_000,
    )

    full = shape(nfields, levels * nrows, ncols)
    out, heat_out, part, half_winds = call(
        functools.partial(second_stage_early, early, late, nrows),
        "second_stage_early",
        (full, shape(levels * nrows, ncols), shape(2 * late, levels * nrows, ncols), shape(nrows, levels, ncols)),
        [VMEM] * 11,
        (HBM, HBM, VMEM, VMEM),
        (tiles0, section0, ce, cn, below, *lat2, side, heating, tiles1, section1),
        [
            scratch(2 * early, levels * nrows, ncols),
            pltpu.SemaphoreType.DMA((early + 1,)),
            scratch(SUB * ntiles, LANES),
            *edges,
        ],
    )
    out = call(
        functools.partial(second_stage_late, late, early, nrows),
        "second_stage_late",
        full,
        [VMEM] * 4 + [HBM],
        HBM,
        (part, half_winds, *lat3, out),
        [scratch(2 * late, levels * nrows, ncols), pltpu.SemaphoreType.DMA((late,))],
        input_output_aliases={4: 0},
    )
    return out.reshape(fields.shape), heat_out.reshape(levels, nrows, ncols)


def solution(mesh):
    in_specs = (
        P(None, None, "lat", "lon"),
        P(None, None, "lat", "lon"),
        P("lat", "lon"),
        P("lat", "lon"),
        P(),
        P(),
        P(),
        P("lat", "lon", None),
        P("lat", "lon"),
    )
    out_specs = (P(None, None, "lat", "lon"), P(None, "lat", "lon"))
    return jax.shard_map(
        per_device, mesh=mesh, in_specs=in_specs, out_specs=out_specs, check_vma=False
    )
```

```python
import functools
import math

import jax
import jax.numpy as jnp
from jax import lax
from jax.experimental import pallas as pl
from jax.experimental.pallas import tpu as pltpu
from jax.sharding import PartitionSpec as P

SPLIT = 2
SUB = 8
LANES = 128
LOG2E = math.log2(math.e)
VMEM = pl.BlockSpec(memory_space=pltpu.VMEM)
HBM = pl.BlockSpec(memory_space=pltpu.HBM)
MIB = 1024 * 1024


def scratch(*dims):
    return pltpu.VMEM(dims, jnp.float32)


def shape(*dims):
    return jax.ShapeDtypeStruct(dims, jnp.float32)


def lon_swaps(first_block, second_block):
    n = lax.axis_size("lon")
    first = [(i, i ^ 1) for i in range(n)]
    second = [(i, (i + 1 if i % 2 else i - 1) % n) for i in range(n)]
    return lax.ppermute(first_block, "lon", first), lax.ppermute(second_block, "lon", second)


def lat_swaps(first_block, second_block):
    nlon, nlat = lax.axis_size("lon"), lax.axis_size("lat")
    second = []
    for i in range(nlon):
        for j in range(nlat):
            k = j + 1 if j % 2 else j - 1
            to = i * nlat + k if 0 <= k < nlat else (i ^ 1) * nlat + j
            second.append((i * nlat + j, to))
    got = lax.ppermute(second_block, ("lon", "lat"), second)
    return lax.ppermute(first_block, "lat", [(j, j ^ 1) for j in range(nlat)]), got


def is_even(axis):
    return lax.rem(lax.axis_index(axis), 2) == 0


def sublanes():
    return lax.broadcasted_iota(jnp.int32, (SUB, LANES), 0)


def lanes():
    return lax.broadcasted_iota(jnp.int32, (SUB, LANES), 1)


def half_turn(block):
    return pltpu.roll(block, SUB // 2, 0)


def native(ref, index, r, nrows):
    levels = ref.shape[1] // nrows
    return ref[index, pl.ds(r, levels, stride=nrows), :]


def tile_of(low, high):
    return jnp.transpose(jnp.concatenate([low, high], axis=0))


def put_lat_sends(even, tiles, pair, nrows, za, zb):
    north = jnp.where(even, 2, 0)
    for k in range(2):
        span = pl.ds(pl.multiple_of((2 * pair + k) * LANES, LANES), LANES)
        za[span, :] = tiles[nrows * pair + north + k]
        zb[span, :] = tiles[nrows * pair + (2 - north) + k]


def take_sides(tile):
    head = sublanes() < SUB // 2
    return jnp.where(head, tile[pl.ds(0, SUB), :], tile[pl.ds(LANES - SUB, SUB), :])


def pack_first(pairs, nrows, fields, courant, tiles, za, zb, nat, nat_late, nat_wind, sems):
    n = 2 * pairs
    first = [
        pltpu.make_async_copy(fields.at[pl.ds(2 * p, 2)], nat.at[pl.ds(2 * p, 2)], sems.at[p]) for p in range(pairs)
    ]
    north = pltpu.make_async_copy(courant.at[pl.ds(1, 1)], nat_wind.at[pl.ds(1, 1)], sems.at[pairs])
    late = pltpu.make_async_copy(fields.at[pl.ds(n, nat_late.shape[0])], nat_late, sems.at[pairs + 1])
    east = pltpu.make_async_copy(courant.at[pl.ds(0, 1)], nat_wind.at[pl.ds(0, 1)], sems.at[pairs + 2])
    for copy in first + [north, late, east]:
        copy.start()
    half = LANES // 2
    even = is_even("lat")

    def body(p, up, down):
        for r in range(nrows):
            tile = tile_of(native(nat, 2 * p, r, nrows), native(nat, 2 * p + 1, r, nrows))
            tiles[nrows * p + r] = tile
            (up if r >= 2 else down)[pl.ds((2 * p + r % 2) * LANES, LANES), :] = tile
        if p < pairs - 1:
            return
        lane = lax.broadcasted_iota(jnp.int32, (half, LANES), 1)
        top = native(nat_wind, 1, nrows - 1, nrows) * (1.0 / 12.0)
        top = tile_of(top, top)
        top = jnp.where(lane < half, top[:half], top[half:])
        for ref in (up, down):
            ref[pl.ds(2 * pairs * LANES, half), :] = top

    for p in range(pairs):
        first[p].wait()
        if p == pairs - 1:
            north.wait()
        pl.when(even)(functools.partial(body, p, za, zb))
        pl.when(jnp.logical_not(even))(functools.partial(body, p, zb, za))
    late.wait()
    east.wait()


def pack_middle(pairs, nrows, nat, nat_wind, tiles_first, tiles, ce, cn, la, lb, za, zb):
    up = jnp.where(is_even("lat"), 2, 0)
    for p in range(pairs):
        for r in range(nrows):
            tiles[nrows * p + r] = tile_of(native(nat, 2 * p, r, nrows), native(nat, 2 * p + 1, r, nrows))
    for r in range(nrows):
        east = native(nat_wind, 0, r, nrows) * (1.0 / 12.0)
        north = native(nat_wind, 1, r, nrows) * (1.0 / 12.0)
        ce[r] = tile_of(east, east)
        cn[r] = tile_of(north, north)
    for i in range(2 * pairs):
        p, k = divmod(i, 2)
        span = pl.ds(i * LANES, LANES)
        za[span, :] = tiles[nrows * p + up + k]
        zb[span, :] = tiles[nrows * p + (2 - up) + k]
    even = is_even("lon")
    head, low = sublanes() < SUB // 2, lanes() < LANES // 2
    blocks = [take_sides(ref.at[t]) for ref in (tiles_first, tiles) for t in range(ref.shape[0])]
    blocks += [jnp.where(low, take_sides(ce.at[r]), take_sides(cn.at[r])) for r in range(nrows)]
    for i in range(0, len(blocks), 2):
        one, two = blocks[i : i + 2]
        east = jnp.where(head, half_turn(one), two)
        west = jnp.where(head, one, half_turn(two))
        span = pl.ds(SUB * (i // 2), SUB)
        la[span, :] = jnp.where(even, east, west)
        lb[span, :] = jnp.where(even, west, east)


def put_side(la, lb, ntiles, side):
    lon_even = is_even("lon")
    head, low = sublanes() < SUB // 2, lanes() < LANES // 2
    blocks = []
    for i in range(la.shape[0] // SUB):
        span = pl.ds(SUB * i, SUB)
        a, b = la[span, :], lb[span, :]
        east, west = jnp.where(lon_even, a, b), jnp.where(lon_even, b, a)
        blocks += [jnp.where(head, east, half_turn(west)), jnp.where(head, half_turn(east), west)]
    winds = blocks[ntiles:]
    turned = [pltpu.roll(wind, LANES // 2, 1) for wind in winds]
    blocks[ntiles:] = [jnp.where(low, x, y) for x, y in zip(winds, turned)]
    blocks += [jnp.where(low, y, x) for x, y in zip(winds, turned)]
    for t, value in enumerate(blocks):
        side[pl.ds(SUB * t, SUB), :] = value


def put_corners(lat_even, ntiles, nrows, at, side, za, zb):
    row = sublanes()
    outer = (row < 2) | (row >= SUB - 2)
    north = jnp.where(lat_even, 2, 0)

    def corner(p, first):
        start = pl.multiple_of(SUB * (nrows * p + first), SUB)
        one, two = side[pl.ds(start, SUB), :], side[pl.ds(start + SUB, SUB), :]
        return jnp.where(outer, one, half_turn(two))

    npairs = ntiles // nrows
    for p in range(npairs):
        to = pl.ds(at + SUB * p, SUB)
        za[to, :] = corner(p, north)
        zb[to, :] = corner(p, 2 - north)
    to = pl.ds(at + SUB * npairs, SUB)
    top = side[pl.ds(SUB * (ntiles + 2 * nrows - 1), SUB), :]
    za[to, :] = top
    zb[to, :] = top


def put_edges(q, first, side, at, nrows, edge_w, edge_e):
    for r in range(nrows):
        beside = side[pl.ds(pl.multiple_of(SUB * (at + r), SUB), SUB), :]
        edge_w[r, pl.ds(SUB, SUB), :] = beside
        edge_w[r, pl.ds(2 * SUB, SUB), :] = q[first + r, pl.ds(0, SUB), :]
        edge_e[r, pl.ds(0, SUB), :] = q[first + r, pl.ds(LANES - SUB, SUB), :]
        edge_e[r, pl.ds(SUB, SUB), :] = beside


def through(c, before, left, right, after):
    return c * (7.0 * (left + right) - (before + after))


def put_fluxes(q, first, nrows, ce, edge_w, edge_e, edge_c, flux):
    for r in range(nrows):
        window = [edge_w[r, pl.ds(SUB + k, SUB), :] for k in range(4)]
        flux[r, pl.ds(1, SUB), :] = through(edge_c[r, pl.ds(SUB + 1, SUB), :], *window)
        for b in range(LANES // SUB):
            at = SUB * b

            def load(shift):
                if at + shift < 0:
                    return edge_w[r, pl.ds(2 * SUB + shift, SUB), :]
                if at + shift + SUB > LANES:
                    return edge_e[r, pl.ds(shift, SUB), :]
                return q[first + r, pl.ds(at + shift, SUB), :]

            flux[r, pl.ds(SUB + at, SUB), :] = through(
                ce[r, pl.ds(at, SUB), :], load(-1), load(0), load(1), load(2)
            )


def lat_divergence(rows, winds):
    north = [through(winds[r], *rows[r : r + 4]) for r in range(len(winds))]
    return [north[r + 1] - north[r] for r in range(len(winds) - 1)]


def sources():
    at, n = lax.axis_index("lat"), lax.axis_size("lat")
    even = lax.rem(at, 2) == 0
    return (even, jnp.logical_not(even), jnp.logical_and(even, at > 0), jnp.logical_and(jnp.logical_not(even), at < n - 1))


def partners(where, ra, rb, span):
    north_a, south_a, south_b, north_b = where
    a, b = ra[span, :], rb[span, :]
    south = jnp.where(south_a, a, jnp.where(south_b, b, 0.0))
    return south, jnp.where(north_a, a, jnp.where(north_b, b, 0.0))


def divergence(q, pair, nrows, b, halo, cn, below, flux):
    at = SUB * b
    here = pl.ds(at, SUB)
    (s0, n0), (s1, n1) = halo(0, at), halo(1, at)
    own = [q[nrows * pair + r, here, :] for r in range(nrows)]
    winds = [below[here, :]] + [cn[r, here, :] for r in range(nrows)]
    north = lat_divergence([s0, s1] + own + [n0, n1], winds)
    div = []
    for r in range(nrows):
        east = flux[r, pl.ds(SUB + at, SUB), :] - flux[r, pl.ds(SUB + at - 1, SUB), :]
        div.append(east + north[r])
    return own, div


def put_side_section(at, nrows, where, ra, rb, corner, side, ntiles, edge_w, edge_e, edge_c, edge_d, out):
    head = sublanes() < SUB // 2

    def shifted(w, e, r, k):
        return jnp.where(head, e[r, pl.ds(SUB + k, SUB), :], w[r, pl.ds(SUB + k, SUB), :])

    def beside(t):
        return side[pl.ds(pl.multiple_of(SUB * t, SUB), SUB), :]

    start = pl.multiple_of(corner + SUB * (at // nrows), SUB)
    south, above = partners(where, ra, rb, pl.ds(start, SUB))
    s0, s1 = south, half_turn(south)
    n0, n1 = above, half_turn(above)
    own = [beside(at + r) for r in range(nrows)]
    last = pl.ds(corner + SUB * (ntiles // nrows), SUB)
    winds = [partners(where, ra, rb, last)[0]]
    winds += [beside(ntiles + nrows + r) for r in range(nrows)]
    north = lat_divergence([s0, s1] + own + [n0, n1], winds)
    for r in range(nrows):
        v = [shifted(edge_w, edge_e, r, k) for k in range(-2, 3)]
        east = through(beside(ntiles + r), *v[1:])
        west = through(shifted(edge_c, edge_d, r, -1), *v[:-1])
        new = own[r] - ((east - west) + north[r])
        out[pl.ds(pl.multiple_of(SUB * (at + r), SUB), SUB), :] = new


def edge_scratch(nrows):
    return [scratch(nrows, 3 * SUB, LANES)] * 4 + [scratch(nrows, LANES + SUB, LANES)]


def first_stage_early(pairs, ntiles, nrows, q, ce, cn, la, lb, ra, rb, section, za, zb, below, side, *edges):
    edge_w, edge_e, edge_c, edge_d, flux = edges
    lat_even, where = is_even("lat"), sources()
    half = LANES // 2
    a = partners(where, ra, rb, pl.ds(2 * pairs * LANES, half))[0]
    turned = pltpu.roll(a, half, 1)
    low = lax.broadcasted_iota(jnp.int32, (half, LANES), 1) < half
    below[pl.ds(0, half), :] = jnp.where(low, a, turned)
    below[pl.ds(half, half), :] = jnp.where(low, turned, a)
    put_side(la, lb, ntiles, side)
    put_corners(lat_even, ntiles, nrows, 2 * pairs * LANES, side, za, zb)
    put_edges(ce, 0, side, side.shape[0] // SUB - 2 * nrows, nrows, edge_c, edge_d)

    def one(p, _):
        def halo(k, shift):
            start = pl.multiple_of((2 * p + k) * LANES, LANES)
            return partners(where, ra, rb, pl.ds(start + shift, SUB))

        put_edges(q, nrows * p, side, nrows * p, nrows, edge_w, edge_e)
        put_fluxes(q, nrows * p, nrows, ce, edge_w, edge_e, edge_c, flux)
        for b in range(LANES // SUB):
            own, div = divergence(q, p, nrows, b, halo, cn, below, flux)
            for r in range(nrows):
                section[nrows * p + r, pl.ds(SUB * b, SUB), :] = own[r] - div[r]
        put_lat_sends(lat_even, section, p, nrows, za, zb)
        return 0

    lax.fori_loop(0, pairs, one, 0)


def first_stage_late(
    pairs, done, nrows, q, ce, cn, side, ra, rb, below, section, za, zb, *edges
):
    edge_w, edge_e, edge_c, edge_d, flux = edges
    lat_even, where = is_even("lat"), sources()
    put_edges(ce, 0, side, side.shape[0] // SUB - 2 * nrows, nrows, edge_c, edge_d)
    for p in range(pairs):

        def halo(k, shift):
            return partners(where, ra, rb, pl.ds((2 * p + k) * LANES + shift, SUB))

        put_edges(q, nrows * p, side, nrows * (done + p), nrows, edge_w, edge_e)
        put_fluxes(q, nrows * p, nrows, ce, edge_w, edge_e, edge_c, flux)
        for b in range(LANES // SUB):
            own, div = divergence(q, p, nrows, b, halo, cn, below, flux)
            for r in range(nrows):
                section[nrows * p + r, pl.ds(SUB * b, SUB), :] = own[r] - div[r]
        up = jnp.where(lat_even, 2, 0)
        for k in range(2):
            span = pl.ds((2 * p + k) * LANES, LANES)
            za[span, :] = jnp.transpose(section[nrows * p + up + k])
            zb[span, :] = jnp.transpose(section[nrows * p + (2 - up) + k])


def put_rows(buffer, pair, rows, nrows):
    levels = LANES // 2
    for r in range(nrows):
        turned = jnp.transpose(jnp.concatenate(rows[r], axis=0))
        for h in range(2):
            buffer[2 * pair + h, pl.ds(r, levels, stride=nrows), :] = turned[levels * h : levels * (h + 1)]


def second_stage_early(
    pairs, later, nrows, q, s, ce, cn, below, ra, rb, side, heating, q_late, s_late,
    out, heat_out, part, winds, buffer, sems, sides, *edges
):
    edge_w, edge_e, edge_c, edge_d, flux = edges
    where = sources()
    heat_copy = pltpu.make_async_copy(heating, heat_out, sems.at[pairs])
    heat_copy.start()
    put_edges(ce, 0, side, side.shape[0] // SUB - 2 * nrows, nrows, edge_c, edge_d)

    ntiles = nrows * (pairs + later)
    for ref, first, n in ((q, 0, pairs), (q_late, pairs, later)):

        def beside(p, _):
            at = nrows * (first + p)
            put_edges(ref, nrows * p, side, at, nrows, edge_w, edge_e)
            put_side_section(
                at, nrows, where, ra, rb, 2 * pairs * LANES, side, ntiles, edge_w, edge_e, edge_c, edge_d, sides
            )
            return 0

        lax.fori_loop(0, n, beside, 0)

    def copy(p):
        return pltpu.make_async_copy(buffer.at[pl.ds(2 * p, 2)], out.at[pl.ds(2 * p, 2)], sems.at[p])

    def one(p, _):
        def halo(k, shift):
            start = pl.multiple_of((2 * p + k) * LANES, LANES)
            return partners(where, ra, rb, pl.ds(start + shift, SUB))

        put_edges(s, nrows * p, sides, nrows * p, nrows, edge_w, edge_e)
        put_fluxes(s, nrows * p, nrows, ce, edge_w, edge_e, edge_c, flux)
        parts = [[] for _ in range(nrows)]
        for b in range(LANES // SUB):
            own, div = divergence(s, p, nrows, b, halo, cn, below, flux)
            for r in range(nrows):
                old = q[nrows * p + r, pl.ds(SUB * b, SUB), :]
                parts[r].append(0.5 * ((old + own[r]) - div[r]))
        put_rows(buffer, p, parts, nrows)

        @pl.when(p == 0)
        def _():
            buffer[0] = buffer[0] + 0.5 * heating[...]

        copy(p).start()
        return 0

    def another(p, _):
        put_edges(s_late, nrows * p, sides, nrows * (pairs + p), nrows, edge_w, edge_e)
        put_fluxes(s_late, nrows * p, nrows, ce, edge_w, edge_e, edge_c, flux)
        rows = [[] for _ in range(nrows)]
        for b in range(LANES // SUB):
            here = pl.ds(SUB * b, SUB)
            s0, s1, s2, s3 = own = [s_late[nrows * p + r, here, :] for r in range(nrows)]
            c = [below[here, :]] + [cn[r, here, :] for r in range(nrows)]
            north = [
                c[0] * (7.0 * s0 - s1),
                c[1] * (7.0 * (s0 + s1) - s2),
                through(c[2], *own),
                c[3] * (7.0 * (s2 + s3) - s1),
                c[4] * (7.0 * s3 - s2),
            ]
            for r in range(nrows):
                east = flux[r, pl.ds(SUB * (b + 1), SUB), :] - flux[r, pl.ds(SUB * (b + 1) - 1, SUB), :]
                old = q_late[nrows * p + r, here, :]
                rows[r].append(0.5 * ((old + own[r]) - (east + (north[r + 1] - north[r]))))
        put_rows(part, p, rows, nrows)
        return 0

    lax.fori_loop(0, pairs, one, 0)
    lax.fori_loop(0, later, another, 0)
    for i, tile in enumerate((cn[0], cn[2], below[...], cn[3])):
        winds[i] = 0.5 * jnp.transpose(tile)[: LANES // 2]
    for p in range(pairs):
        copy(p).wait()
    heat_copy.wait()


def second_stage_late(pairs, done, nrows, part, winds, ra, rb, before, out, buffer, sems):
    del before
    levels = LANES // 2

    def copy(i):
        return pltpu.make_async_copy(buffer.at[i], out.at[2 * done + i], sems.at[i])

    def finish(south, north):
        for p in range(pairs):
            for h in range(2):
                for b in range(levels // SUB):
                    here = pl.ds(SUB * b, SUB)
                    one, two = (pl.ds((2 * p + k) * LANES + levels * h + SUB * b, SUB) for k in range(2))
                    more = [None] * nrows
                    if south is not None:
                        low = winds[0, here, :] * south[two, :]
                        more[0] = low + winds[2, here, :] * (7.0 * south[two, :] - south[one, :])
                        more[1] = -low
                    if north is not None:
                        high = winds[1, here, :] * north[one, :]
                        more[2] = high
                        more[3] = -(winds[3, here, :] * (7.0 * north[one, :] - north[two, :]) + high)
                    for r in range(nrows):
                        rows = pl.ds(nrows * SUB * b + r, SUB, stride=nrows)
                        value = part[2 * p + h, rows, :]
                        buffer[2 * p + h, rows, :] = value if more[r] is None else value + more[r]
                copy(2 * p + h).start()
        for i in range(2 * pairs):
            copy(i).wait()

    at, n = lax.axis_index("lat"), lax.axis_size("lat")
    even, inner = is_even("lat"), jnp.logical_and(at > 0, at < n - 1)
    pl.when(at == 0)(lambda: finish(None, ra))
    pl.when(at == n - 1)(lambda: finish(ra, None))
    pl.when(jnp.logical_and(inner, even))(lambda: finish(rb, ra))
    pl.when(jnp.logical_and(inner, jnp.logical_not(even)))(lambda: finish(ra, rb))


def radiation(
    nat, cosz_in, albedo_in, ext_in, single_in, weight_in, order_in, count_in, after, heat,
    water, depth, save_c, save_d, save_t, save_g, cosz, albedo, ext, single, weight, order, count, sems
):
    del after
    copies = []
    for i, (src, dst) in enumerate(
        (
            (cosz_in, cosz), (albedo_in, albedo), (ext_in, ext), (single_in, single),
            (weight_in, weight), (order_in, order), (count_in, count),
        )
    ):
        copies.append(pltpu.make_async_copy(src, dst, sems.at[i]))
        copies[-1].start()
    nrows, _ = cosz.shape
    levels = nat.shape[1] // nrows
    pairs = ext.shape[0] // 2
    x = nat[1]
    heat[...] = jnp.maximum(x, 0.0) + jnp.log1p(jnp.exp(-jnp.abs(x)))
    total = jnp.zeros((nrows, LANES), jnp.float32)
    depth[0] = jnp.zeros((2 * nrows, LANES), jnp.float32)
    for l in range(levels):
        w = heat[pl.ds(nrows * l, nrows), :]
        total = total + w
        water[l, pl.ds(0, nrows), :] = w
        water[l, pl.ds(nrows, nrows), :] = w
        depth[l + 1, pl.ds(0, nrows), :] = total
        depth[l + 1, pl.ds(nrows, nrows), :] = total
    for copy in copies:
        copy.wait()

    mu = jnp.concatenate([cosz[...], cosz[...]], axis=0)
    floor_albedo = jnp.concatenate([albedo[...], albedo[...]], axis=0)
    first = lax.broadcasted_iota(jnp.int32, (2 * nrows, LANES), 0) < nrows

    def by_band(ref):
        return [jnp.where(first, ref[2 * p], ref[2 * p + 1]) for p in range(pairs)]

    scale = 4.0 / levels
    inv_mu = 1.0 / mu
    ext_of, single_of, weight_of = by_band(ext), by_band(single), by_band(weight)
    beam = [-(e * scale * LOG2E) * inv_mu for e in ext_of]
    diffuse = [-(1.66 * scale * LOG2E) * e for e in ext_of]
    half = [0.5 * s for s in single_of]
    strength = [weight_of[p] * mu * (1.0 - single_of[p]) for p in range(pairs)]

    def up(step, carry):
        l = levels - 1 - step
        a_all, b_all, s_all = carry
        w = water[l]
        above = depth[l]
        new_a, new_b, new_s = [], [], []
        known = jnp.zeros((2 * nrows, LANES), jnp.float32)
        for p in range(pairs):
            a, b, s_bot = a_all[p], b_all[p], s_all[p]
            decay = jnp.exp2(diffuse[p] * w)
            s_top = strength[p] * jnp.exp2(beam[p] * above)
            lost = 1.0 - decay
            reflect = half[p] * lost
            transmit = decay + reflect
            taken = s_top - s_bot
            source = half[p] * taken
            den = 1.0 - reflect * a
            inv = pl.reciprocal(den, approx=True)
            inv = inv * (2.0 - den * inv)
            t = transmit * inv
            ta = t * a
            g = (reflect * b + source) * inv
            save_t[l, p] = t
            save_g[l, p] = g
            save_d[l, p] = lost + lost * ta
            known = known + (lost * (a * g + b) + taken)
            new_a.append(reflect + transmit * ta)
            new_b.append(t * (a * source + b) + source)
            new_s.append(s_top)
        save_c[l] = known
        return tuple(new_a), tuple(new_b), tuple(new_s)

    s_floor = [strength[p] * jnp.exp2(beam[p] * depth[levels]) for p in range(pairs)]
    a_floor = [floor_albedo for _ in range(pairs)]
    b_floor = [floor_albedo * s_floor[p] for p in range(pairs)]
    lax.fori_loop(0, levels, up, (tuple(a_floor), tuple(b_floor), tuple(s_floor)))

    sunlit = []
    column = lax.broadcasted_iota(jnp.int32, (LANES, LANES), 1)
    rank = lax.broadcasted_iota(jnp.int32, (LANES, LANES), 0)
    for r in range(nrows):
        place = jnp.transpose(jnp.broadcast_to(order[r], (LANES, LANES)))
        hit = (place == column) & (rank < count[r])
        sunlit.append(jnp.max(jnp.where(hit, 1.0, 0.0), axis=0, keepdims=True))
    gain = float(levels) * jnp.concatenate(sunlit, axis=0)

    def down(l, d_all):
        absorbed = save_c[l]
        for p in range(pairs):
            absorbed = absorbed + save_d[l, p] * d_all[p]
        both = absorbed[:nrows] + absorbed[nrows:]
        heat[pl.ds(pl.multiple_of(nrows * l, nrows), nrows), :] = gain * both
        return tuple(save_t[l, p] * d_all[p] + save_g[l, p] for p in range(pairs))

    d_top = tuple(jnp.zeros((2 * nrows, LANES), jnp.float32) for _ in range(pairs))
    lax.fori_loop(0, levels, down, d_top, unroll=4)


def in_hbm(x):
    return pltpu.with_memory_space_constraint(x, pltpu.HBM)


def call(kernel, name, out_shape, specs, out_specs, args, scratches, moved=1000, limit=24, **kw):
    return pl.pallas_call(
        kernel,
        out_shape=out_shape,
        in_specs=specs,
        out_specs=out_specs,
        scratch_shapes=scratches,
        compiler_params=pltpu.CompilerParams(vmem_limit_bytes=limit * MIB),
        name=name,
        cost_estimate=pl.CostEstimate(flops=moved, bytes_accessed=moved, transcendentals=0),
        **kw,
    )(*args)


def per_device(
    fields, courant, cos_zenith, albedo, extinction, single_albedo, band_weight, sun_order, sun_count
):
    nfields, levels, nrows, ncols = fields.shape
    flat = fields.reshape(nfields, levels * nrows, ncols)
    wind = courant.reshape(2, levels * nrows, ncols)
    npairs = nfields // 2
    early, late = SPLIT, npairs - SPLIT

    z0 = shape(2 * early * ncols + ncols // 2, LANES)
    tiles0, za, zb, nat, nat_late, nat_wind = call(
        functools.partial(pack_first, early, nrows),
        "pack_first",
        (
            shape(nrows * early, ncols, LANES), z0, z0,
            shape(2 * early, levels * nrows, ncols), shape(2 * late, levels * nrows, ncols),
            shape(2, levels * nrows, ncols),
        ),
        [HBM, HBM],
        (VMEM,) * 6,
        (in_hbm(flat), in_hbm(wind)),
        [pltpu.SemaphoreType.DMA((early + 3,))],
    )
    lat0 = lat_swaps(za, zb)
    ntiles = nrows * npairs
    winds = shape(nrows, ncols, LANES)
    sides = shape(SUB * (ntiles + 2 * nrows), LANES)
    edge = shape(SUB * (ntiles + nrows) // 2, LANES)
    z1 = shape(2 * late * ncols, LANES)
    tiles1, ce, cn, la, lb, za, zb = call(
        functools.partial(pack_middle, late, nrows),
        "pack_middle",
        (shape(nrows * late, ncols, LANES), winds, winds, edge, edge, z1, z1),
        [VMEM] * 3,
        (VMEM,) * 7,
        (nat_late, nat_wind, tiles0),
        [],
    )
    lat1 = lat_swaps(za, zb)
    lon = lon_swaps(la, lb)

    edges = edge_scratch(nrows)
    z0 = shape(2 * early * ncols + SUB * (npairs + 1), LANES)
    section0, za, zb, below, side = call(
        functools.partial(first_stage_early, early, ntiles, nrows),
        "first_stage_early",
        (shape(nrows * early, ncols, LANES), z0, z0, shape(ncols, LANES), sides),
        [VMEM] * 7,
        (VMEM,) * 5,
        (tiles0, ce, cn, *lon, *lat0),
        edges,
        moved=1000_000_000,
    )
    lat2 = lat_swaps(za, zb)
    z1 = shape(2 * late * ncols, LANES)
    section1, za, zb = call(
        functools.partial(first_stage_late, late, early, nrows),
        "first_stage_late",
        (shape(nrows * late, ncols, LANES), z1, z1),
        [VMEM] * 7,
        (VMEM,) * 3,
        (tiles1, ce, cn, side, *lat1, below),
        edges,
        moved=12_000_000,
    )
    lat3 = lat_swaps(za, zb)

    pairs = extinction.shape[0] // 2
    store = scratch(levels, pairs, 2 * nrows, ncols)
    heating = call(
        radiation,
        "radiation",
        shape(levels * nrows, ncols),
        [VMEM] + [HBM] * 7 + [VMEM],
        VMEM,
        (
            nat, in_hbm(cos_zenith), in_hbm(albedo), in_hbm(extinction), in_hbm(single_albedo),
            in_hbm(band_weight), in_hbm(sun_order), in_hbm(sun_count.reshape(nrows)), section1,
        ),
        [
            scratch(levels, 2 * nrows, ncols), scratch(levels + 1, 2 * nrows, ncols),
            scratch(levels, 2 * nrows, ncols), store, store, store,
            scratch(nrows, ncols), scratch(nrows, ncols),
            pltpu.SMEM(extinction.shape, jnp.float32), pltpu.SMEM(extinction.shape, jnp.float32),
            pltpu.SMEM(extinction.shape, jnp.float32), pltpu.VMEM((nrows, 1, ncols), jnp.int32),
            pltpu.SMEM((nrows,), jnp.int32), pltpu.SemaphoreType.DMA((7,)),
        ],
        moved=16_000_000,
    )

    full = shape(nfields, levels * nrows, ncols)
    out, heat_out, part, half_winds = call(
        functools.partial(second_stage_early, early, late, nrows),
        "second_stage_early",
        (full, shape(levels * nrows, ncols), shape(2 * late, levels * nrows, ncols), shape(nrows, levels, ncols)),
        [VMEM] * 11,
        (HBM, HBM, VMEM, VMEM),
        (tiles0, section0, ce, cn, below, *lat2, side, heating, tiles1, section1),
        [
            scratch(2 * early, levels * nrows, ncols),
            pltpu.SemaphoreType.DMA((early + 1,)),
            scratch(SUB * ntiles, LANES),
            *edges,
        ],
    )
    out = call(
        functools.partial(second_stage_late, late, early, nrows),
        "second_stage_late",
        full,
        [VMEM] * 4 + [HBM],
        HBM,
        (part, half_winds, *lat3, out),
        [scratch(2 * late, levels * nrows, ncols), pltpu.SemaphoreType.DMA((2 * late,))],
        input_output_aliases={4: 0},
    )
    return out.reshape(fields.shape), heat_out.reshape(levels, nrows, ncols)


def solution(mesh):
    in_specs = (
        P(None, None, "lat", "lon"),
        P(None, None, "lat", "lon"),
        P("lat", "lon"),
        P("lat", "lon"),
        P(),
        P(),
        P(),
        P("lat", "lon", None),
        P("lat", "lon"),
    )
    out_specs = (P(None, None, "lat", "lon"), P(None, "lat", "lon"))
    return jax.shard_map(
        per_device, mesh=mesh, in_specs=in_specs, out_specs=out_specs, check_vma=False
    )
```

```python
import functools
import math

import jax
import jax.numpy as jnp
from jax import lax
from jax.experimental import pallas as pl
from jax.experimental.pallas import tpu as pltpu
from jax.sharding import PartitionSpec as P

SPLIT = 2
SUB = 8
LANES = 128
LOG2E = math.log2(math.e)
VMEM = pl.BlockSpec(memory_space=pltpu.VMEM)
HBM = pl.BlockSpec(memory_space=pltpu.HBM)
MIB = 1024 * 1024


def scratch(*dims):
    return pltpu.VMEM(dims, jnp.float32)


def shape(*dims):
    return jax.ShapeDtypeStruct(dims, jnp.float32)


def lon_swaps(first_block, second_block):
    n = lax.axis_size("lon")
    first = [(i, i ^ 1) for i in range(n)]
    second = [(i, (i + 1 if i % 2 else i - 1) % n) for i in range(n)]
    return lax.ppermute(first_block, "lon", first), lax.ppermute(second_block, "lon", second)


def lat_swaps(first_block, second_block):
    nlon, nlat = lax.axis_size("lon"), lax.axis_size("lat")
    second = []
    for i in range(nlon):
        for j in range(nlat):
            k = j + 1 if j % 2 else j - 1
            to = i * nlat + k if 0 <= k < nlat else (i ^ 1) * nlat + j
            second.append((i * nlat + j, to))
    got = lax.ppermute(second_block, ("lon", "lat"), second)
    return lax.ppermute(first_block, "lat", [(j, j ^ 1) for j in range(nlat)]), got


def is_even(axis):
    return lax.rem(lax.axis_index(axis), 2) == 0


def sublanes():
    return lax.broadcasted_iota(jnp.int32, (SUB, LANES), 0)


def lanes():
    return lax.broadcasted_iota(jnp.int32, (SUB, LANES), 1)


def half_turn(block):
    return pltpu.roll(block, SUB // 2, 0)


def native(ref, index, r, nrows):
    levels = ref.shape[1] // nrows
    return ref[index, pl.ds(r, levels, stride=nrows), :]


def tile_of(low, high):
    return jnp.transpose(jnp.concatenate([low, high], axis=0))


def put_lat_sends(even, tiles, pair, nrows, za, zb):
    north = jnp.where(even, 2, 0)
    for k in range(2):
        span = pl.ds(pl.multiple_of((2 * pair + k) * LANES, LANES), LANES)
        za[span, :] = tiles[nrows * pair + north + k]
        zb[span, :] = tiles[nrows * pair + (2 - north) + k]


def take_sides(tile):
    head = sublanes() < SUB // 2
    return jnp.where(head, tile[pl.ds(0, SUB), :], tile[pl.ds(LANES - SUB, SUB), :])


def pack_first(pairs, nrows, fields, courant, za, zb, nat, nat_late, nat_wind, sems):
    n = 2 * pairs
    first = [
        pltpu.make_async_copy(fields.at[pl.ds(2 * p, 2)], nat.at[pl.ds(2 * p, 2)], sems.at[p]) for p in range(pairs)
    ]
    north = pltpu.make_async_copy(courant.at[pl.ds(1, 1)], nat_wind.at[pl.ds(1, 1)], sems.at[pairs])
    late = pltpu.make_async_copy(fields.at[pl.ds(n, nat_late.shape[0])], nat_late, sems.at[pairs + 1])
    east = pltpu.make_async_copy(courant.at[pl.ds(0, 1)], nat_wind.at[pl.ds(0, 1)], sems.at[pairs + 2])
    for copy in first + [north, late, east]:
        copy.start()
    half = LANES // 2
    even = is_even("lat")

    def body(p, up, down):
        for r in range(nrows):
            for h in range(2):
                span = pl.ds((2 * p + r % 2) * LANES + half * h, half)
                (up if r >= 2 else down)[span, :] = native(nat, 2 * p + h, r, nrows)
        if p < pairs - 1:
            return
        top = native(nat_wind, 1, nrows - 1, nrows) * (1.0 / 12.0)
        for ref in (up, down):
            ref[pl.ds(2 * pairs * LANES, half), :] = top

    for p in range(pairs):
        first[p].wait()
        if p == pairs - 1:
            north.wait()
        pl.when(even)(functools.partial(body, p, za, zb))
        pl.when(jnp.logical_not(even))(functools.partial(body, p, zb, za))
    late.wait()
    east.wait()


def pack_middle(pairs, nrows, nat, nat_late, nat_wind, tiles_first, tiles, ce, cn, la, lb, za, zb):
    up = jnp.where(is_even("lat"), 2, 0)
    for source, ref in ((nat, tiles_first), (nat_late, tiles)):
        for t in range(ref.shape[0]):
            p, r = divmod(t, nrows)
            ref[t] = tile_of(native(source, 2 * p, r, nrows), native(source, 2 * p + 1, r, nrows))
    for r in range(nrows):
        east = native(nat_wind, 0, r, nrows) * (1.0 / 12.0)
        north = native(nat_wind, 1, r, nrows) * (1.0 / 12.0)
        ce[r] = tile_of(east, east)
        cn[r] = tile_of(north, north)
    for i in range(2 * pairs):
        p, k = divmod(i, 2)
        span = pl.ds(i * LANES, LANES)
        za[span, :] = tiles[nrows * p + up + k]
        zb[span, :] = tiles[nrows * p + (2 - up) + k]
    even = is_even("lon")
    head, low = sublanes() < SUB // 2, lanes() < LANES // 2
    blocks = [take_sides(ref.at[t]) for ref in (tiles_first, tiles) for t in range(ref.shape[0])]
    blocks += [jnp.where(low, take_sides(ce.at[r]), take_sides(cn.at[r])) for r in range(nrows)]
    for i in range(0, len(blocks), 2):
        one, two = blocks[i : i + 2]
        east = jnp.where(head, half_turn(one), two)
        west = jnp.where(head, one, half_turn(two))
        span = pl.ds(SUB * (i // 2), SUB)
        la[span, :] = jnp.where(even, east, west)
        lb[span, :] = jnp.where(even, west, east)


def put_side(la, lb, ntiles, side):
    lon_even = is_even("lon")
    head, low = sublanes() < SUB // 2, lanes() < LANES // 2
    blocks = []
    for i in range(la.shape[0] // SUB):
        span = pl.ds(SUB * i, SUB)
        a, b = la[span, :], lb[span, :]
        east, west = jnp.where(lon_even, a, b), jnp.where(lon_even, b, a)
        blocks += [jnp.where(head, east, half_turn(west)), jnp.where(head, half_turn(east), west)]
    winds = blocks[ntiles:]
    turned = [pltpu.roll(wind, LANES // 2, 1) for wind in winds]
    blocks[ntiles:] = [jnp.where(low, x, y) for x, y in zip(winds, turned)]
    blocks += [jnp.where(low, y, x) for x, y in zip(winds, turned)]
    for t, value in enumerate(blocks):
        side[pl.ds(SUB * t, SUB), :] = value


def put_corners(lat_even, ntiles, nrows, at, side, za, zb):
    row = sublanes()
    outer = (row < 2) | (row >= SUB - 2)
    north = jnp.where(lat_even, 2, 0)

    def corner(p, first):
        start = pl.multiple_of(SUB * (nrows * p + first), SUB)
        one, two = side[pl.ds(start, SUB), :], side[pl.ds(start + SUB, SUB), :]
        return jnp.where(outer, one, half_turn(two))

    npairs = ntiles // nrows
    for p in range(npairs):
        to = pl.ds(at + SUB * p, SUB)
        za[to, :] = corner(p, north)
        zb[to, :] = corner(p, 2 - north)
    to = pl.ds(at + SUB * npairs, SUB)
    top = side[pl.ds(SUB * (ntiles + 2 * nrows - 1), SUB), :]
    za[to, :] = top
    zb[to, :] = top


def put_edges(q, first, side, at, nrows, edge_w, edge_e):
    for r in range(nrows):
        beside = side[pl.ds(pl.multiple_of(SUB * (at + r), SUB), SUB), :]
        edge_w[r, pl.ds(SUB, SUB), :] = beside
        edge_w[r, pl.ds(2 * SUB, SUB), :] = q[first + r, pl.ds(0, SUB), :]
        edge_e[r, pl.ds(0, SUB), :] = q[first + r, pl.ds(LANES - SUB, SUB), :]
        edge_e[r, pl.ds(SUB, SUB), :] = beside


def through(c, before, left, right, after):
    return c * (7.0 * (left + right) - (before + after))


def put_fluxes(q, first, nrows, ce, edge_w, edge_e, edge_c, flux):
    for r in range(nrows):
        window = [edge_w[r, pl.ds(SUB + k, SUB), :] for k in range(4)]
        flux[r, pl.ds(1, SUB), :] = through(edge_c[r, pl.ds(SUB + 1, SUB), :], *window)
        for b in range(LANES // SUB):
            at = SUB * b

            def load(shift):
                if at + shift < 0:
                    return edge_w[r, pl.ds(2 * SUB + shift, SUB), :]
                if at + shift + SUB > LANES:
                    return edge_e[r, pl.ds(shift, SUB), :]
                return q[first + r, pl.ds(at + shift, SUB), :]

            flux[r, pl.ds(SUB + at, SUB), :] = through(
                ce[r, pl.ds(at, SUB), :], load(-1), load(0), load(1), load(2)
            )


def lat_divergence(rows, winds):
    north = [through(winds[r], *rows[r : r + 4]) for r in range(len(winds))]
    return [north[r + 1] - north[r] for r in range(len(winds) - 1)]


def sources():
    at, n = lax.axis_index("lat"), lax.axis_size("lat")
    even = lax.rem(at, 2) == 0
    return (even, jnp.logical_not(even), jnp.logical_and(even, at > 0), jnp.logical_and(jnp.logical_not(even), at < n - 1))


def partners(where, ra, rb, span):
    north_a, south_a, south_b, north_b = where
    a, b = ra[span, :], rb[span, :]
    south = jnp.where(south_a, a, jnp.where(south_b, b, 0.0))
    return south, jnp.where(north_a, a, jnp.where(north_b, b, 0.0))


def divergence(q, pair, nrows, b, halo, cn, below, flux):
    at = SUB * b
    here = pl.ds(at, SUB)
    (s0, n0), (s1, n1) = halo(0, at), halo(1, at)
    own = [q[nrows * pair + r, here, :] for r in range(nrows)]
    winds = [below[here, :]] + [cn[r, here, :] for r in range(nrows)]
    north = lat_divergence([s0, s1] + own + [n0, n1], winds)
    div = []
    for r in range(nrows):
        east = flux[r, pl.ds(SUB + at, SUB), :] - flux[r, pl.ds(SUB + at - 1, SUB), :]
        div.append(east + north[r])
    return own, div


def put_side_section(at, nrows, where, ra, rb, corner, side, ntiles, edge_w, edge_e, edge_c, edge_d, out):
    head = sublanes() < SUB // 2

    def shifted(w, e, r, k):
        return jnp.where(head, e[r, pl.ds(SUB + k, SUB), :], w[r, pl.ds(SUB + k, SUB), :])

    def beside(t):
        return side[pl.ds(pl.multiple_of(SUB * t, SUB), SUB), :]

    start = pl.multiple_of(corner + SUB * (at // nrows), SUB)
    south, above = partners(where, ra, rb, pl.ds(start, SUB))
    s0, s1 = south, half_turn(south)
    n0, n1 = above, half_turn(above)
    own = [beside(at + r) for r in range(nrows)]
    last = pl.ds(corner + SUB * (ntiles // nrows), SUB)
    winds = [partners(where, ra, rb, last)[0]]
    winds += [beside(ntiles + nrows + r) for r in range(nrows)]
    north = lat_divergence([s0, s1] + own + [n0, n1], winds)
    for r in range(nrows):
        v = [shifted(edge_w, edge_e, r, k) for k in range(-2, 3)]
        east = through(beside(ntiles + r), *v[1:])
        west = through(shifted(edge_c, edge_d, r, -1), *v[:-1])
        new = own[r] - ((east - west) + north[r])
        out[pl.ds(pl.multiple_of(SUB * (at + r), SUB), SUB), :] = new


def edge_scratch(nrows):
    return [scratch(nrows, 3 * SUB, LANES)] * 4 + [scratch(nrows, LANES + SUB, LANES)]


def first_stage_early(pairs, ntiles, nrows, q, ce, cn, la, lb, ra, rb, section, za, zb, below, side, *edges):
    edge_w, edge_e, edge_c, edge_d, flux, beyond = edges
    lat_even, where = is_even("lat"), sources()
    half = LANES // 2
    wind = partners(where, ra, rb, pl.ds(2 * pairs * LANES, half))[0]
    below[...] = tile_of(wind, wind)
    put_side(la, lb, ntiles, side)
    put_corners(lat_even, ntiles, nrows, 2 * pairs * LANES, side, za, zb)
    put_edges(ce, 0, side, side.shape[0] // SUB - 2 * nrows, nrows, edge_c, edge_d)

    def one(p, _):
        for k in range(2):
            span = pl.ds(pl.multiple_of((2 * p + k) * LANES, LANES), LANES)
            south, north = partners(where, ra, rb, span)
            beyond[k] = jnp.transpose(south)
            beyond[2 + k] = jnp.transpose(north)

        def halo(k, shift):
            here = pl.ds(shift, SUB)
            return beyond[k, here, :], beyond[2 + k, here, :]

        put_edges(q, nrows * p, side, nrows * p, nrows, edge_w, edge_e)
        put_fluxes(q, nrows * p, nrows, ce, edge_w, edge_e, edge_c, flux)
        for b in range(LANES // SUB):
            own, div = divergence(q, p, nrows, b, halo, cn, below, flux)
            for r in range(nrows):
                section[nrows * p + r, pl.ds(SUB * b, SUB), :] = own[r] - div[r]
        put_lat_sends(lat_even, section, p, nrows, za, zb)
        return 0

    lax.fori_loop(0, pairs, one, 0)


def first_stage_late(
    pairs, done, nrows, q, ce, cn, side, ra, rb, below, section, za, zb, *edges
):
    edge_w, edge_e, edge_c, edge_d, flux = edges
    lat_even, where = is_even("lat"), sources()
    put_edges(ce, 0, side, side.shape[0] // SUB - 2 * nrows, nrows, edge_c, edge_d)
    for p in range(pairs):

        def halo(k, shift):
            return partners(where, ra, rb, pl.ds((2 * p + k) * LANES + shift, SUB))

        put_edges(q, nrows * p, side, nrows * (done + p), nrows, edge_w, edge_e)
        put_fluxes(q, nrows * p, nrows, ce, edge_w, edge_e, edge_c, flux)
        for b in range(LANES // SUB):
            own, div = divergence(q, p, nrows, b, halo, cn, below, flux)
            for r in range(nrows):
                section[nrows * p + r, pl.ds(SUB * b, SUB), :] = own[r] - div[r]
        up = jnp.where(lat_even, 2, 0)
        for k in range(2):
            span = pl.ds((2 * p + k) * LANES, LANES)
            za[span, :] = jnp.transpose(section[nrows * p + up + k])
            zb[span, :] = jnp.transpose(section[nrows * p + (2 - up) + k])


def put_rows(buffer, pair, rows, nrows):
    levels = LANES // 2
    for r in range(nrows):
        turned = jnp.transpose(jnp.concatenate(rows[r], axis=0))
        for h in range(2):
            buffer[2 * pair + h, pl.ds(r, levels, stride=nrows), :] = turned[levels * h : levels * (h + 1)]


def second_stage_early(
    pairs, later, nrows, q, s, ce, cn, below, ra, rb, side, heating, q_late, s_late,
    out, heat_out, part, winds, buffer, sems, sides, *edges
):
    edge_w, edge_e, edge_c, edge_d, flux = edges
    where = sources()
    heat_copy = pltpu.make_async_copy(heating, heat_out, sems.at[pairs])
    heat_copy.start()
    put_edges(ce, 0, side, side.shape[0] // SUB - 2 * nrows, nrows, edge_c, edge_d)

    ntiles = nrows * (pairs + later)
    for ref, first, n in ((q, 0, pairs), (q_late, pairs, later)):

        def beside(p, _):
            at = nrows * (first + p)
            put_edges(ref, nrows * p, side, at, nrows, edge_w, edge_e)
            put_side_section(
                at, nrows, where, ra, rb, 2 * pairs * LANES, side, ntiles, edge_w, edge_e, edge_c, edge_d, sides
            )
            return 0

        lax.fori_loop(0, n, beside, 0)

    def copy(p):
        return pltpu.make_async_copy(buffer.at[pl.ds(2 * p, 2)], out.at[pl.ds(2 * p, 2)], sems.at[p])

    def one(p, _):
        def halo(k, shift):
            start = pl.multiple_of((2 * p + k) * LANES, LANES)
            return partners(where, ra, rb, pl.ds(start + shift, SUB))

        put_edges(s, nrows * p, sides, nrows * p, nrows, edge_w, edge_e)
        put_fluxes(s, nrows * p, nrows, ce, edge_w, edge_e, edge_c, flux)
        parts = [[] for _ in range(nrows)]
        for b in range(LANES // SUB):
            own, div = divergence(s, p, nrows, b, halo, cn, below, flux)
            for r in range(nrows):
                old = q[nrows * p + r, pl.ds(SUB * b, SUB), :]
                parts[r].append(0.5 * ((old + own[r]) - div[r]))
        put_rows(buffer, p, parts, nrows)

        @pl.when(p == 0)
        def _():
            buffer[0] = buffer[0] + 0.5 * heating[...]

        copy(p).start()
        return 0

    def another(p, _):
        put_edges(s_late, nrows * p, sides, nrows * (pairs + p), nrows, edge_w, edge_e)
        put_fluxes(s_late, nrows * p, nrows, ce, edge_w, edge_e, edge_c, flux)
        rows = [[] for _ in range(nrows)]
        for b in range(LANES // SUB):
            here = pl.ds(SUB * b, SUB)
            s0, s1, s2, s3 = own = [s_late[nrows * p + r, here, :] for r in range(nrows)]
            c = [below[here, :]] + [cn[r, here, :] for r in range(nrows)]
            north = [
                c[0] * (7.0 * s0 - s1),
                c[1] * (7.0 * (s0 + s1) - s2),
                through(c[2], *own),
                c[3] * (7.0 * (s2 + s3) - s1),
                c[4] * (7.0 * s3 - s2),
            ]
            for r in range(nrows):
                east = flux[r, pl.ds(SUB * (b + 1), SUB), :] - flux[r, pl.ds(SUB * (b + 1) - 1, SUB), :]
                old = q_late[nrows * p + r, here, :]
                rows[r].append(0.5 * ((old + own[r]) - (east + (north[r + 1] - north[r]))))
        put_rows(part, p, rows, nrows)
        return 0

    lax.fori_loop(0, pairs, one, 0)
    lax.fori_loop(0, later, another, 0)
    for i, tile in enumerate((cn[0], cn[2], below[...], cn[3])):
        winds[i] = 0.5 * jnp.transpose(tile)[: LANES // 2]
    for p in range(pairs):
        copy(p).wait()
    heat_copy.wait()


def second_stage_late(pairs, done, nrows, part, winds, ra, rb, before, out, buffer, sems):
    del before
    levels = LANES // 2

    def copy(i):
        return pltpu.make_async_copy(buffer.at[i], out.at[2 * done + i], sems.at[i])

    def finish(south, north):
        for p in range(pairs):
            for h in range(2):
                for b in range(levels // SUB):
                    here = pl.ds(SUB * b, SUB)
                    one, two = (pl.ds((2 * p + k) * LANES + levels * h + SUB * b, SUB) for k in range(2))
                    more = [None] * nrows
                    if south is not None:
                        low = winds[0, here, :] * south[two, :]
                        more[0] = low + winds[2, here, :] * (7.0 * south[two, :] - south[one, :])
                        more[1] = -low
                    if north is not None:
                        high = winds[1, here, :] * north[one, :]
                        more[2] = high
                        more[3] = -(winds[3, here, :] * (7.0 * north[one, :] - north[two, :]) + high)
                    for r in range(nrows):
                        rows = pl.ds(nrows * SUB * b + r, SUB, stride=nrows)
                        value = part[2 * p + h, rows, :]
                        buffer[2 * p + h, rows, :] = value if more[r] is None else value + more[r]
                copy(2 * p + h).start()
        for i in range(2 * pairs):
            copy(i).wait()

    at, n = lax.axis_index("lat"), lax.axis_size("lat")
    even, inner = is_even("lat"), jnp.logical_and(at > 0, at < n - 1)
    pl.when(at == 0)(lambda: finish(None, ra))
    pl.when(at == n - 1)(lambda: finish(ra, None))
    pl.when(jnp.logical_and(inner, even))(lambda: finish(rb, ra))
    pl.when(jnp.logical_and(inner, jnp.logical_not(even)))(lambda: finish(ra, rb))


def radiation(
    nat, cosz_in, albedo_in, ext_in, single_in, weight_in, order_in, count_in, after, heat,
    water, depth, save_c, save_d, save_t, save_g, cosz, albedo, ext, single, weight, order, count, sems
):
    del after
    copies = []
    for i, (src, dst) in enumerate(
        (
            (cosz_in, cosz), (albedo_in, albedo), (ext_in, ext), (single_in, single),
            (weight_in, weight), (order_in, order), (count_in, count),
        )
    ):
        copies.append(pltpu.make_async_copy(src, dst, sems.at[i]))
        copies[-1].start()
    nrows, _ = cosz.shape
    levels = nat.shape[1] // nrows
    pairs = ext.shape[0] // 2
    x = nat[1]
    heat[...] = jnp.maximum(x, 0.0) + jnp.log1p(jnp.exp(-jnp.abs(x)))
    total = jnp.zeros((nrows, LANES), jnp.float32)
    depth[0] = jnp.zeros((2 * nrows, LANES), jnp.float32)
    for l in range(levels):
        w = heat[pl.ds(nrows * l, nrows), :]
        total = total + w
        water[l, pl.ds(0, nrows), :] = w
        water[l, pl.ds(nrows, nrows), :] = w
        depth[l + 1, pl.ds(0, nrows), :] = total
        depth[l + 1, pl.ds(nrows, nrows), :] = total
    for copy in copies:
        copy.wait()

    mu = jnp.concatenate([cosz[...], cosz[...]], axis=0)
    floor_albedo = jnp.concatenate([albedo[...], albedo[...]], axis=0)
    first = lax.broadcasted_iota(jnp.int32, (2 * nrows, LANES), 0) < nrows

    def by_band(ref):
        return [jnp.where(first, ref[2 * p], ref[2 * p + 1]) for p in range(pairs)]

    scale = 4.0 / levels
    inv_mu = 1.0 / mu
    ext_of, single_of, weight_of = by_band(ext), by_band(single), by_band(weight)
    beam = [-(e * scale * LOG2E) * inv_mu for e in ext_of]
    diffuse = [-(1.66 * scale * LOG2E) * e for e in ext_of]
    half = [0.5 * s for s in single_of]
    strength = [weight_of[p] * mu * (1.0 - single_of[p]) for p in range(pairs)]

    def up(step, carry):
        l = levels - 1 - step
        a_all, b_all, s_all = carry
        w = water[l]
        above = depth[l]
        new_a, new_b, new_s = [], [], []
        known = jnp.zeros((2 * nrows, LANES), jnp.float32)
        for p in range(pairs):
            a, b, s_bot = a_all[p], b_all[p], s_all[p]
            decay = jnp.exp2(diffuse[p] * w)
            s_top = strength[p] * jnp.exp2(beam[p] * above)
            lost = 1.0 - decay
            reflect = half[p] * lost
            transmit = decay + reflect
            taken = s_top - s_bot
            source = half[p] * taken
            den = 1.0 - reflect * a
            inv = pl.reciprocal(den, approx=True)
            inv = inv * (2.0 - den * inv)
            t = transmit * inv
            ta = t * a
            g = (reflect * b + source) * inv
            save_t[l, p] = t
            save_g[l, p] = g
            save_d[l, p] = lost + lost * ta
            known = known + (lost * (a * g + b) + taken)
            new_a.append(reflect + transmit * ta)
            new_b.append(t * (a * source + b) + source)
            new_s.append(s_top)
        save_c[l] = known
        return tuple(new_a), tuple(new_b), tuple(new_s)

    s_floor = [strength[p] * jnp.exp2(beam[p] * depth[levels]) for p in range(pairs)]
    a_floor = [floor_albedo for _ in range(pairs)]
    b_floor = [floor_albedo * s_floor[p] for p in range(pairs)]
    lax.fori_loop(0, levels, up, (tuple(a_floor), tuple(b_floor), tuple(s_floor)))

    sunlit = []
    column = lax.broadcasted_iota(jnp.int32, (LANES, LANES), 1)
    rank = lax.broadcasted_iota(jnp.int32, (LANES, LANES), 0)
    for r in range(nrows):
        place = jnp.transpose(jnp.broadcast_to(order[r], (LANES, LANES)))
        hit = (place == column) & (rank < count[r])
        sunlit.append(jnp.max(jnp.where(hit, 1.0, 0.0), axis=0, keepdims=True))
    gain = float(levels) * jnp.concatenate(sunlit, axis=0)

    def down(l, d_all):
        absorbed = save_c[l]
        for p in range(pairs):
            absorbed = absorbed + save_d[l, p] * d_all[p]
        both = absorbed[:nrows] + absorbed[nrows:]
        heat[pl.ds(pl.multiple_of(nrows * l, nrows), nrows), :] = gain * both
        return tuple(save_t[l, p] * d_all[p] + save_g[l, p] for p in range(pairs))

    d_top = tuple(jnp.zeros((2 * nrows, LANES), jnp.float32) for _ in range(pairs))
    lax.fori_loop(0, levels, down, d_top, unroll=4)


def in_hbm(x):
    return pltpu.with_memory_space_constraint(x, pltpu.HBM)


def call(kernel, name, out_shape, specs, out_specs, args, scratches, moved=1000, limit=24, **kw):
    return pl.pallas_call(
        kernel,
        out_shape=out_shape,
        in_specs=specs,
        out_specs=out_specs,
        scratch_shapes=scratches,
        compiler_params=pltpu.CompilerParams(vmem_limit_bytes=limit * MIB),
        name=name,
        cost_estimate=pl.CostEstimate(flops=moved, bytes_accessed=moved, transcendentals=0),
        **kw,
    )(*args)


def per_device(
    fields, courant, cos_zenith, albedo, extinction, single_albedo, band_weight, sun_order, sun_count
):
    nfields, levels, nrows, ncols = fields.shape
    flat = fields.reshape(nfields, levels * nrows, ncols)
    wind = courant.reshape(2, levels * nrows, ncols)
    npairs = nfields // 2
    early, late = SPLIT, npairs - SPLIT

    z0 = shape(2 * early * ncols + ncols // 2, LANES)
    za, zb, nat, nat_late, nat_wind = call(
        functools.partial(pack_first, early, nrows),
        "pack_first",
        (
            z0, z0,
            shape(2 * early, levels * nrows, ncols), shape(2 * late, levels * nrows, ncols),
            shape(2, levels * nrows, ncols),
        ),
        [HBM, HBM],
        (VMEM,) * 5,
        (in_hbm(flat), in_hbm(wind)),
        [pltpu.SemaphoreType.DMA((early + 3,))],
    )
    lat0 = lat_swaps(za, zb)
    ntiles = nrows * npairs
    winds = shape(nrows, ncols, LANES)
    sides = shape(SUB * (ntiles + 2 * nrows), LANES)
    edge = shape(SUB * (ntiles + nrows) // 2, LANES)
    z1 = shape(2 * late * ncols, LANES)
    tiles0, tiles1, ce, cn, la, lb, za, zb = call(
        functools.partial(pack_middle, late, nrows),
        "pack_middle",
        (
            shape(nrows * early, ncols, LANES), shape(nrows * late, ncols, LANES),
            winds, winds, edge, edge, z1, z1,
        ),
        [VMEM] * 3,
        (VMEM,) * 8,
        (nat, nat_late, nat_wind),
        [],
    )
    lat1 = lat_swaps(za, zb)
    lon = lon_swaps(la, lb)

    edges = edge_scratch(nrows)
    z0 = shape(2 * early * ncols + SUB * (npairs + 1), LANES)
    section0, za, zb, below, side = call(
        functools.partial(first_stage_early, early, ntiles, nrows),
        "first_stage_early",
        (shape(nrows * early, ncols, LANES), z0, z0, shape(ncols, LANES), sides),
        [VMEM] * 7,
        (VMEM,) * 5,
        (tiles0, ce, cn, *lon, *lat0),
        [*edges, scratch(nrows, ncols, LANES)],
        moved=1000_000_000,
    )
    lat2 = lat_swaps(za, zb)
    z1 = shape(2 * late * ncols, LANES)
    section1, za, zb = call(
        functools.partial(first_stage_late, late, early, nrows),
        "first_stage_late",
        (shape(nrows * late, ncols, LANES), z1, z1),
        [VMEM] * 7,
        (VMEM,) * 3,
        (tiles1, ce, cn, side, *lat1, below),
        edges,
        moved=12_000_000,
    )
    lat3 = lat_swaps(za, zb)

    pairs = extinction.shape[0] // 2
    store = scratch(levels, pairs, 2 * nrows, ncols)
    heating = call(
        radiation,
        "radiation",
        shape(levels * nrows, ncols),
        [VMEM] + [HBM] * 7 + [VMEM],
        VMEM,
        (
            nat, in_hbm(cos_zenith), in_hbm(albedo), in_hbm(extinction), in_hbm(single_albedo),
            in_hbm(band_weight), in_hbm(sun_order), in_hbm(sun_count.reshape(nrows)), section1,
        ),
        [
            scratch(levels, 2 * nrows, ncols), scratch(levels + 1, 2 * nrows, ncols),
            scratch(levels, 2 * nrows, ncols), store, store, store,
            scratch(nrows, ncols), scratch(nrows, ncols),
            pltpu.SMEM(extinction.shape, jnp.float32), pltpu.SMEM(extinction.shape, jnp.float32),
            pltpu.SMEM(extinction.shape, jnp.float32), pltpu.VMEM((nrows, 1, ncols), jnp.int32),
            pltpu.SMEM((nrows,), jnp.int32), pltpu.SemaphoreType.DMA((7,)),
        ],
        moved=16_000_000,
    )

    full = shape(nfields, levels * nrows, ncols)
    out, heat_out, part, half_winds = call(
        functools.partial(second_stage_early, early, late, nrows),
        "second_stage_early",
        (full, shape(levels * nrows, ncols), shape(2 * late, levels * nrows, ncols), shape(nrows, levels, ncols)),
        [VMEM] * 11,
        (HBM, HBM, VMEM, VMEM),
        (tiles0, section0, ce, cn, below, *lat2, side, heating, tiles1, section1),
        [
            scratch(2 * early, levels * nrows, ncols),
            pltpu.SemaphoreType.DMA((early + 1,)),
            scratch(SUB * ntiles, LANES),
            *edges,
        ],
    )
    out = call(
        functools.partial(second_stage_late, late, early, nrows),
        "second_stage_late",
        full,
        [VMEM] * 4 + [HBM],
        HBM,
        (part, half_winds, *lat3, out),
        [scratch(2 * late, levels * nrows, ncols), pltpu.SemaphoreType.DMA((2 * late,))],
        input_output_aliases={4: 0},
    )
    return out.reshape(fields.shape), heat_out.reshape(levels, nrows, ncols)


def solution(mesh):
    in_specs = (
        P(None, None, "lat", "lon"),
        P(None, None, "lat", "lon"),
        P("lat", "lon"),
        P("lat", "lon"),
        P(),
        P(),
        P(),
        P("lat", "lon", None),
        P("lat", "lon"),
    )
    out_specs = (P(None, None, "lat", "lon"), P(None, "lat", "lon"))
    return jax.shard_map(
        per_device, mesh=mesh, in_specs=in_specs, out_specs=out_specs, check_vma=False
    )
```
